32 devices in a mesh: bucket: 4 (over x, core), dp: 8 (over z, y).
Axes of the slice: x: 2, y: 2, z: 4, core: 2. Of those that a mesh axis runs over, the one named last changes fastest.
Arguments:
- features: bfloat16 [4, 16384, 4, 100], P(None, ('bucket', 'dp')), may hold values from -24 to 24
- buckets: int32 [4, 16384, 1], P(None, ('bucket', 'dp')), may hold values from 0 to 3; in each aligned block of 512 rows (0 to 511, 512 to 1023, ..., all dimensions but the last counted through in order) at most 192 rows name the same one
- hop_mask: int32 [4, 16384, 3], P(None, ('bucket', 'dp')), may hold values 0 or 1
- labels: int32 [4, 16384], P(None, ('bucket', 'dp')), may hold values from 0 to 46
- w_hops: bfloat16 [4, 100, 512], replicated, may hold values from -0.625 to 0.625
- gain_hops: float32 [4, 512], replicated, may hold values from 0.5 to 1.5
- shift_hops: float32 [4, 512], replicated, may hold values from -3 to 3
- slope_hops: float32 [4, 512], replicated, may hold values from 0 to 0.5
- slope_cat: float32 [2048], replicated, may hold values from 0 to 0.5
- w_mid: bfloat16 [2048, 512], replicated, may hold values from -0.125 to 0.125
- gain_mid: float32 [512], replicated, may hold values from 0.5 to 1.5
- shift_mid: float32 [512], replicated, may hold values from -3 to 3
- slope_mid: float32 [512], replicated, may hold values from 0 to 0.5
- w_out: bfloat16 [512, 47], replicated, may hold values from -0.75 to 0.75
- bias_out: float32 [47], replicated, may hold values from -3 to 3
Outputs:
- loss: float32 [], replicated
- features_grad: float32 [4, 16384, 4, 100], P(None, ('bucket', 'dp'))
- grad_w_hops: float32 [4, 100, 512], replicated
- grad_gain_hops: float32 [4, 512], replicated
- grad_shift_hops: float32 [4, 512], replicated
- grad_slope_hops: float32 [4, 512], replicated
- grad_slope_cat: float32 [2048], replicated
- grad_w_mid: float32 [2048, 512], replicated
- grad_gain_mid: float32 [512], replicated
- grad_shift_mid: float32 [512], replicated
- grad_slope_mid: float32 [512], replicated
- grad_w_out: float32 [512, 47], replicated
- grad_bias_out: float32 [47], replicated
The draws below stay inside these ranges and needn't reach their ends.
Inputs may be any that keep to these rules, and one draw needn't show every extreme that they name: `buckets`: in each micro-batch, at most 192 of the 512 nodes of one device share a bucket, every bucket is named by at least one of them, and some device has exactly 192 in one bucket.
All inputs are finite; a program needn't handle non-finite values. No bound on the sum of `hop_mask` on one device may be relied on, other than what follows from the above.
Results may differ from the reference program's by a relative error of at most 0.0063.
Values may be sent and summed in bfloat16 or wider, within the bound.
A program may use at most 192 MiB of HBM per device.

```python
import math
import jax
import jax.numpy as jnp
import numpy as np
from jax import lax

FIN = 100
HID = 512
CLS = 47
HOPS = 4
MB = 4
ROWS = 512
BUCKETS = 4
CAP = 192
NODES_MB = 16384


def draw_features(key, part):
    key = jax.random.fold_in(key, 11)
    row_key, column_key, base_key = jax.random.split(key, 3)
    ramp = 1.0 + 2.0 * jnp.arange(NODES_MB, dtype=jnp.float32) / NODES_MB
    row_scale = jnp.exp(jax.random.uniform(row_key, (MB, NODES_MB, 1, 1), minval=-0.69, maxval=0.69)) * ramp[None, :, None, None]
    column_scale = jnp.exp(jax.random.uniform(column_key, (1, 1, HOPS, FIN), minval=-0.69, maxval=0.69))
    values = jax.random.normal(base_key, (MB, NODES_MB, HOPS, FIN)) * row_scale * column_scale
    return jnp.clip(values, -24.0, 24.0).astype(jnp.bfloat16)


def place_ends(result, own_key, smallest, top_value):
    extent = result.shape
    index_at = [jax.random.randint(jax.random.fold_in(own_key, axis), (), 0, extent[axis]) for axis in range(len(extent))]
    result = result.at[tuple(index_at)].set(smallest)
    longest = extent.index(max(extent))
    index_at[longest] = (index_at[longest] + 1) % extent[longest]
    return result.at[tuple(index_at)].set(top_value)


def assign_block(stream_key, own, number, rows, amount, top, limit, skew):
    order = jax.random.permutation(stream_key, amount)
    crowded, usual = shares(amount, rows * top, limit, skew, True), shares(amount, rows * top, limit, skew, False)
    places = jnp.arange(amount)

    def named(lengths, turn):
        used = int((lengths > 0).sum())
        fixed = max(1, used // 4)
        passed = fixed + (places - fixed + turn * (used - fixed)) % max(1, amount - fixed)
        return jnp.zeros((amount,), jnp.int32).at[order[jnp.where(places < fixed, places, passed)]].set(jnp.asarray(lengths, jnp.int32))

    lengths = jnp.where(number % 4 == 0, named(crowded, number // 4), named(usual, number - number // 4 - 1))
    mixed = jax.random.permutation(jax.random.fold_in(own, 3), amount)
    source_of, taker = mixed[0:amount // 2 * 2:2], mixed[1:amount // 2 * 2:2]
    slack = jnp.minimum(lengths[source_of] - 1, limit - lengths[taker]) // 2
    slack = jnp.where((source_of == order[0]) | (taker == order[0]) | (lengths[taker] == 0), 0, jnp.maximum(slack, 0))
    passed = jax.random.randint(jax.random.fold_in(own, 4), (amount // 2,), 0, 1 << 20) % (slack + 1)
    lengths = lengths.at[source_of].add(-passed).at[taker].add(passed)
    items = jnp.searchsorted(jnp.cumsum(lengths), jnp.arange(rows * top), side="right").astype(jnp.int32)
    table = items.reshape(top, rows).T
    table = table[jax.random.permutation(jax.random.fold_in(own, 1), rows)]
    turn = jax.random.randint(jax.random.fold_in(own, 2), (rows, 1), 0, top)
    return jnp.take_along_axis(table, (jnp.arange(top)[None, :] + turn) % top, axis=1)


def shares(amount, total, reach, slope, full):
    portions = [(1 << 20) // math.isqrt(rank ** slope) + 1 for rank in range(1, amount + 1)]
    largest = reach if full else min(reach, max(-(-total // amount), total * portions[0] // sum(portions)))
    least = 1 if total - largest >= amount - 1 else 0
    holding, surplus = [largest] + [least] * (amount - 1), total - largest - least * (amount - 1)
    while surplus > 0:
        movable = [i for i in range(1, amount) if holding[i] < largest] or [i for i in range(1, amount) if holding[i] < reach]
        mass, remaining = sum([portions[i] for i in movable]), surplus
        for i in movable:
            extra = min(reach - holding[i], max(1, remaining * portions[i] // mass), surplus)
            holding[i] = holding[i] + extra
            surplus = surplus - extra
    return np.array(holding)


def normal_values(rng, extent, deviation, bound, kind=jnp.bfloat16):
    entries = jax.random.normal(rng, extent, jnp.float32) * deviation
    return jnp.minimum(jnp.maximum(entries, -bound), bound).astype(kind)


def setup_inputs(seed: int = 0) -> dict:
    key_list = jax.random.split(jax.random.key(seed), 16)
    features = draw_features(jax.random.fold_in(key_list[15], 71), 0)
    buckets_keys = jax.random.split(jax.random.fold_in(key_list[1], 1), MB * NODES_MB // ROWS)
    buckets_turns = jax.random.permutation(jax.random.fold_in(key_list[1], 3), MB * NODES_MB // ROWS)
    buckets = jax.vmap(lambda own, number: assign_block(jax.random.fold_in(key_list[1], 2), own, number, ROWS, BUCKETS, 1, CAP, 2))(buckets_keys, buckets_turns).reshape((MB, NODES_MB, 1))
    hop_mask = place_ends((jax.random.randint(key_list[2], (MB, NODES_MB, HOPS - 1), 0, 4) < 3).astype(jnp.int32), jax.random.fold_in(key_list[2], 1), 0, 1)
    labels = place_ends(jax.random.randint(key_list[3], (MB, NODES_MB), 0, CLS), jax.random.fold_in(key_list[3], 1), 0, CLS - 1).astype(jnp.int32)
    w_hops = normal_values(key_list[4], (HOPS, FIN, HID), FIN ** -0.5, 0.625)
    gain_hops = jnp.clip(1.0 + 0.1 * jax.random.normal(key_list[5], (HOPS, HID), jnp.float32), 0.5, 1.5)
    shift_hops = normal_values(key_list[6], (HOPS, HID), 0.5, 3.0, jnp.float32)
    slope_hops = jnp.clip(jax.random.uniform(key_list[7], (HOPS, HID), jnp.float32, 0.0, 0.5), 0.0, 0.5)
    slope_cat = jnp.clip(jax.random.uniform(key_list[8], (HOPS * HID,), jnp.float32, 0.0, 0.5), 0.0, 0.5)
    w_mid = normal_values(key_list[9], (HOPS * HID, HID), (HOPS * HID) ** -0.5, 0.125)
    gain_mid = jnp.clip(1.0 + 0.1 * jax.random.normal(key_list[10], (HID,), jnp.float32), 0.5, 1.5)
    shift_mid = normal_values(key_list[11], (HID,), 0.5, 3.0, jnp.float32)
    slope_mid = jnp.clip(jax.random.uniform(key_list[12], (HID,), jnp.float32, 0.0, 0.5), 0.0, 0.5)
    w_out = normal_values(key_list[13], (HID, CLS), (HID // 8) ** -0.5, 0.75)
    bias_out = normal_values(key_list[14], (CLS,), 0.5, 3.0, jnp.float32)
    return dict(features=features, buckets=buckets, hop_mask=hop_mask, labels=labels, w_hops=w_hops, gain_hops=gain_hops, shift_hops=shift_hops, slope_hops=slope_hops, slope_cat=slope_cat, w_mid=w_mid, gain_mid=gain_mid, shift_mid=shift_mid, slope_mid=slope_mid, w_out=w_out, bias_out=bias_out)


EPSILON = 1e-05
HIGHEST = lax.Precision.HIGHEST

@jax.custom_vjp
def low(v):
    return lax.optimization_barrier(v.astype(jnp.bfloat16)).astype(jnp.float32)

@jax.custom_vjp
def low_back(v):
    return v

def low_keep(v):
    return (low(v), None)

def low_pass(kept, grad):
    return (grad,)

def back_keep(v):
    return (v, None)

def back_low(kept, grad):
    return (low(grad),)
low.defvjp(low_keep, low_pass)
low_back.defvjp(back_keep, back_low)

def soft_prelu(values, slopes):
    smooth = values * jax.nn.sigmoid(values)
    return smooth + slopes * (values - smooth)

def batch_loss(params, feature_rows, active, member, label_rows):
    w_hops, gain_hops, shift_hops, slope_hops, slope_cat, w_mid, gain_mid, shift_mid, slope_mid, w_out, bias_out = params
    node_count = feature_rows.shape[0]
    pre = low_back(jnp.einsum('nkf,kfc->nkc', feature_rows, w_hops, precision=HIGHEST))
    weighted = member[:, :, None] * active[:, None, :]
    counts = lax.optimization_barrier(jnp.sum(weighted, axis=0))
    sum_first = jnp.einsum('ngk,nkc->gkc', weighted, pre, precision=HIGHEST)
    sum_second = jnp.einsum('ngk,nkc->gkc', weighted, pre * pre, precision=HIGHEST)
    bucket_mean = sum_first / counts[:, :, None]
    bucket_inv = lax.rsqrt(sum_second / counts[:, :, None] - bucket_mean * bucket_mean + EPSILON)
    mean_rows = jnp.einsum('ng,gkc->nkc', member, bucket_mean, precision=HIGHEST)
    inv_rows = jnp.einsum('ng,gkc->nkc', member, bucket_inv, precision=HIGHEST)
    normed = (pre - mean_rows) * inv_rows
    shaped = gain_hops * normed + shift_hops
    branch = soft_prelu(shaped, slope_hops) * active[:, :, None]
    joined = soft_prelu(branch.reshape(node_count, -1), slope_cat)
    middle = low_back(jnp.dot(low(joined), w_mid, precision=HIGHEST))
    mid_mean = lax.optimization_barrier(jnp.mean(middle, axis=0))
    mid_inv = lax.rsqrt(lax.optimization_barrier(jnp.mean(middle * middle, axis=0)) - mid_mean * mid_mean + EPSILON)
    mid_norm = (middle - mid_mean) * mid_inv
    outer = soft_prelu(gain_mid * mid_norm + shift_mid, slope_mid)
    logits = low_back(jnp.dot(low(outer), w_out, precision=HIGHEST)) + bias_out
    log_probs = jax.nn.log_softmax(logits, axis=-1)
    picked = jnp.take_along_axis(log_probs, label_rows[:, None], axis=1)
    return -jnp.sum(picked)

def reference(features, buckets, hop_mask, labels, w_hops, gain_hops, shift_hops, slope_hops, slope_cat, w_mid, gain_mid, shift_mid, slope_mid, w_out, bias_out):
    total_nodes = MB * NODES_MB
    params = (w_hops.astype(jnp.float32), gain_hops.astype(jnp.float32), shift_hops.astype(jnp.float32), slope_hops.astype(jnp.float32), slope_cat.astype(jnp.float32), w_mid.astype(jnp.float32), gain_mid.astype(jnp.float32), shift_mid.astype(jnp.float32), slope_mid.astype(jnp.float32), w_out.astype(jnp.float32), bias_out.astype(jnp.float32))
    feature_data = features.astype(jnp.float32)
    active = jnp.concatenate([jnp.ones((MB, NODES_MB, 1), jnp.float32), hop_mask.astype(jnp.float32)], axis=2)
    member = (buckets[:, :, 0][:, :, None] == jnp.arange(BUCKETS, dtype=jnp.int32)[None, None, :]).astype(jnp.float32)

    def whole_loss(param_list, feature_list):

        def one_batch(running, pieces):
            rows_f, active_f, member_f, labels_f = pieces
            return (running + jax.checkpoint(batch_loss)(param_list, rows_f, active_f, member_f, labels_f), None)
        summed, unused = lax.scan(one_batch, jnp.zeros((), jnp.float32), (feature_list, active, member, labels))
        return summed / total_nodes
    loss, pullback = jax.vjp(whole_loss, params, feature_data)
    param_grads, feature_grads = pullback(jnp.ones((), jnp.float32))
    return (loss, feature_grads * total_nodes, param_grads[0], param_grads[1], param_grads[2], param_grads[3], param_grads[4], param_grads[5], param_grads[6], param_grads[7], param_grads[8], param_grads[9], param_grads[10])
```

```python
import functools

import jax
import jax.numpy as jnp
from jax import lax
from jax.experimental import pallas as pl
from jax.experimental.pallas import tpu as pltpu
from jax.sharding import PartitionSpec as P

F32 = jnp.float32
BF16 = jnp.bfloat16
EPSILON = 1e-05
MESH = pl.DeviceIdType.MESH
LANES = 128
HOT = 112
NN, NT, TN = ((1,), (0,)), ((1,), (1,)), ((0,), (0,))


def dot(left, right, dims=NN):
    return lax.dot_general(left, right, (dims, ((), ())), preferred_element_type=F32)


def split_high(values):
    high = values.astype(BF16)
    return high, (values - high.astype(F32)).astype(BF16)


class Place:
    def __init__(self, groups, dps):
        self.groups, self.dps = groups, dps
        self.high = 4
        self.low = dps // self.high
        self.wide = groups // 2
        self.b = lax.axis_index("bucket")
        self.d = lax.axis_index("dp")
        self.core = lax.rem(self.b, 2)
        self.x = lax.div(self.b, 2)
        self.lo = lax.rem(self.d, self.low)
        self.hi = lax.div(self.d, self.low)

    def at(self, b=None, d=None):
        return {"bucket": self.b if b is None else b, "dp": self.d if d is None else d}

    def bucket(self, o):
        b = lax.rem(self.b + o, self.groups)
        return b, self.at(b=b)

    def dp(self, o):
        d = lax.rem(self.d + o, self.dps)
        return d, self.at(d=d)

    def axis(self, name):
        if name == "core":
            return self.core, 2, lambda o: (1 - self.core, self.at(b=2 * self.x + 1 - self.core))
        if name == "wide":
            def peer(o):
                i = lax.rem(self.x + o, self.wide)
                return i, self.at(b=2 * i + self.core)
            return self.x, self.wide, peer
        if name == "low":
            def peer(o):
                i = lax.rem(self.lo + o, self.low)
                return i, self.at(d=self.hi * self.low + i)
            return self.lo, self.low, peer

        def peer(o):
            i = lax.rem(self.hi + o, self.high)
            return i, self.at(d=i * self.low + self.lo)
        return self.hi, self.high, peer


def remote(src, dst, sems, index, device):
    send, recv = sems
    return pltpu.make_async_remote_copy(
        src_ref=src,
        dst_ref=dst,
        send_sem=send.at[index],
        recv_sem=recv.at[index],
        device_id=device,
        device_id_type=MESH,
    )


class SmallSum:
    def __init__(self, place, near, far, total, near_sems, far_sems):
        self.place, self.near, self.far, self.total = place, near, far, total
        self.near_sems, self.far_sems = near_sems, far_sems

    def own(self, m):
        return self.near.at[m, self.place.b]

    def near_copies(self, m):
        mine = self.near.at[m, self.place.b]
        return [
            remote(mine, mine, self.near_sems, (m, o - 1), self.place.bucket(o)[1])
            for o in range(1, self.place.groups)
        ]

    def far_copies(self, m):
        mine = self.far.at[m, self.place.d]
        return [
            remote(mine, mine, self.far_sems, (m, o - 1), self.place.dp(o)[1])
            for o in range(1, self.place.dps)
        ]

    def start(self, m):
        for copy in self.near_copies(m):
            copy.start()

    def forward(self, m):
        for copy in self.near_copies(m):
            copy.wait()
        total = self.near[m, 0]
        for i in range(1, self.place.groups):
            total = total + self.near[m, i]
        self.far[m, self.place.d] = total
        for copy in self.far_copies(m):
            copy.start()

    def finish(self, m):
        for copy in self.far_copies(m):
            copy.wait()
        total = self.far[m, 0]
        for i in range(1, self.place.dps):
            total = total + self.far[m, i]
        self.total[m] = total


class TableSum:
    def __init__(self, place, table, near, far, total, near_sems, far_sems, back_sems):
        self.place, self.table, self.near, self.far, self.total = place, table, near, far, total
        self.near_sems, self.far_sems, self.back_sems = near_sems, far_sems, back_sems
        self.rows = table.shape[1] // place.groups

    def share(self, b):
        return pl.ds(pl.multiple_of(b * self.rows, 8), self.rows)

    def near_copies(self, m):
        mine = self.near.at[m, self.place.b]
        copies = []
        for o in range(1, self.place.groups):
            b, device = self.place.bucket(o)
            copies.append(remote(self.table.at[m, self.share(b)], mine, self.near_sems, (m, o - 1), device))
        return copies

    def far_copies(self, m):
        mine = self.far.at[m, self.place.d]
        return [
            remote(mine, mine, self.far_sems, (m, o - 1), self.place.dp(o)[1])
            for o in range(1, self.place.dps)
        ]

    def back_copies(self, m):
        mine = self.total.at[m, self.share(self.place.b)]
        return [
            remote(mine, mine, self.back_sems, (m, o - 1), self.place.bucket(o)[1])
            for o in range(1, self.place.groups)
        ]

    def start(self, m):
        for copy in self.near_copies(m):
            copy.start()
        self.near[m, self.place.b] = self.table[m, self.share(self.place.b)]

    def forward(self, m):
        for copy in self.near_copies(m):
            copy.wait()
        total = self.near[m, 0]
        for i in range(1, self.place.groups):
            total = total + self.near[m, i]
        self.far[m, self.place.d] = total
        for copy in self.far_copies(m):
            copy.start()

    def back(self, m):
        for copy in self.far_copies(m):
            copy.wait()
        total = self.far[m, 0]
        for i in range(1, self.place.dps):
            total = total + self.far[m, i]
        self.total[m, self.share(self.place.b)] = total
        for copy in self.back_copies(m):
            copy.start()

    def finish(self, m):
        for copy in self.back_copies(m):
            copy.wait()


class GradSum:
    def __init__(self, place, part, total, stages, sems):
        self.part, self.total, self.stages, self.sems = part, total, stages, sems
        rows = part.shape[0]
        core, wide, low, high = (place.axis(n) for n in ("core", "wide", "low", "high"))
        self.steps = []
        half, quarter = rows // 2, rows // 4
        base = core[0] * half
        self.steps.append([(core, 0, half, 0, 0)])
        second, third, fourth = [], [], []
        used = 1
        for h, (first, then) in enumerate(((wide, low), (low, wide))):
            start = base + h * quarter
            size = quarter // first[1]
            second.append((first, start, size, 1 + 3 * h, used))
            used += first[1] - 1
            start = start + first[0] * size
            size = size // then[1]
            third.append((then, start, size, 2 + 3 * h, used))
            used += then[1] - 1
            start = start + then[0] * size
            self.shared = size % (16 * high[1]) != 0
            size = size if self.shared else size // high[1]
            fourth.append((high, start, size, 3 + 3 * h, used))
            used += high[1] - 1
        self.steps += [second, third, fourth]

    @staticmethod
    def stage_shapes(rows, columns, wide, low, high):
        half, quarter = rows // 2, rows // 4
        shapes, used = [(1, half, columns)], 1
        for first, then in ((wide, low), (low, wide)):
            size = quarter
            for n in (first, then):
                size //= n
                shapes.append((n - 1, size, columns))
                used += n - 1
            if size % (16 * high):
                shapes.append((high, size, columns))
            else:
                shapes.append((high - 1, size // high, columns))
            used += high - 1
        assert size % 16 == 0
        return shapes, used

    def rows(self, base, size, index):
        return pl.ds(pl.multiple_of(base + index * size, 16), size)

    def whole(self, step):
        return self.shared and step == len(self.steps) - 1

    def down(self, step):
        copies = []
        for (own, n, peer), base, size, slot, sem in self.steps[step]:
            for o in range(1, n):
                i, device = peer(o)
                if self.whole(step):
                    src = self.part.at[self.rows(base, size, 0)]
                    copies.append(remote(src, self.stages[slot].at[own], self.sems[:2], sem + o - 1, device))
                    continue
                src = self.part.at[self.rows(base, size, i)]
                copies.append(remote(src, self.stages[slot].at[o - 1], self.sems[:2], sem + o - 1, device))
        return copies

    def up(self, step):
        copies = []
        for (own, n, peer), base, size, slot, sem in [] if self.whole(step) else self.steps[step]:
            mine = self.total.at[self.rows(base, size, own)]
            for o in range(1, n):
                copies.append(remote(mine, mine, self.sems[2:], sem + o - 1, peer(o)[1]))
        return copies

    def start_down(self, step):
        for copy in self.down(step):
            copy.start()

    def end_down(self, step):
        for copy in self.down(step):
            copy.wait()
        last = step == len(self.steps) - 1
        for (own, n, peer), base, size, slot, sem in self.steps[step]:
            piece = min(size, 64)
            if self.whole(step):
                rows = self.rows(base, size, 0)
                self.stages[slot][own] = self.part[rows]
                self.total[rows] = sum(self.stages[slot][i].astype(F32) for i in range(n)).astype(BF16)
                continue

            def add(i, carry):
                rows = pl.ds(pl.multiple_of(base + own * size + i * piece, 16), piece)
                there = pl.ds(pl.multiple_of(i * piece, 16), piece)
                total = self.part[rows].astype(F32)
                for o in range(1, n):
                    total = total + self.stages[slot][o - 1, there].astype(F32)
                (self.total if last else self.part)[rows] = total.astype(BF16)
                return carry

            lax.fori_loop(0, size // piece, add, 0)

    def start_up(self, step):
        for copy in self.up(step):
            copy.start()

    def end_up(self, step):
        for copy in self.up(step):
            copy.wait()


def make_kernel(dims):
    (groups, dps, batches, nodes, hops, feats, width, classes) = dims
    joined_width = hops * width
    pieces = width // LANES
    tables = hops * groups
    nodes_batch = nodes * groups * dps
    total_nodes = batches * nodes_batch
    chunk = 128
    fg_rows = -(-feats // 8) * 8
    lane = [slice(j * LANES, (j + 1) * LANES) for j in range(pieces)]

    def kernel(
        xt_ref, labels_ref, w_ref, gain_ref, shift_ref, slope_ref, slope_cat_ref, w_mid_ref, gain_mid_ref,
        shift_mid_ref, slope_mid_ref, w_out_ref, bias_ref,
        out_features, out_mid, out_rest, out_small,
        u_ref, join_ref, cat_ref, mid_ref, dshaped_ref, dmid_ref, dpre_ref, grad_hops_ref, grad_out_ref,
        gain_rep, shift_rep, tab_a, tab_b, tab_i, tab_e, tab_f, slopes_ref,
        t_in, table_near, table_far, t_total, s_near, s_far, s_total, e_near, e_far, e_total, d_in, d_total,
        part_mid, total_mid, part_rest, total_rest, stages_mid, stages_rest,
        t_sems, s_sems, e_sems, d_sems, mid_sems, rest_sems, out_sems, file_sems,
    ):
        place = Place(groups, dps)
        barrier = pltpu.get_barrier_semaphore()
        for o in range(1, groups):
            pl.semaphore_signal(barrier, inc=1, device_id=place.bucket(o)[1], device_id_type=MESH)
        for o in range(1, dps):
            pl.semaphore_signal(barrier, inc=1, device_id=place.dp(o)[1], device_id_type=MESH)
        pl.semaphore_wait(barrier, groups + dps - 2)

        stats = TableSum(place, t_in, table_near, table_far, t_total, t_sems[0:2], t_sems[2:4], t_sems[4:6])
        heads = SmallSum(place, s_near, s_far, s_total, s_sems[0:2], s_sems[2:4])
        backs = SmallSum(place, e_near, e_far, e_total, e_sems[0:2], e_sems[2:4])
        dots = TableSum(place, d_in, table_near, table_far, d_total, d_sems[0:2], d_sems[2:4], d_sems[4:6])
        mids = GradSum(place, part_mid, total_mid, stages_mid, mid_sems)
        rests = GradSum(place, part_rest, total_rest, stages_rest, rest_sems)
        filled = 2 * tables * pieces

        for k in range(hops):
            for g in range(groups):
                gain_rep[k * groups + g : k * groups + g + 1] = gain_ref[k : k + 1]
                shift_rep[k * groups + g : k * groups + g + 1] = shift_ref[k : k + 1]
        grad_hops_ref[...] = jnp.zeros_like(grad_hops_ref)
        grad_out_ref[...] = jnp.zeros_like(grad_out_ref)
        slopes_ref[...] = jnp.zeros_like(slopes_ref)

        def loop(body):
            def step(m, carry):
                body(m)
                return carry

            lax.fori_loop(0, batches, step, 0)

        def moments(m):
            t_in[m, filled:] = jnp.zeros((t_in.shape[1] - filled, LANES), F32)
            for k in range(hops):
                xt = xt_ref[m, k]
                hot = xt_ref[m, k, HOT:LANES]
                pre = dot(xt, w_ref[k], TN)
                u_ref[m, k] = pre
                square = (pre * pre).astype(BF16)
                second = dot(hot, square)
                sums = jnp.concatenate(split_high(dot(hot, xt, NT)), axis=1)
                first = dot(sums, jnp.concatenate([w_ref[k], w_ref[k]], axis=0))
                for j in range(pieces):
                    base = 2 * tables * j + k * groups
                    t_in[m, base : base + groups] = first[:groups, lane[j]]
                    t_in[m, base + tables : base + tables + groups] = second[:groups, lane[j]]
                hot32 = hot.astype(F32)
                counts = jnp.sum(hot32, axis=1, keepdims=True)
                t_in[m, filled + k * groups : filled + (k + 1) * groups] = jnp.broadcast_to(
                    counts[:groups], (groups, LANES)
                )
                ids = lax.broadcasted_iota(jnp.int32, hot32.shape, 0).astype(F32) + 1.0
                row = jnp.sum(hot32 * ids, axis=0, keepdims=True)
                cat_ref[m, k] = jnp.transpose(jnp.broadcast_to(row, (LANES, nodes))).astype(BF16)

        def moments_step(m):
            moments(m)
            stats.start(m)

        loop(moments_step)
        loop(stats.forward)
        loop(stats.back)

        def bucket_tables(m):
            counts = t_total[m, filled : filled + tables]
            for j in range(pieces):
                base = 2 * tables * j
                mean = t_total[m, base : base + tables] / counts
                second = t_total[m, base + tables : base + 2 * tables] / counts
                inv = lax.rsqrt(second - mean * mean + EPSILON)
                a = 0.5 * gain_rep[:, lane[j]] * inv
                tab_a[m, :, lane[j]] = a
                tab_b[m, :, lane[j]] = 0.5 * shift_rep[:, lane[j]] - a * mean
                tab_i[m, :, lane[j]] = inv

        def choose(masks, table, m, k, j):
            result = table[m, k * groups + groups - 1 : k * groups + groups, lane[j]]
            for g in range(groups - 2, -1, -1):
                result = jnp.where(masks[g], table[m, k * groups + g : k * groups + g + 1, lane[j]], result)
            return result

        def masks_of(m, k, rows):
            cat = cat_ref[m, k, rows].astype(F32)
            return [cat == float(g + 1) for g in range(groups)], cat > 0.0

        def chunks(body):
            for i in range(nodes // chunk):
                body(slice(i * chunk, (i + 1) * chunk))

        def forward(m):
            bucket_tables(m)
            for k in range(hops):
                def part(rows, k=k):
                    masks, active = masks_of(m, k, rows)
                    for j in range(pieces):
                        bend = 0.5 - 0.5 * slope_ref[k : k + 1, lane[j]]
                        bend_cat = 0.5 - 0.5 * slope_cat_ref[k : k + 1, lane[j]]
                        scale = choose(masks, tab_a, m, k, j)
                        offset = jnp.where(active, choose(masks, tab_b, m, k, j), 0.0)
                        u = u_ref[m, k, rows, lane[j]] * scale + offset
                        u_ref[m, k, rows, lane[j]] = u
                        half = u - bend * (u * (1.0 - jnp.tanh(u)))
                        half = half - bend_cat * (half * (1.0 - jnp.tanh(half)))
                        at = slice(k * width + j * LANES, k * width + (j + 1) * LANES)
                        join_ref[m, rows, at] = half.astype(BF16)

                chunks(part)
            middle = dot(join_ref[m], w_mid_ref[...])
            mid_ref[m] = middle
            first = jnp.sum(middle, axis=0, keepdims=True)
            second = jnp.sum(middle * middle, axis=0, keepdims=True)
            own = heads.own(m)
            for j in range(pieces):
                own[j : j + 1] = first[:, lane[j]]
                own[pieces + j : pieces + j + 1] = second[:, lane[j]]

        def forward_step(m):
            stats.finish(m)
            forward(m)
            heads.start(m)

        loop(forward_step)
        loop(heads.forward)

        def row_of(ref, m, first):
            return jnp.concatenate([ref[m, first + j : first + j + 1] for j in range(pieces)], axis=1)

        def head_scale(m):
            mean = row_of(s_total, m, 0) * (1.0 / nodes_batch)
            second = row_of(s_total, m, pieces) * (1.0 / nodes_batch)
            inv = lax.rsqrt(4.0 * (second - mean * mean) + EPSILON)
            return mean, inv

        def head(m):
            mean, inv = head_scale(m)
            scale = gain_mid_ref[...] * inv
            offset = 0.5 * shift_mid_ref[...] - scale * mean
            slope = slope_mid_ref[...]
            u = mid_ref[m] * scale + offset
            mid_ref[m] = u
            tanh = jnp.tanh(u)
            gap = u * (1.0 - tanh)
            outer = (2.0 * u - (1.0 - slope) * gap).astype(BF16)
            logits = dot(w_out_ref[...], outer, NT) + bias_ref[:, 0:1]
            top = jnp.max(logits, axis=0, keepdims=True)
            powers = jnp.exp(logits - top)
            total = jnp.sum(powers, axis=0, keepdims=True)
            wanted = (
                lax.broadcasted_iota(jnp.int32, logits.shape, 0) == labels_ref[m]
            ).astype(F32)
            loss = jnp.log(total) + top - jnp.sum(logits * wanted, axis=0, keepdims=True)
            dlogits = (powers / total - wanted) * (1.0 / total_nodes)
            low = dlogits.astype(BF16)
            grad_out_ref[...] += dot(low, outer)
            douter = dot(low, w_out_ref[...], TN)
            grad_slope = jnp.sum(douter * gap, axis=0, keepdims=True)
            dshaped = douter * (slope + (0.5 - 0.5 * slope) * (1.0 + tanh) * (1.0 + gap))
            dshaped_ref[m] = dshaped
            head_sum = jnp.sum(dshaped, axis=0, keepdims=True)
            head_dot = jnp.sum(dshaped * u, axis=0, keepdims=True)
            own = backs.own(m)
            for j in range(pieces):
                own[j : j + 1] = head_sum[:, lane[j]]
                own[pieces + j : pieces + j + 1] = head_dot[:, lane[j]]
                own[2 * pieces + j : 2 * pieces + j + 1] = grad_slope[:, lane[j]]
            folded = sum(dlogits[:, i * LANES : (i + 1) * LANES] for i in range(nodes // LANES))
            square = jnp.concatenate([folded, jnp.zeros((LANES - folded.shape[0], LANES), F32)], axis=0)
            own[3 * pieces : 3 * pieces + 1] = jnp.sum(jnp.transpose(square), axis=0, keepdims=True)
            own[3 * pieces + 1 : 3 * pieces + 2] = sum(
                loss[:, i * LANES : (i + 1) * LANES] for i in range(nodes // LANES)
            )
            own[3 * pieces + 2 :] = jnp.zeros((own.shape[0] - 3 * pieces - 2, LANES), F32)

        def head_step(m):
            heads.finish(m)
            head(m)
            backs.start(m)

        loop(head_step)
        loop(backs.forward)

        def head_grads(m):
            inv = head_scale(m)[1]
            head_sum = row_of(e_total, m, 0)
            head_dot = (2.0 * row_of(e_total, m, pieces) - shift_mid_ref[...] * head_sum) / gain_mid_ref[...]
            return inv, head_sum, head_dot

        def back_head(m):
            backs.finish(m)
            inv, head_sum, head_dot = head_grads(m)
            scale = gain_mid_ref[...] * inv
            tilt = 2.0 * inv * head_dot * (1.0 / nodes_batch)
            level = scale * head_sum * (1.0 / nodes_batch) - 0.5 * shift_mid_ref[...] * tilt
            dmid_ref[m] = (scale * dshaped_ref[m] - level - mid_ref[m] * tilt).astype(BF16)

        loop(back_head)

        def mid_grad(k, carry):
            at = pl.ds(pl.multiple_of(k * width, width), width)
            total = dot(join_ref[0, :, at], dmid_ref[0], TN)
            for m in range(1, batches):
                total = total + dot(join_ref[m, :, at], dmid_ref[m], TN)
            part_mid[at] = (2.0 * total).astype(BF16)
            return carry

        lax.fori_loop(0, hops, mid_grad, 0)
        mids.start_down(0)

        def backward(m):
            for k in range(hops):
                slope_sums = [jnp.zeros((8, LANES), F32) for _ in range(2 * pieces)]
                at = slice(k * width, (k + 1) * width)
                hot = xt_ref[m, k, HOT:LANES]
                for i in range(nodes // chunk):
                    rows = slice(i * chunk, (i + 1) * chunk)
                    djoined = dot(dmid_ref[m, rows], w_mid_ref[at], NT)
                    masks, active = masks_of(m, k, rows)
                    for j in range(pieces):
                        slope = slope_ref[k : k + 1, lane[j]]
                        slope_cat = slope_cat_ref[k : k + 1, lane[j]]
                        bend, bend_cat = 0.5 - 0.5 * slope, 0.5 - 0.5 * slope_cat
                        u = u_ref[m, k, rows, lane[j]]
                        tanh = jnp.tanh(u)
                        gap = u * (1.0 - tanh)
                        half = u - bend * gap
                        tanh_cat = jnp.tanh(half)
                        gap_cat = half * (1.0 - tanh_cat)
                        grad = djoined[:, lane[j]]
                        slope_sums[pieces + j] += jnp.sum((grad * gap_cat).reshape(-1, 8, LANES), axis=0)
                        grad = grad * (slope_cat + bend_cat * (1.0 + tanh_cat) * (1.0 + gap_cat))
                        slope_sums[j] += jnp.sum((grad * gap).reshape(-1, 8, LANES), axis=0)
                        grad = grad * (slope + bend * (1.0 + tanh) * (1.0 + gap))
                        grad = (grad * choose(masks, tab_a, m, k, j)).astype(BF16)
                        join_ref[m, rows, k * width + j * LANES : k * width + (j + 1) * LANES] = grad
                        dpre_ref[rows, lane[j]] = (grad.astype(F32) * u).astype(BF16)
                first = dot(hot, join_ref[m, :, at])
                second = dot(hot, dpre_ref[...])
                for j in range(pieces):
                    base = 2 * tables * j + k * groups
                    d_in[m, base : base + groups] = first[:groups, lane[j]]
                    d_in[m, base + tables : base + tables + groups] = second[:groups, lane[j]]
                    for s in range(2):
                        row = filled + (s * hops + k) * pieces + j
                        d_in[m, row : row + 1] = jnp.sum(slope_sums[s * pieces + j], axis=0, keepdims=True)
            rest = d_in.shape[1] - filled - 2 * hops * pieces
            if rest:
                d_in[m, filled + 2 * hops * pieces :] = jnp.zeros((rest, LANES), F32)

        def backward_step(m):
            backward(m)
            dots.start(m)

            @pl.when(m == 0)
            def _():
                mids.end_down(0)
                mids.start_down(1)

            @pl.when(m == 1)
            def _():
                mids.end_down(1)
                mids.start_down(2)

            @pl.when(m == 2)
            def _():
                mids.end_down(2)
                mids.start_down(3)

        loop(backward_step)
        loop(dots.forward)
        mids.end_down(3)
        mids.start_up(3)
        loop(dots.back)

        def last_tables(m):
            counts = t_total[m, filled : filled + tables]
            for j in range(pieces):
                base = 2 * tables * j
                a = tab_a[m, :, lane[j]]
                inv = tab_i[m, :, lane[j]]
                shift = shift_rep[:, lane[j]]
                scaled = d_total[m, base : base + tables]
                bucket_sum = scaled / a
                bucket_dot = (2.0 * d_total[m, base + tables : base + 2 * tables] / a - shift * bucket_sum) / gain_rep[
                    :, lane[j]
                ]
                tilt = inv * bucket_dot / counts
                tab_f[m, :, lane[j]] = 2.0 * tilt
                tab_e[m, :, lane[j]] = 2.0 * scaled / counts - shift * tilt
                for k in range(hops):
                    at = slice(k * groups, (k + 1) * groups)
                    slopes_ref[k : k + 1, lane[j]] += jnp.sum(bucket_dot[at], axis=0, keepdims=True)
                    slopes_ref[hops + k : hops + k + 1, lane[j]] += jnp.sum(bucket_sum[at], axis=0, keepdims=True)
                    for s in range(2):
                        row = filled + (s * hops + k) * pieces + j
                        slopes_ref[(2 + s) * hops + k : (2 + s) * hops + k + 1, lane[j]] += d_total[m, row : row + 1]

        def features_copy(m, k):
            return pltpu.make_async_copy(u_ref.at[m, k, :fg_rows], out_features.at[m, k], out_sems.at[m, k])

        def last(m):
            last_tables(m)
            for k in range(hops):
                def part(rows, k=k):
                    masks, _ = masks_of(m, k, rows)
                    for j in range(pieces):
                        at = slice(k * width + j * LANES, k * width + (j + 1) * LANES)
                        grad = 2.0 * join_ref[m, rows, at].astype(F32) - choose(masks, tab_e, m, k, j)
                        grad = grad - choose(masks, tab_f, m, k, j) * u_ref[m, k, rows, lane[j]]
                        dpre_ref[rows, lane[j]] = grad.astype(BF16)

                chunks(part)
                xt = xt_ref[m, k]
                grad_hops_ref[k] += dot(xt, dpre_ref[...])
                active = jnp.sum(xt_ref[m, k, HOT:LANES].astype(F32), axis=0, keepdims=True) * float(total_nodes)
                features = dot(w_ref[k], dpre_ref[...], NT) * active
                u_ref[m, k, :fg_rows] = features[:fg_rows]
                features_copy(m, k).start()

        def last_step(m):
            dots.finish(m)
            last(m)

            @pl.when(m == 0)
            def _():
                mids.end_up(3)
                mids.start_up(2)

            @pl.when(m == 1)
            def _():
                mids.end_up(2)
                mids.start_up(1)

            @pl.when(m == 3)
            def _():
                mids.end_up(1)
                mids.start_up(0)

        loop(last_step)

        stacked = part_rest.shape[0] // 2
        used = hops * HOT
        for k in range(hops):
            rows = grad_hops_ref[k, :HOT]
            part_rest[k * HOT : (k + 1) * HOT] = rows[:, : width // 2].astype(BF16)
            part_rest[stacked + k * HOT : stacked + (k + 1) * HOT] = rows[:, width // 2 :].astype(BF16)
        rows = grad_out_ref[...]
        end = used + rows.shape[0]
        part_rest[used:end] = rows[:, : width // 2].astype(BF16)
        part_rest[stacked + used : stacked + end] = rows[:, width // 2 :].astype(BF16)
        part_rest[end:stacked] = jnp.zeros((stacked - end, width // 2), BF16)
        part_rest[stacked + end :] = jnp.zeros((stacked - end, width // 2), BF16)
        rests.start_down(0)

        for i in range(4 * hops):
            out_small[i : i + 1] = slopes_ref[i : i + 1]
        grad_gain = jnp.zeros((1, width), F32)
        grad_shift = jnp.zeros((1, width), F32)
        grad_slope = jnp.zeros((1, width), F32)
        bias_loss = jnp.zeros((2, LANES), F32)
        for m in range(batches):
            _, head_sum, head_dot = head_grads(m)
            grad_gain = grad_gain + head_dot
            grad_shift = grad_shift + head_sum
            grad_slope = grad_slope + row_of(e_total, m, 2 * pieces)
            bias_loss = bias_loss + e_total[m, 3 * pieces : 3 * pieces + 2]
        out_small[4 * hops : 4 * hops + 1] = grad_gain
        out_small[4 * hops + 1 : 4 * hops + 2] = grad_shift
        out_small[4 * hops + 2 : 4 * hops + 3] = grad_slope
        loss = jnp.sum(bias_loss[1:2], axis=1, keepdims=True) * (1.0 / total_nodes)
        out_small[4 * hops + 3 : 4 * hops + 4] = jnp.concatenate(
            [bias_loss[0:1], jnp.broadcast_to(loss, (1, LANES)), jnp.zeros((1, width - 2 * LANES), F32)], axis=1
        )
        out_small[4 * hops + 4 :] = jnp.zeros((out_small.shape[0] - 4 * hops - 4, width), F32)

        for step in range(3):
            rests.end_down(step)
            rests.start_down(step + 1)
        rests.end_down(3)
        mids.end_up(0)
        mid_file = pltpu.make_async_copy(total_mid, out_mid, file_sems.at[0])
        mid_file.start()
        rests.start_up(3)
        for step in (2, 1, 0):
            rests.end_up(step + 1)
            rests.start_up(step)
        rests.end_up(0)
        rest_file = pltpu.make_async_copy(total_rest, out_rest, file_sems.at[1])
        rest_file.start()
        for m in range(batches):
            for k in range(hops):
                features_copy(m, k).wait()
        mid_file.wait()
        rest_file.wait()

    return kernel


def shards(
    features,
    buckets,
    hop_mask,
    labels,
    w_hops,
    gain_hops,
    shift_hops,
    slope_hops,
    slope_cat,
    w_mid,
    gain_mid,
    shift_mid,
    slope_mid,
    w_out,
    bias_out,
):
    batches, nodes, hops, feats = features.shape
    width, classes = w_out.shape
    groups, dps = lax.axis_size("bucket"), lax.axis_size("dp")
    dims = (groups, dps, batches, nodes, hops, feats, width, classes)
    pieces = width // LANES
    joined_width = hops * width
    tables = hops * groups

    active = jnp.concatenate([jnp.ones((batches, nodes, 1), jnp.int32), hop_mask], axis=2).astype(BF16)
    active = jnp.transpose(active, (0, 2, 1))[:, :, None, :]
    by_hop = jnp.transpose(features, (0, 2, 3, 1))
    hot = (buckets[:, None, None, :, 0] == jnp.arange(LANES - HOT, dtype=jnp.int32)[None, None, :, None]).astype(BF16)
    hot = jnp.broadcast_to(hot, (batches, hops, LANES - HOT, nodes))
    by_hop = jnp.concatenate([jnp.pad(by_hop, ((0, 0), (0, 0), (0, HOT - feats), (0, 0))), hot], axis=2) * active

    padded = -(-classes // 16) * 16
    w_pad = jnp.pad(w_hops, ((0, 0), (0, LANES - feats), (0, 0)))
    out_pad = jnp.pad(w_out.T, ((0, padded - classes), (0, 0)))
    bias_pad = jnp.broadcast_to(
        jnp.pad(bias_out, (0, padded - classes), constant_values=-1e30)[:, None], (padded, LANES)
    )

    wide, low, high = groups // 2, dps // 4, 4
    rows_rest = max(2 * (hops * HOT + 64), 4 * wide * low * 16)
    mid_shapes, mid_sems = GradSum.stage_shapes(joined_width, width, wide, low, high)
    rest_shapes, rest_sems = GradSum.stage_shapes(rows_rest, width // 2, wide, low, high)
    table_rows = -(-(2 * tables * pieces + max(tables, 2 * hops * pieces)) // (8 * groups)) * 8 * groups
    share = table_rows // groups
    fg_rows = -(-feats // 8) * 8
    sem = pltpu.SemaphoreType.DMA

    def small_scratch(rows):
        return [
            pltpu.VMEM((batches, groups, rows, LANES), F32),
            pltpu.VMEM((batches, dps, rows, LANES), F32),
            pltpu.VMEM((batches, rows, LANES), F32),
        ]

    near, far = sem((batches, groups - 1)), sem((batches, dps - 1))
    vmem = pl.BlockSpec(memory_space=pltpu.VMEM)
    hbm = pl.BlockSpec(memory_space=pl.ANY)
    outs = pl.pallas_call(
        make_kernel(dims),
        name="train_step",
        out_shape=(
            jax.ShapeDtypeStruct((batches, hops, fg_rows, nodes), F32),
            jax.ShapeDtypeStruct((joined_width, width), BF16),
            jax.ShapeDtypeStruct((rows_rest, width // 2), BF16),
            jax.ShapeDtypeStruct((24, width), F32),
        ),
        in_specs=[vmem] * 13,
        out_specs=(hbm, hbm, hbm, vmem),
        scratch_shapes=[
            pltpu.VMEM((batches, hops, nodes, width), F32),
            pltpu.VMEM((batches, nodes, joined_width), BF16),
            pltpu.VMEM((batches, hops, nodes, LANES), BF16),
            pltpu.VMEM((batches, nodes, width), F32),
            pltpu.VMEM((batches, nodes, width), F32),
            pltpu.VMEM((batches, nodes, width), BF16),
            pltpu.VMEM((nodes, width), BF16),
            pltpu.VMEM((hops, LANES, width), F32),
            pltpu.VMEM((padded, width), F32),
            pltpu.VMEM((tables, width), F32),
            pltpu.VMEM((tables, width), F32),
        ]
        + [pltpu.VMEM((batches, tables, width), F32) for _ in range(5)]
        + [pltpu.VMEM((4 * hops, width), F32)]
        + [pltpu.VMEM((batches, table_rows, LANES), F32)]
        + [pltpu.VMEM((batches, groups, share, LANES), F32), pltpu.VMEM((batches, dps, share, LANES), F32)]
        + [pltpu.VMEM((batches, table_rows, LANES), F32)]
        + small_scratch(8)
        + small_scratch(16)
        + [pltpu.VMEM((batches, table_rows, LANES), F32) for _ in range(2)]
        + [
            pltpu.VMEM((joined_width, width), BF16),
            pltpu.VMEM((joined_width, width), BF16),
            pltpu.VMEM((rows_rest, width // 2), BF16),
            pltpu.VMEM((rows_rest, width // 2), BF16),
            [pltpu.VMEM(s, BF16) for s in mid_shapes],
            [pltpu.VMEM(s, BF16) for s in rest_shapes],
            [near, near, far, far, near, near],
            [near, near, far, far],
            [near, near, far, far],
            [near, near, far, far, near, near],
            [sem((mid_sems,)) for _ in range(4)],
            [sem((rest_sems,)) for _ in range(4)],
            sem((batches, hops)),
            sem((2,)),
        ],
        compiler_params=pltpu.CompilerParams(
            collective_id=0, has_side_effects=True, vmem_limit_bytes=63 * 2**20
        ),
    )(
        by_hop,
        labels[:, None, :],
        w_pad,
        gain_hops,
        shift_hops,
        slope_hops,
        slope_cat.reshape(hops, width),
        w_mid,
        gain_mid[None],
        shift_mid[None],
        slope_mid[None],
        out_pad,
        bias_pad,
    )
    by_hop_grad, mid_grad, rest_grad, small = outs
    features_grad = jnp.transpose(by_hop_grad[:, :, :feats, :], (0, 3, 1, 2))
    stacked = rows_rest // 2
    rest_grad = jnp.concatenate([rest_grad[:stacked], rest_grad[stacked:]], axis=1).astype(F32)
    grad_hops = rest_grad[: hops * HOT].reshape(hops, HOT, width)[:, :feats]
    grad_out = rest_grad[hops * HOT : hops * HOT + classes].T
    return (
        small[4 * hops + 3, LANES],
        features_grad,
        grad_hops,
        small[0:hops],
        small[hops : 2 * hops],
        small[2 * hops : 3 * hops],
        small[3 * hops : 4 * hops].reshape(joined_width),
        mid_grad.astype(F32),
        small[4 * hops],
        small[4 * hops + 1],
        small[4 * hops + 2],
        grad_out,
        small[4 * hops + 3, :classes],
    )


def solution(mesh):
    nodes_split = ("bucket", "dp")
    placed = (
        P(None, nodes_split, None, None),
        P(None, nodes_split, None),
        P(None, nodes_split, None),
        P(None, nodes_split),
    ) + (P(),) * 11
    return jax.shard_map(
        shards,
        mesh=mesh,
        in_specs=placed,
        out_specs=(P(), P(None, nodes_split, None, None)) + (P(),) * 11,
        check_vma=False,
    )
```

```python
import functools

import jax
import jax.numpy as jnp
from jax import lax
from jax.experimental import pallas as pl
from jax.experimental.pallas import tpu as pltpu
from jax.sharding import PartitionSpec as P

F32 = jnp.float32
BF16 = jnp.bfloat16
EPSILON = 1e-05
MESH = pl.DeviceIdType.MESH
LANES = 128
HOT = 112
SPARE = 104
MID_ORDERS = (("wide", "low", "high"), ("low", "wide", "high"))
REST_ORDERS = (("plane", "high"),)
NN, NT, TN = ((1,), (0,)), ((1,), (1,)), ((0,), (0,))


def dot(left, right, dims=NN):
    return lax.dot_general(left, right, (dims, ((), ())), preferred_element_type=F32)


def split_high(values):
    high = values.astype(BF16)
    return high, (values - high.astype(F32)).astype(BF16)


class Place:
    def __init__(self, groups, dps):
        self.groups, self.dps = groups, dps
        self.high = 4
        self.low = dps // self.high
        self.wide = groups // 2
        self.b = lax.axis_index("bucket")
        self.d = lax.axis_index("dp")
        self.core = lax.rem(self.b, 2)
        self.x = lax.div(self.b, 2)
        self.lo = lax.rem(self.d, self.low)
        self.hi = lax.div(self.d, self.low)
        self.fold, self.nears, self.fars = self.group_sizes(groups, dps)
        self.near = self.b * self.fold + lax.rem(self.d, self.fold)
        self.far = lax.div(self.d, self.fold)

    @staticmethod
    def group_sizes(groups, dps):
        low = dps // 4
        fold = low if groups * low <= 8 else 1
        return fold, groups * fold, dps // fold

    def at(self, b=None, d=None):
        return {"bucket": self.b if b is None else b, "dp": self.d if d is None else d}

    def near_peer(self, o):
        i = lax.rem(self.near + o, self.nears)
        b, lo = lax.div(i, self.fold), lax.rem(i, self.fold)
        return i, self.at(b=b, d=lax.div(self.d, self.fold) * self.fold + lo)

    def far_peer(self, o):
        i = lax.rem(self.far + o, self.fars)
        return i, self.at(d=i * self.fold + lax.rem(self.d, self.fold))

    def axis(self, name):
        if name == "core":
            return self.core, 2, lambda o: (1 - self.core, self.at(b=2 * self.x + 1 - self.core))
        if name == "wide":
            def peer(o):
                i = lax.rem(self.x + o, self.wide)
                return i, self.at(b=2 * i + self.core)
            return self.x, self.wide, peer
        if name == "low":
            def peer(o):
                i = lax.rem(self.lo + o, self.low)
                return i, self.at(d=self.hi * self.low + i)
            return self.lo, self.low, peer

        if name == "plane":
            own = self.x * self.low + self.lo

            def peer(o):
                i = lax.rem(own + o, self.wide * self.low)
                b = 2 * lax.div(i, self.low) + self.core
                return i, self.at(b=b, d=self.hi * self.low + lax.rem(i, self.low))
            return own, self.wide * self.low, peer

        def peer(o):
            i = lax.rem(self.hi + o, self.high)
            return i, self.at(d=i * self.low + self.lo)
        return self.hi, self.high, peer


def remote(src, dst, sems, index, device):
    send, recv = sems
    return pltpu.make_async_remote_copy(
        src_ref=src,
        dst_ref=dst,
        send_sem=send.at[index],
        recv_sem=recv.at[index],
        device_id=device,
        device_id_type=MESH,
    )


class SmallSum:
    def __init__(self, place, near, far, total, near_sems, far_sems):
        self.place, self.near, self.far, self.total = place, near, far, total
        self.near_sems, self.far_sems = near_sems, far_sems

    def own(self, m):
        return self.near.at[m, self.place.near]

    def near_copies(self, m):
        mine = self.near.at[m, self.place.near]
        return [
            remote(mine, mine, self.near_sems, (m, o - 1), self.place.near_peer(o)[1])
            for o in range(1, self.place.nears)
        ]

    def far_copies(self, m):
        mine = self.far.at[m, self.place.far]
        return [
            remote(mine, mine, self.far_sems, (m, o - 1), self.place.far_peer(o)[1])
            for o in range(1, self.place.fars)
        ]

    def start(self, m):
        for copy in self.near_copies(m):
            copy.start()

    def forward(self, m):
        for copy in self.near_copies(m):
            copy.wait()
        self.far[m, self.place.far] = sum(self.near[m, i] for i in range(self.place.nears))
        for copy in self.far_copies(m):
            copy.start()

    def finish(self, m):
        for copy in self.far_copies(m):
            copy.wait()
        self.total[m] = sum(self.far[m, i] for i in range(self.place.fars))


class TableSum:
    def __init__(self, place, table, near, far, total, near_sems, far_sems, back_sems):
        self.place, self.table, self.near, self.far, self.total = place, table, near, far, total
        self.near_sems, self.far_sems, self.back_sems = near_sems, far_sems, back_sems
        self.rows = table.shape[1] // place.nears

    def share(self, i):
        return pl.ds(pl.multiple_of(i * self.rows, 8), self.rows)

    def near_copies(self, m):
        mine = self.near.at[m, self.place.near]
        copies = []
        for o in range(1, self.place.nears):
            i, device = self.place.near_peer(o)
            copies.append(remote(self.table.at[m, self.share(i)], mine, self.near_sems, (m, o - 1), device))
        return copies

    def far_copies(self, m):
        mine = self.far.at[m, self.place.far]
        return [
            remote(mine, mine, self.far_sems, (m, o - 1), self.place.far_peer(o)[1])
            for o in range(1, self.place.fars)
        ]

    def back_copies(self, m):
        mine = self.total.at[m, self.share(self.place.near)]
        return [
            remote(mine, mine, self.back_sems, (m, o - 1), self.place.near_peer(o)[1])
            for o in range(1, self.place.nears)
        ]

    def start(self, m):
        for copy in self.near_copies(m):
            copy.start()
        self.near[m, self.place.near] = self.table[m, self.share(self.place.near)]

    def forward(self, m):
        for copy in self.near_copies(m):
            copy.wait()
        self.far[m, self.place.far] = sum(self.near[m, i] for i in range(self.place.nears))
        for copy in self.far_copies(m):
            copy.start()

    def back(self, m):
        for copy in self.far_copies(m):
            copy.wait()
        self.total[m, self.share(self.place.near)] = sum(self.far[m, i] for i in range(self.place.fars))
        for copy in self.back_copies(m):
            copy.start()

    def finish(self, m):
        for copy in self.back_copies(m):
            copy.wait()


class GradSum:
    def __init__(self, place, part, total, stages, sems, orders):
        self.part, self.total, self.stages, self.sems = part, total, stages, sems
        half = part.shape[0] // 2
        core = place.axis("core")
        self.steps = [[(core, 0, half, 0, 0)]] + [[] for _ in orders[0]]
        slot, used = 1, 1
        for h, order in enumerate(orders):
            size = half // len(orders)
            start = core[0] * half + h * size
            for i, name in enumerate(order):
                axis = place.axis(name)
                self.shared = i == len(order) - 1 and size % (16 * axis[1]) != 0
                if not self.shared:
                    size = size // axis[1]
                self.steps[i + 1].append((axis, start, size, slot, used))
                start = start + axis[0] * size
                slot, used = slot + 1, used + axis[1] - 1

    @staticmethod
    def stage_shapes(rows, columns, orders, sizes):
        shapes, used = [(1, rows // 2, columns)], 1
        for order in orders:
            size = rows // 2 // len(orders)
            for i, name in enumerate(order):
                n = sizes[name]
                if i == len(order) - 1 and size % (16 * n):
                    shapes.append((n, size, columns))
                else:
                    size //= n
                    shapes.append((n - 1, size, columns))
                used += n - 1
            assert size % 16 == 0
        return shapes, used

    def rows(self, base, size, index):
        return pl.ds(pl.multiple_of(base + index * size, 16), size)

    def whole(self, step):
        return self.shared and step == len(self.steps) - 1

    def down(self, step):
        copies = []
        for (own, n, peer), base, size, slot, sem in self.steps[step]:
            for o in range(1, n):
                i, device = peer(o)
                if self.whole(step):
                    src = self.part.at[self.rows(base, size, 0)]
                    copies.append(remote(src, self.stages[slot].at[own], self.sems[:2], sem + o - 1, device))
                    continue
                src = self.part.at[self.rows(base, size, i)]
                copies.append(remote(src, self.stages[slot].at[o - 1], self.sems[:2], sem + o - 1, device))
        return copies

    def up(self, step):
        copies = []
        for (own, n, peer), base, size, slot, sem in [] if self.whole(step) else self.steps[step]:
            mine = self.total.at[self.rows(base, size, own)]
            for o in range(1, n):
                copies.append(remote(mine, mine, self.sems[2:], sem + o - 1, peer(o)[1]))
        return copies

    def start_down(self, step):
        for copy in self.down(step):
            copy.start()

    def end_down(self, step):
        for copy in self.down(step):
            copy.wait()
        last = step == len(self.steps) - 1
        for (own, n, peer), base, size, slot, sem in self.steps[step]:
            piece = min(size, 64)
            if self.whole(step):
                rows = self.rows(base, size, 0)
                self.stages[slot][own] = self.part[rows]
                self.total[rows] = sum(self.stages[slot][i].astype(F32) for i in range(n)).astype(BF16)
                continue

            def add(i, carry):
                rows = pl.ds(pl.multiple_of(base + own * size + i * piece, 16), piece)
                there = pl.ds(pl.multiple_of(i * piece, 16), piece)
                total = self.part[rows].astype(F32)
                for o in range(1, n):
                    total = total + self.stages[slot][o - 1, there].astype(F32)
                (self.total if last else self.part)[rows] = total.astype(BF16)
                return carry

            lax.fori_loop(0, size // piece, add, 0)

    def start_up(self, step):
        for copy in self.up(step):
            copy.start()

    def end_up(self, step):
        for copy in self.up(step):
            copy.wait()

    def advance(self, stage):
        last = len(self.steps) - 1
        if stage <= last:
            self.end_down(stage)
            if stage < last:
                self.start_down(stage + 1)
            else:
                self.start_up(last)
        else:
            step = 2 * last + 1 - stage
            self.end_up(step)
            if step:
                self.start_up(step - 1)


def make_kernel(dims):
    (groups, dps, batches, nodes, hops, feats, width, classes) = dims
    pieces = width // LANES
    tables = hops * groups
    nodes_batch = nodes * groups * dps
    total_nodes = batches * nodes_batch
    chunk = 128
    final = batches - 1
    lane = [slice(j * LANES, (j + 1) * LANES) for j in range(pieces)]
    columns = [slice(k * width, (k + 1) * width) for k in range(hops)]

    def kernel(
        x_in, bucket_ref, mask_ref, labels_ref, w_in, gain_ref, shift_ref, slope_ref, slope_cat_ref, w_mid_in,
        gain_mid_ref, shift_mid_ref, slope_mid_ref, w_out_in, bias_in,
        out_features, out_mid, out_rest, out_small,
        spread, u_ref, join_ref, xt_ref, cat_ref, mid_ref, dshaped_ref, dmid_ref, grad_hops_ref, grad_out_ref,
        w_ref, w_mid_ref, w_out_ref, bias_ref, gain_rep, shift_rep, tab_a, tab_b, tab_e, tab_f, slopes_ref,
        table, table_near, table_far, t_total, s_near, s_far, s_total, e_near, e_far, e_total, c_near, c_far, c_total,
        part_mid, total_mid, part_rest, total_rest, stages_mid, stages_rest,
        t_sems, s_sems, e_sems, c_sems, d_sems, mid_sems, rest_sems, in_sems, out_sems, file_sems,
    ):
        spread_rows = feats * pieces * hops
        place = Place(groups, dps)
        barrier = pltpu.get_barrier_semaphore()
        for o in range(1, place.nears):
            pl.semaphore_signal(barrier, inc=1, device_id=place.near_peer(o)[1], device_id_type=MESH)
        for o in range(1, place.fars):
            pl.semaphore_signal(barrier, inc=1, device_id=place.far_peer(o)[1], device_id_type=MESH)

        def landing(ref, m):
            return ref.at[pl.ds(0, spread_rows), pl.ds(pl.multiple_of(m * LANES, LANES), LANES)]

        def x_copy(m):
            return pltpu.make_async_copy(x_in.at[m], landing(part_mid, m), in_sems.at[m])

        w_copy = pltpu.make_async_copy(w_in, landing(total_mid, 0), file_sems.at[1])
        w_mid_copy = pltpu.make_async_copy(w_mid_in, w_mid_ref, file_sems.at[2])
        w_copy.start()
        for m in range(batches):
            x_copy(m).start()
        w_mid_copy.start()

        stats = TableSum(place, table, table_near, table_far, t_total, t_sems[0:2], t_sems[2:4], t_sems[4:6])
        heads = SmallSum(place, s_near, s_far, s_total, s_sems[0:2], s_sems[2:4])
        backs = SmallSum(place, e_near, e_far, e_total, e_sems[0:2], e_sems[2:4])
        dots = TableSum(place, table, table_near, table_far, t_total, d_sems[0:2], d_sems[2:4], d_sems[4:6])
        amounts = SmallSum(place, c_near, c_far, c_total, c_sems[0:2], c_sems[2:4])
        mids = GradSum(place, part_mid, total_mid, stages_mid, mid_sems, MID_ORDERS)
        rests = GradSum(place, part_rest, total_rest, stages_rest, rest_sems, REST_ORDERS)

        def loop(first, last, body):
            def step(m, carry):
                body(m)
                return carry

            lax.fori_loop(first, last, step, 0)

        def at(m, when, body):
            pl.when(m == when)(body)

        spread[spread_rows:] = jnp.zeros((spread.shape[0] - spread_rows, LANES), F32)

        def hop_rows(k):
            parts = [spread[pl.ds(j * hops + k, HOT, stride=pieces * hops)] for j in range(pieces)]
            return jnp.concatenate(parts, axis=1)

        w_copy.wait()
        spread[:spread_rows] = landing(total_mid, 0)[...].astype(F32)
        for k in range(hops):
            w_ref[k] = jnp.concatenate([hop_rows(k), jnp.zeros((LANES - HOT, width), F32)], axis=0).astype(BF16)
            for g in range(groups):
                gain_rep[k * groups + g : k * groups + g + 1] = gain_ref[k : k + 1]
                shift_rep[k * groups + g : k * groups + g + 1] = shift_ref[k : k + 1]
        w_out_ref[...] = jnp.zeros_like(w_out_ref)
        w_out_ref[:classes] = w_out_in[...]
        bias_ref[...] = jnp.full(bias_ref.shape, -1e30, F32)
        bias_ref[0:1, :classes] = bias_in[...]
        bias_row = jnp.broadcast_to(bias_ref[0:1], (LANES, LANES))
        bias_ref[...] = jnp.transpose(bias_row)[: bias_ref.shape[0]]
        grad_hops_ref[...] = jnp.zeros_like(grad_hops_ref)
        grad_out_ref[...] = jnp.zeros_like(grad_out_ref)
        slopes_ref[...] = jnp.zeros_like(slopes_ref)

        def hot_rows(m):
            ids = lax.broadcasted_iota(jnp.int32, (LANES - HOT, nodes), 0)
            return (ids == bucket_ref[m]).astype(F32)

        def active_row(m, k):
            if k == 0:
                return jnp.ones((1, nodes), F32)
            return mask_ref[k - 1, pl.ds(m, 1)].astype(F32)

        which = lax.broadcasted_iota(jnp.int32, (groups, LANES), 1)
        amount = [jnp.zeros((groups, LANES), F32) for _ in range(hops)]
        for m in range(batches):
            hot = hot_rows(m)
            for k in range(hops):
                here = jnp.sum(hot * active_row(m, k), axis=1, keepdims=True)
                amount[k] = jnp.where(which == m, here[:groups], amount[k])
        for k in range(hops):
            c_near[0, place.near, k * groups : (k + 1) * groups] = amount[k]

        def moments(m):
            x_copy(m).wait()
            spread[:spread_rows] = landing(part_mid, m)[...].astype(F32)
            hot_all = hot_rows(m)
            ids = lax.broadcasted_iota(jnp.int32, hot_all.shape, 0).astype(F32) + 1.0
            for k in range(hops):
                block = jnp.concatenate([hop_rows(k), hot_all], axis=0) * active_row(m, k)
                row = jnp.sum(block[HOT:] * ids, axis=0, keepdims=True)
                cat_ref[m, k] = jnp.transpose(jnp.broadcast_to(row, (LANES, nodes))).astype(BF16)
                xt = block.astype(BF16)
                hot = xt[HOT:]
                xt_ref[m, k] = xt
                pre = dot(xt, w_ref[k], TN)
                u_ref[m, k] = pre
                square = (pre * pre).astype(BF16)
                second = dot(hot, square)
                sums = jnp.concatenate(split_high(dot(hot, xt, NT)), axis=1)
                first = dot(sums, jnp.concatenate([w_ref[k], w_ref[k]], axis=0))
                for j in range(pieces):
                    base = 2 * tables * j + k * groups
                    table[m, base : base + groups] = first[:groups, lane[j]]
                    table[m, base + tables : base + tables + groups] = second[:groups, lane[j]]

        def moments_step(m):
            moments(m)

            @pl.when(m == 0)
            def _():
                pl.semaphore_wait(barrier, place.nears + place.fars - 2)
                amounts.start(0)

            stats.start(m)
            at(m, 2, lambda: amounts.forward(0))
            pl.when(m >= 2)(lambda: stats.forward(m - 2))

        loop(0, batches, moments_step)
        stats.forward(final - 1)
        stats.back(0)
        stats.forward(final)
        stats.back(1)
        amounts.finish(0)
        w_mid_copy.wait()
        stats.finish(0)
        stats.back(final - 1)

        def counts_of(m):
            here = lax.broadcasted_iota(jnp.int32, (tables, LANES), 1) == m
            counts = jnp.sum(jnp.where(here, c_total[0], 0.0), axis=1, keepdims=True)
            return jnp.broadcast_to(counts, (tables, LANES))

        def bucket_tables(m):
            counts = counts_of(m)
            for j in range(pieces):
                base = 2 * tables * j
                mean = t_total[m, base : base + tables] / counts
                second = t_total[m, base + tables : base + 2 * tables] / counts
                inv = lax.rsqrt(second - mean * mean + EPSILON)
                a = 0.5 * gain_rep[:, lane[j]] * inv
                tab_a[m, :, lane[j]] = a
                tab_b[m, :, lane[j]] = 0.5 * shift_rep[:, lane[j]] - a * mean

        def choose(masks, values, k, j):
            result = values[k * groups + groups - 1 : k * groups + groups, lane[j]]
            for g in range(groups - 2, -1, -1):
                result = jnp.where(masks[g], values[k * groups + g : k * groups + g + 1, lane[j]], result)
            return result

        def masks_of(m, k, rows):
            cat = cat_ref[m, k, rows].astype(F32)
            return [cat == float(g + 1) for g in range(groups)], cat > 0.0

        chunks = [slice(i * chunk, (i + 1) * chunk) for i in range(nodes // chunk)]

        def forward(m):
            bucket_tables(m)
            for k in range(hops):
                for rows in chunks:
                    masks, active = masks_of(m, k, rows)
                    for j in range(pieces):
                        bend = 0.5 - 0.5 * slope_ref[k : k + 1, lane[j]]
                        bend_cat = 0.5 - 0.5 * slope_cat_ref[:, k * width + j * LANES : k * width + (j + 1) * LANES]
                        scale = choose(masks, tab_a.at[m], k, j)
                        offset = jnp.where(active, choose(masks, tab_b.at[m], k, j), 0.0)
                        u = u_ref[m, k, rows, lane[j]] * scale + offset
                        u_ref[m, k, rows, lane[j]] = u
                        half = u - (bend * u) * (1.0 - jnp.tanh(u))
                        half = half - (bend_cat * half) * (1.0 - jnp.tanh(half))
                        join_ref[m, rows, k * width + j * LANES : k * width + (j + 1) * LANES] = half.astype(BF16)
            middle = dot(join_ref[m], w_mid_ref[...])
            mid_ref[m] = middle
            first = jnp.sum(middle, axis=0, keepdims=True)
            second = jnp.sum(middle * middle, axis=0, keepdims=True)
            own = heads.own(m)
            for j in range(pieces):
                own[j : j + 1] = first[:, lane[j]]
                own[pieces + j : pieces + j + 1] = second[:, lane[j]]

        def row_of(ref, m, first):
            return jnp.concatenate([ref[m, first + j : first + j + 1] for j in range(pieces)], axis=1)

        def head_scale(m):
            mean = row_of(s_total, m, 0) * (1.0 / nodes_batch)
            second = row_of(s_total, m, pieces) * (1.0 / nodes_batch)
            inv = lax.rsqrt(4.0 * (second - mean * mean) + EPSILON)
            return mean, inv

        def head(m):
            heads.finish(m)
            mean, inv = head_scale(m)
            scale = gain_mid_ref[...] * inv
            offset = 0.5 * shift_mid_ref[...] - scale * mean
            slope = slope_mid_ref[...]
            u = mid_ref[m] * scale + offset
            mid_ref[m] = u
            tanh = jnp.tanh(u)
            gap = u * (1.0 - tanh)
            outer = (2.0 * u - (1.0 - slope) * gap).astype(BF16)
            logits = dot(w_out_ref[...], outer, NT) + bias_ref[:, 0:1]
            top = jnp.max(logits, axis=0, keepdims=True)
            powers = jnp.exp(logits - top)
            total = jnp.sum(powers, axis=0, keepdims=True)
            wanted = (lax.broadcasted_iota(jnp.int32, logits.shape, 0) == labels_ref[pl.ds(m, 1)]).astype(F32)
            loss = jnp.log(total) + top - jnp.sum(logits * wanted, axis=0, keepdims=True)
            dlogits = (powers / total - wanted) * (1.0 / total_nodes)
            low = dlogits.astype(BF16)
            grad_out_ref[...] += dot(low, outer)
            douter = dot(low, w_out_ref[...], TN)
            grad_slope = jnp.sum(douter * gap, axis=0, keepdims=True)
            dshaped = douter * (slope + (0.5 - 0.5 * slope) * (1.0 + tanh) * (1.0 + gap))
            dshaped_ref[m] = dshaped
            head_sum = jnp.sum(dshaped, axis=0, keepdims=True)
            head_dot = jnp.sum(dshaped * u, axis=0, keepdims=True)
            own = backs.own(m)
            for j in range(pieces):
                own[j : j + 1] = head_sum[:, lane[j]]
                own[pieces + j : pieces + j + 1] = head_dot[:, lane[j]]
                own[2 * pieces + j : 2 * pieces + j + 1] = grad_slope[:, lane[j]]
            folded = sum(dlogits[:, i * LANES : (i + 1) * LANES] for i in range(nodes // LANES))
            square = jnp.concatenate([folded, jnp.zeros((LANES - folded.shape[0], LANES), F32)], axis=0)
            own[3 * pieces : 3 * pieces + 1] = jnp.sum(jnp.transpose(square), axis=0, keepdims=True)
            own[3 * pieces + 1 : 3 * pieces + 2] = sum(
                loss[:, i * LANES : (i + 1) * LANES] for i in range(nodes // LANES)
            )
            own[3 * pieces + 2 :] = jnp.zeros((own.shape[0] - 3 * pieces - 2, LANES), F32)
            backs.start(m)

        def head_grads(m):
            inv = head_scale(m)[1]
            head_sum = row_of(e_total, m, 0)
            head_dot = (2.0 * row_of(e_total, m, pieces) - shift_mid_ref[...] * head_sum) / gain_mid_ref[...]
            return inv, head_sum, head_dot

        def back_head(m):
            backs.finish(m)
            inv, head_sum, head_dot = head_grads(m)
            scale = gain_mid_ref[...] * inv
            tilt = 2.0 * inv * head_dot * (1.0 / nodes_batch)
            level = scale * head_sum * (1.0 / nodes_batch) - 0.5 * shift_mid_ref[...] * tilt
            dmid_ref[m] = (scale * dshaped_ref[m] - level - mid_ref[m] * tilt).astype(BF16)

        gradients = [mid_ref.at[0], dshaped_ref.at[0]]
        products = part_rest.at[pl.ds(0, nodes)]

        def backward(m, which_hops, target, tick):
            def into(k):
                gradients[k % 2][...] = dot(dmid_ref[m], w_mid_ref[columns[k]], NT)

            into(which_hops[0])
            for k in which_hops:
                if k + 1 in which_hops:
                    into(k + 1)
                slope_sums = [jnp.zeros((8, LANES), F32) for _ in range(2 * pieces)]
                result = target(k)
                hot = xt_ref[m, k, HOT:LANES]
                for rows in chunks:
                    masks, _ = masks_of(m, k, rows)
                    for j in range(pieces):
                        slope = slope_ref[k : k + 1, lane[j]]
                        slope_cat = slope_cat_ref[:, k * width + j * LANES : k * width + (j + 1) * LANES]
                        bend, bend_cat = 0.5 - 0.5 * slope, 0.5 - 0.5 * slope_cat
                        u = u_ref[m, k, rows, lane[j]]
                        tanh = jnp.tanh(u)
                        gap = (bend * u) * (1.0 - tanh)
                        half = u - gap
                        tanh_cat = jnp.tanh(half)
                        gap_cat = (bend_cat * half) * (1.0 - tanh_cat)
                        grad = gradients[k % 2][rows, lane[j]]
                        slope_sums[pieces + j] += jnp.sum((grad * gap_cat).reshape(-1, 8, LANES), axis=0)
                        grad = grad * (slope_cat + (1.0 + tanh_cat) * (bend_cat + gap_cat))
                        slope_sums[j] += jnp.sum((grad * gap).reshape(-1, 8, LANES), axis=0)
                        grad = grad * (slope + (1.0 + tanh) * (bend + gap))
                        grad = (grad * choose(masks, tab_a.at[m], k, j)).astype(BF16)
                        result[rows, lane[j]] = grad
                        products[rows, lane[j]] = (grad.astype(F32) * u).astype(BF16)
                first = dot(hot, result[...])
                second = dot(hot, products[...])
                for j in range(pieces):
                    base = 2 * tables * j + k * groups
                    table[m, base : base + groups] = first[:groups, lane[j]]
                    table[m, base + tables : base + tables + groups] = second[:groups, lane[j]]
                    slope = slope_ref[k : k + 1, lane[j]]
                    slope_cat = slope_cat_ref[:, k * width + j * LANES : k * width + (j + 1) * LANES]
                    for s, values in enumerate((slope, slope_cat)):
                        grad_hops_ref[k, feats + s : feats + s + 1, lane[j]] += jnp.sum(
                            slope_sums[s * pieces + j], axis=0, keepdims=True
                        ) / (0.5 - 0.5 * values)
                tick(k)

        def first_target(k):
            return total_mid.at[pl.ds(k * nodes, nodes)]

        def first_copy(k):
            return pltpu.make_async_copy(first_target(k), join_ref.at[0, :, pl.ds(k * width, width)], in_sems.at[k])

        def no_tick(k):
            pass

        def forward_step(m):
            pl.when(m >= 1)(lambda: stats.finish(m))
            forward(m)
            heads.start(m)
            pl.when(m >= 1)(lambda: heads.forward(m - 1))
            at(m, 0, lambda: stats.back(final))
            at(m, 2, lambda: head(0))

        loop(0, batches, forward_step)
        backs.forward(0)

        def head_step(m):
            head(m)

            @pl.when(m == 1)
            def _():
                heads.forward(final)

            @pl.when(m == 2)
            def _():
                backs.forward(1)
                back_head(0)
                backward(0, [0, 1], first_target, no_tick)

        loop(1, batches, head_step)
        backs.forward(2)

        def late_tick(k):
            if k == hops - 1:
                backs.forward(final)

        backward(0, list(range(2, hops)), first_target, late_tick)
        dots.start(0)
        for m in range(1, final):
            back_head(m)

        held = [mid_ref.at[m] for m in range(final)] + [dshaped_ref.at[0]]
        for k in range(hops):
            held[k][...] = sum(dot(join_ref[m, :, columns[k]], dmid_ref[m], TN) for m in range(final))
        back_head(final)
        for k in range(hops):
            total = held[k][...] + dot(join_ref[final, :, columns[k]], dmid_ref[final], TN)
            part_mid[columns[k]] = (2.0 * total).astype(BF16)
        mids.start_down(0)
        for k in range(hops):
            first_copy(k).start()
        dots.forward(0)

        def backward_step(m):
            def tick(k):
                if k == 1:
                    at(m, 1, lambda: mids.advance(0))
                    at(m, 3, lambda: dots.back(1))
                if k == 2:
                    at(m, 1, lambda: dots.back(0))
                    at(m, 2, lambda: dots.forward(1))
                    at(m, 2, lambda: mids.advance(1))
                    at(m, 3, lambda: dots.forward(2))
                    at(m, 3, lambda: mids.advance(2))

            backward(m, list(range(hops)), lambda k: join_ref.at[m, :, columns[k]], tick)
            dots.start(m)

        loop(1, batches, backward_step)
        for k in range(hops):
            first_copy(k).wait()

        def last_tables(m):
            counts = counts_of(m)
            for j in range(pieces):
                base = 2 * tables * j
                a = tab_a[m, :, lane[j]]
                inv = 2.0 * a / gain_rep[:, lane[j]]
                shift = shift_rep[:, lane[j]]
                scaled = t_total[m, base : base + tables]
                bucket_sum = scaled / a
                bucket_dot = (2.0 * t_total[m, base + tables : base + 2 * tables] / a - shift * bucket_sum) / gain_rep[
                    :, lane[j]
                ]
                tilt = inv * bucket_dot / counts
                tab_f[:, lane[j]] = tilt
                tab_e[:, lane[j]] = scaled / counts - 0.5 * shift * tilt
                for k in range(hops):
                    here = slice(k * groups, (k + 1) * groups)
                    slopes_ref[k : k + 1, lane[j]] += jnp.sum(bucket_dot[here], axis=0, keepdims=True)
                    slopes_ref[hops + k : hops + k + 1, lane[j]] += jnp.sum(bucket_sum[here], axis=0, keepdims=True)

        def last(m):
            dots.finish(m)
            last_tables(m)
            for k in range(hops):
                for rows in chunks:
                    masks, _ = masks_of(m, k, rows)
                    for j in range(pieces):
                        here = slice(k * width + j * LANES, k * width + (j + 1) * LANES)
                        grad = join_ref[m, rows, here].astype(F32) - choose(masks, tab_e, k, j)
                        grad = grad - choose(masks, tab_f, k, j) * u_ref[m, k, rows, lane[j]]
                        join_ref[m, rows, here] = grad.astype(BF16)
                grad_hops_ref[k, :HOT] += dot(xt_ref[m, k, :HOT], join_ref[m, :, columns[k]]) * 2.0

        def features_copy(m):
            return pltpu.make_async_copy(spread.at[pl.ds(0, spread_rows)], out_features.at[m], out_sems.at[m])

        def features(m):
            pl.when(m >= 1)(lambda: features_copy(m - 1).wait())
            for k in range(hops):
                scale = active_row(m, k) * float(2 * total_nodes)
                values = dot(w_ref[k], join_ref[m, :, columns[k]], NT) * scale
                for j in range(pieces):
                    spread[pl.ds(j * hops + k, feats, stride=pieces * hops)] = values[:feats, lane[j]]
            features_copy(m).start()

        def start_rests():
            rows = grad_out_ref.shape[0] // hops
            for k in range(hops):
                grad_hops_ref[k, SPARE : SPARE + rows] = grad_out_ref[k * rows : (k + 1) * rows]
                part_rest[k * LANES : (k + 1) * LANES] = grad_hops_ref[k].astype(BF16)
            if part_rest.shape[0] > hops * LANES:
                part_rest[hops * LANES :] = jnp.zeros((part_rest.shape[0] - hops * LANES, width), BF16)
            rests.start_down(0)

        def last_step(m):
            last(m)
            at(m, 0, lambda: dots.back(2))
            at(m, 2, lambda: mids.advance(3))
            at(m, 3, start_rests)
            features(m)
            at(m, 0, lambda: dots.forward(final))
            at(m, 1, lambda: dots.back(final))

        loop(0, batches, last_step)
        rests.advance(0)
        mids.advance(4)

        grad_gain = jnp.zeros((1, width), F32)
        grad_shift = jnp.zeros((1, width), F32)
        grad_slope = jnp.zeros((1, width), F32)
        bias_loss = jnp.zeros((2, LANES), F32)
        for m in range(batches):
            _, head_sum, head_dot = head_grads(m)
            grad_gain = grad_gain + head_dot
            grad_shift = grad_shift + head_sum
            grad_slope = grad_slope + row_of(e_total, m, 2 * pieces)
            bias_loss = bias_loss + e_total[m, 3 * pieces : 3 * pieces + 2]
        out_small[: 2 * hops] = slopes_ref[...]
        loss = jnp.sum(bias_loss[1:2], axis=1, keepdims=True) * (1.0 / total_nodes)
        last_row = [bias_loss[0:1], jnp.broadcast_to(loss, (1, LANES)), jnp.zeros((1, width - 2 * LANES), F32)]
        for i, row in enumerate((grad_gain, grad_shift, grad_slope, jnp.concatenate(last_row, axis=1))):
            out_small[2 * hops + i : 2 * hops + i + 1] = row

        rests.advance(1)
        mids.advance(5)
        rests.advance(2)
        rests.advance(3)
        mids.advance(6)
        rests.advance(4)
        mids.advance(7)
        mid_file = pltpu.make_async_copy(total_mid, out_mid, file_sems.at[0])
        mid_file.start()
        rests.advance(5)
        rest_file = pltpu.make_async_copy(total_rest.at[pl.ds(0, hops * LANES)], out_rest, file_sems.at[1])
        rest_file.start()
        features_copy(final).wait()
        mid_file.wait()
        rest_file.wait()

    return kernel


def make_finish(dims):
    (groups, dps, batches, nodes, hops, feats, width, classes) = dims
    pieces = width // LANES
    spare = -(-classes // 16) * 16 // hops

    def kernel(
        features_in, mid_in, rest_in, small_in,
        features, mid, hops_grad, gain, shift, slope, cat, gain_mid, shift_mid, slope_mid, out_grad, bias, loss,
        low, wide, held, sems,
    ):
        in_copy = [pltpu.make_async_copy(features_in.at[m], held.at[m], sems.at[0, m]) for m in range(batches)]
        out_copy = [pltpu.make_async_copy(held.at[m], features.at[m], sems.at[3, m]) for m in range(batches)]
        low_copy = [pltpu.make_async_copy(mid_in.at[pl.ds(k * width, width)], low.at[k], sems.at[1, k]) for k in range(hops)]
        wide_copy = [pltpu.make_async_copy(wide.at[k], mid.at[pl.ds(k * width, width)], sems.at[2, k]) for k in range(hops)]
        for copy in low_copy + in_copy:
            copy.start()
        for k in range(hops):
            values = rest_in[k * LANES : (k + 1) * LANES].astype(F32)
            for j in range(pieces):
                hops_grad[pl.ds(j * hops + k, feats, stride=pieces * hops)] = values[
                    :feats, j * LANES : (j + 1) * LANES
                ]
            slope[k : k + 1] = values[feats : feats + 1]
            cat[:, k * width : (k + 1) * width] = values[feats + 1 : feats + 2]
            count = min(spare, classes - k * spare)
            out_grad[k * spare : k * spare + count] = values[SPARE : SPARE + count]
        gain[...] = small_in[:hops]
        shift[...] = small_in[hops : 2 * hops]
        gain_mid[...] = small_in[2 * hops : 2 * hops + 1]
        shift_mid[...] = small_in[2 * hops + 1 : 2 * hops + 2]
        slope_mid[...] = small_in[2 * hops + 2 : 2 * hops + 3]
        bias[...] = small_in[2 * hops + 3 : 2 * hops + 4, :classes]
        loss[...] = small_in[2 * hops + 3 : 2 * hops + 4, LANES : LANES + 1]
        for k in range(hops):
            low_copy[k].wait()
            wide[k] = low[k].astype(F32)
            wide_copy[k].start()
        for m in range(batches):
            in_copy[m].wait()
            out_copy[m].start()
        for copy in wide_copy + out_copy:
            copy.wait()

    return kernel


def by_piece(values):
    *lead, feats, hops, width = values.shape
    values = jnp.swapaxes(values.reshape(*lead, feats, hops, width // LANES, LANES), -3, -2)
    return values.reshape(*lead, feats * hops * width // LANES, LANES)


def by_hop(rows, hops, pieces):
    *lead, count, _ = rows.shape
    values = rows.reshape(*lead, count // (hops * pieces), pieces, hops, LANES)
    return jnp.swapaxes(values, -3, -2).reshape(*lead, count // (hops * pieces), hops, pieces * LANES)


def shards(
    features,
    buckets,
    hop_mask,
    labels,
    w_hops,
    gain_hops,
    shift_hops,
    slope_hops,
    slope_cat,
    w_mid,
    gain_mid,
    shift_mid,
    slope_mid,
    w_out,
    bias_out,
):
    batches, nodes, hops, feats = features.shape
    width, classes = w_out.shape
    groups, dps = lax.axis_size("bucket"), lax.axis_size("dp")
    dims = (groups, dps, batches, nodes, hops, feats, width, classes)
    pieces = width // LANES
    joined_width = hops * width
    tables = hops * groups
    padded = -(-classes // 16) * 16

    wide, low, high = groups // 2, dps // 4, 4
    sizes = {"wide": wide, "low": low, "high": high, "plane": wide * low}
    rows_rest = max(hops * LANES, 2 * wide * low * 16)
    mid_shapes, mid_sems = GradSum.stage_shapes(joined_width, width, MID_ORDERS, sizes)
    rest_shapes, rest_sems = GradSum.stage_shapes(rows_rest, width, REST_ORDERS, sizes)
    _, nears, fars = Place.group_sizes(groups, dps)
    table_rows = 2 * tables * pieces
    share = table_rows // nears
    sem = pltpu.SemaphoreType.DMA

    def small_scratch(rows, copies=batches):
        return [
            pltpu.VMEM((copies, nears, rows, LANES), F32),
            pltpu.VMEM((copies, fars, rows, LANES), F32),
            pltpu.VMEM((copies, rows, LANES), F32),
        ]

    near, far = sem((batches, nears - 1)), sem((batches, fars - 1))
    vmem = pl.BlockSpec(memory_space=pltpu.VMEM)
    hbm = pl.BlockSpec(memory_space=pl.ANY)

    def real(*shape):
        return jax.ShapeDtypeStruct(shape, F32)

    outs = pl.pallas_call(
        make_kernel(dims),
        name="train_step",
        out_shape=(
            real(batches, feats * pieces * hops, LANES),
            jax.ShapeDtypeStruct((joined_width, width), BF16),
            jax.ShapeDtypeStruct((hops * LANES, width), BF16),
            real(2 * hops + 4, width),
        ),
        in_specs=[hbm] + [vmem] * 3 + [hbm] + [vmem] * 4 + [hbm] + [vmem] * 5,
        out_specs=(hbm, hbm, hbm, vmem),
        scratch_shapes=[
            pltpu.VMEM((HOT * pieces * hops, LANES), F32),
            pltpu.VMEM((batches, hops, nodes, width), F32),
            pltpu.VMEM((batches, nodes, joined_width), BF16),
            pltpu.VMEM((batches, hops, LANES, nodes), BF16),
            pltpu.VMEM((batches, hops, nodes, LANES), BF16),
            pltpu.VMEM((batches, nodes, width), F32),
            pltpu.VMEM((batches, nodes, width), F32),
            pltpu.VMEM((batches, nodes, width), BF16),
            pltpu.VMEM((hops, LANES, width), F32),
            pltpu.VMEM((padded, width), F32),
            pltpu.VMEM((hops, LANES, width), BF16),
            pltpu.VMEM((joined_width, width), BF16),
            pltpu.VMEM((padded, width), BF16),
            pltpu.VMEM((padded, LANES), F32),
            pltpu.VMEM((tables, width), F32),
            pltpu.VMEM((tables, width), F32),
        ]
        + [pltpu.VMEM((batches, tables, width), F32) for _ in range(2)]
        + [pltpu.VMEM((tables, width), F32) for _ in range(2)]
        + [pltpu.VMEM((2 * hops, width), F32)]
        + [pltpu.VMEM((batches, table_rows, LANES), F32)]
        + [pltpu.VMEM((batches, nears, share, LANES), F32), pltpu.VMEM((batches, fars, share, LANES), F32)]
        + [pltpu.VMEM((batches, table_rows, LANES), F32)]
        + small_scratch(8)
        + small_scratch(16)
        + small_scratch(tables, 1)
        + [
            pltpu.VMEM((joined_width, width), BF16),
            pltpu.VMEM((joined_width, width), BF16),
            pltpu.VMEM((rows_rest, width), BF16),
            pltpu.VMEM((rows_rest, width), BF16),
            [pltpu.VMEM(s, BF16) for s in mid_shapes],
            [pltpu.VMEM(s, BF16) for s in rest_shapes],
            [near, near, far, far, near, near],
            [near, near, far, far],
            [near, near, far, far],
            [near, near, far, far],
            [near, near, far, far, near, near],
            [sem((mid_sems,)) for _ in range(4)],
            [sem((rest_sems,)) for _ in range(4)],
            sem((max(batches, hops),)),
            sem((batches,)),
            sem((3,)),
        ],
        compiler_params=pltpu.CompilerParams(
            collective_id=0, has_side_effects=True, vmem_limit_bytes=int(63.9 * 2**20)
        ),
    )(
        by_piece(jnp.transpose(features, (0, 3, 2, 1))),
        jnp.transpose(buckets, (0, 2, 1)),
        jnp.transpose(hop_mask, (2, 0, 1)),
        labels,
        by_piece(jnp.transpose(w_hops, (1, 0, 2))),
        gain_hops,
        shift_hops,
        slope_hops,
        slope_cat[None],
        w_mid,
        gain_mid[None],
        shift_mid[None],
        slope_mid[None],
        w_out.T,
        bias_out[None],
    )
    outs = pl.pallas_call(
        make_finish(dims),
        name="finish",
        out_shape=(
            real(batches, feats * pieces * hops, LANES),
            real(joined_width, width),
            real(feats * pieces * hops, LANES),
            real(hops, width),
            real(hops, width),
            real(hops, width),
            real(1, joined_width),
            real(1, width),
            real(1, width),
            real(1, width),
            real(classes, width),
            real(1, classes),
            real(1, 1),
        ),
        in_specs=[hbm, hbm, vmem, vmem],
        out_specs=(hbm, hbm) + (vmem,) * 11,
        scratch_shapes=[
            pltpu.VMEM((hops, width, width), BF16),
            pltpu.VMEM((hops, width, width), F32),
            pltpu.VMEM((batches, feats * pieces * hops, LANES), F32),
            sem((4, max(batches, hops))),
        ],
        compiler_params=pltpu.CompilerParams(vmem_limit_bytes=int(63.9 * 2**20)),
    )(*outs)
    (features_grad, mid_grad, hops_grad, gain, shift, slope, cat, gain_m, shift_m, slope_m, out_grad, bias, loss) = outs
    return (
        loss[0, 0],
        jnp.transpose(by_hop(features_grad, hops, nodes // LANES), (0, 3, 2, 1)),
        jnp.transpose(by_hop(hops_grad, hops, pieces), (1, 0, 2)),
        gain,
        shift,
        slope,
        cat[0],
        mid_grad,
        gain_m[0],
        shift_m[0],
        slope_m[0],
        out_grad.T,
        bias[0],
    )


def solution(mesh):
    nodes_split = ("bucket", "dp")
    placed = (
        P(None, nodes_split, None, None),
        P(None, nodes_split, None),
        P(None, nodes_split, None),
        P(None, nodes_split),
    ) + (P(),) * 11
    return jax.shard_map(
        shards,
        mesh=mesh,
        in_specs=placed,
        out_specs=(P(), P(None, nodes_split, None, None)) + (P(),) * 11,
        check_vma=False,
    )
```

```python
import functools

import jax
import jax.numpy as jnp
from jax import lax
from jax.experimental import pallas as pl
from jax.experimental.pallas import tpu as pltpu
from jax.sharding import PartitionSpec as P

F32 = jnp.float32
BF16 = jnp.bfloat16
EPSILON = 1e-05
MESH = pl.DeviceIdType.MESH
LANES = 128
HOT = 112
SPARE = 104
MID_ORDERS = (("wide", "low", "high"), ("low", "wide", "high"))
REST_ORDERS = (("plane", "high"),)
NN, NT, TN = ((1,), (0,)), ((1,), (1,)), ((0,), (0,))


def dot(left, right, dims=NN):
    return lax.dot_general(left, right, (dims, ((), ())), preferred_element_type=F32)


def split_high(values):
    high = values.astype(BF16)
    return high, (values - high.astype(F32)).astype(BF16)


class Place:
    def __init__(self, groups, dps):
        self.groups, self.dps = groups, dps
        self.high = 4
        self.low = dps // self.high
        self.wide = groups // 2
        self.b = lax.axis_index("bucket")
        self.d = lax.axis_index("dp")
        self.core = lax.rem(self.b, 2)
        self.x = lax.div(self.b, 2)
        self.lo = lax.rem(self.d, self.low)
        self.hi = lax.div(self.d, self.low)
        self.fold, self.nears, self.fars = self.group_sizes(groups, dps)
        self.near = self.b * self.fold + lax.rem(self.d, self.fold)
        self.far = lax.div(self.d, self.fold)

    @staticmethod
    def group_sizes(groups, dps):
        low = dps // 4
        fold = low if groups * low <= 8 else 1
        return fold, groups * fold, dps // fold

    def at(self, b=None, d=None):
        return {"bucket": self.b if b is None else b, "dp": self.d if d is None else d}

    def near_peer(self, o):
        i = lax.rem(self.near + o, self.nears)
        b, lo = lax.div(i, self.fold), lax.rem(i, self.fold)
        return i, self.at(b=b, d=lax.div(self.d, self.fold) * self.fold + lo)

    def far_peer(self, o):
        i = lax.rem(self.far + o, self.fars)
        return i, self.at(d=i * self.fold + lax.rem(self.d, self.fold))

    def axis(self, name):
        if name == "core":
            return self.core, 2, lambda o: (1 - self.core, self.at(b=2 * self.x + 1 - self.core))
        if name == "wide":
            def peer(o):
                i = lax.rem(self.x + o, self.wide)
                return i, self.at(b=2 * i + self.core)
            return self.x, self.wide, peer
        if name == "low":
            def peer(o):
                i = lax.rem(self.lo + o, self.low)
                return i, self.at(d=self.hi * self.low + i)
            return self.lo, self.low, peer

        if name == "plane":
            own = self.x * self.low + self.lo

            def peer(o):
                i = lax.rem(own + o, self.wide * self.low)
                b = 2 * lax.div(i, self.low) + self.core
                return i, self.at(b=b, d=self.hi * self.low + lax.rem(i, self.low))
            return own, self.wide * self.low, peer

        def peer(o):
            i = lax.rem(self.hi + o, self.high)
            return i, self.at(d=i * self.low + self.lo)
        return self.hi, self.high, peer


def remote(src, dst, sems, index, device):
    send, recv = sems
    return pltpu.make_async_remote_copy(
        src_ref=src,
        dst_ref=dst,
        send_sem=send.at[index],
        recv_sem=recv.at[index],
        device_id=device,
        device_id_type=MESH,
    )


def wait_all(copied, sems, index, device):
    remote(copied, copied, sems, index, device).wait()


class SmallSum:
    def __init__(self, place, near, far, total, near_sems, far_sems):
        self.place, self.near, self.far, self.total = place, near, far, total
        self.near_sems, self.far_sems = near_sems, far_sems

    def own(self, m):
        return self.near.at[m, self.place.near]

    def near_copies(self, m):
        mine = self.near.at[m, self.place.near]
        return [
            remote(mine, mine, self.near_sems, m, self.place.near_peer(o)[1])
            for o in range(1, self.place.nears)
        ]

    def far_copies(self, m):
        mine = self.far.at[m, self.place.far]
        return [
            remote(mine, mine, self.far_sems, m, self.place.far_peer(o)[1])
            for o in range(1, self.place.fars)
        ]

    def start(self, m):
        for copy in self.near_copies(m):
            copy.start()

    def forward(self, m):
        place = self.place
        wait_all(self.near.at[m, pl.ds(0, place.nears - 1)], self.near_sems, m, place.near_peer(1)[1])
        self.far[m, self.place.far] = sum(self.near[m, i] for i in range(self.place.nears))
        for copy in self.far_copies(m):
            copy.start()

    def finish(self, m):
        place = self.place
        wait_all(self.far.at[m, pl.ds(0, place.fars - 1)], self.far_sems, m, place.far_peer(1)[1])
        self.total[m] = sum(self.far[m, i] for i in range(self.place.fars))


class TableSum:
    def __init__(self, place, table, near, far, total, near_sems, far_sems, back_sems):
        self.place, self.table, self.near, self.far, self.total = place, table, near, far, total
        self.near_sems, self.far_sems, self.back_sems = near_sems, far_sems, back_sems
        self.rows = table.shape[1] // place.nears

    def share(self, i):
        return pl.ds(pl.multiple_of(i * self.rows, 8), self.rows)

    def near_copies(self, m):
        mine = self.near.at[m, self.place.near]
        copies = []
        for o in range(1, self.place.nears):
            i, device = self.place.near_peer(o)
            copies.append(remote(self.table.at[m, self.share(i)], mine, self.near_sems, m, device))
        return copies

    def far_copies(self, m):
        mine = self.far.at[m, self.place.far]
        return [
            remote(mine, mine, self.far_sems, m, self.place.far_peer(o)[1])
            for o in range(1, self.place.fars)
        ]

    def back_copies(self, m):
        mine = self.total.at[m, self.share(self.place.near)]
        return [
            remote(mine, mine, self.back_sems, m, self.place.near_peer(o)[1])
            for o in range(1, self.place.nears)
        ]

    def start(self, m):
        for copy in self.near_copies(m):
            copy.start()
        self.near[m, self.place.near] = self.table[m, self.share(self.place.near)]

    def forward(self, m):
        place = self.place
        wait_all(self.near.at[m, pl.ds(0, place.nears - 1)], self.near_sems, m, place.near_peer(1)[1])
        self.far[m, self.place.far] = sum(self.near[m, i] for i in range(self.place.nears))
        for copy in self.far_copies(m):
            copy.start()

    def back(self, m):
        place = self.place
        wait_all(self.far.at[m, pl.ds(0, place.fars - 1)], self.far_sems, m, place.far_peer(1)[1])
        self.total[m, self.share(self.place.near)] = sum(self.far[m, i] for i in range(self.place.fars))
        for copy in self.back_copies(m):
            copy.start()

    def finish(self, m):
        place = self.place
        rows = self.total.at[m, pl.ds(0, (place.nears - 1) * self.rows)]
        wait_all(rows, self.back_sems, m, place.near_peer(1)[1])


class GradSum:
    def __init__(self, place, part, total, stages, sems, orders):
        self.part, self.total, self.stages, self.sems = part, total, stages, sems
        half = part.shape[0] // 2
        core = place.axis("core")
        self.steps = [[(core, 0, half, 0)]] + [[] for _ in orders[0]]
        slot = 1
        for h, order in enumerate(orders):
            size = half // len(orders)
            start = core[0] * half + h * size
            for i, name in enumerate(order):
                axis = place.axis(name)
                self.shared = i == len(order) - 1 and size % (16 * axis[1]) != 0
                if not self.shared:
                    size = size // axis[1]
                self.steps[i + 1].append((axis, start, size, slot))
                start = start + axis[0] * size
                slot += 1

    @staticmethod
    def stage_shapes(rows, columns, orders, sizes):
        shapes = [(1, rows // 2, columns)]
        for order in orders:
            size = rows // 2 // len(orders)
            for i, name in enumerate(order):
                n = sizes[name]
                if i == len(order) - 1 and size % (16 * n):
                    shapes.append((n, size, columns))
                else:
                    size //= n
                    shapes.append((n - 1, size, columns))
            assert size % 16 == 0
        return shapes

    def rows(self, base, size, index):
        return pl.ds(pl.multiple_of(base + index * size, 16), size)

    def whole(self, step):
        return self.shared and step == len(self.steps) - 1

    def down(self, step):
        copies = []
        for (own, n, peer), base, size, slot in self.steps[step]:
            for o in range(1, n):
                i, device = peer(o)
                if self.whole(step):
                    src, dst = self.part.at[self.rows(base, size, 0)], self.stages[slot].at[own]
                else:
                    src, dst = self.part.at[self.rows(base, size, i)], self.stages[slot].at[o - 1]
                copies.append(remote(src, dst, self.sems[:2], slot, device))
        return copies

    def up(self, step):
        copies = []
        for (own, n, peer), base, size, slot in [] if self.whole(step) else self.steps[step]:
            mine = self.total.at[self.rows(base, size, own)]
            for o in range(1, n):
                copies.append(remote(mine, mine, self.sems[2:], slot, peer(o)[1]))
        return copies

    def start_down(self, step):
        for copy in self.down(step):
            copy.start()

    def end_down(self, step):
        last = step == len(self.steps) - 1
        for (own, n, peer), base, size, slot in self.steps[step]:
            wait_all(self.stages[slot].at[pl.ds(0, n - 1)], self.sems[:2], slot, peer(1)[1])
            piece = min(size, 64)
            if self.whole(step):
                rows = self.rows(base, size, 0)
                self.stages[slot][own] = self.part[rows]
                self.total[rows] = sum(self.stages[slot][i].astype(F32) for i in range(n)).astype(BF16)
                continue

            def add(i, carry):
                rows = pl.ds(pl.multiple_of(base + own * size + i * piece, 16), piece)
                there = pl.ds(pl.multiple_of(i * piece, 16), piece)
                total = self.part[rows].astype(F32)
                for o in range(1, n):
                    total = total + self.stages[slot][o - 1, there].astype(F32)
                (self.total if last else self.part)[rows] = total.astype(BF16)
                return carry

            lax.fori_loop(0, size // piece, add, 0)

    def start_up(self, step):
        for copy in self.up(step):
            copy.start()

    def end_up(self, step):
        for (own, n, peer), base, size, slot in [] if self.whole(step) else self.steps[step]:
            rows = self.total.at[pl.ds(pl.multiple_of(base, 16), (n - 1) * size)]
            wait_all(rows, self.sems[2:], slot, peer(1)[1])

    def advance(self, stage):
        last = len(self.steps) - 1
        if stage <= last:
            self.end_down(stage)
            if stage < last:
                self.start_down(stage + 1)
            else:
                self.start_up(last)
        else:
            step = 2 * last + 1 - stage
            self.end_up(step)
            if step:
                self.start_up(step - 1)


def make_kernel(dims):
    (groups, dps, batches, nodes, hops, feats, width, classes) = dims
    pieces = width // LANES
    tables = hops * groups
    nodes_batch = nodes * groups * dps
    total_nodes = batches * nodes_batch
    chunk = 32
    final = batches - 1
    lane = [slice(j * LANES, (j + 1) * LANES) for j in range(pieces)]
    columns = [slice(k * width, (k + 1) * width) for k in range(hops)]

    def kernel(
        x_in, bucket_ref, mask_ref, labels_ref, w_in, gain_ref, shift_ref, slope_ref, slope_cat_ref, w_mid_in,
        gain_mid_ref, shift_mid_ref, slope_mid_ref, w_out_in, bias_in,
        out_features, out_mid, out_rest, out_small,
        spread, u_ref, join_ref, xt_ref, cat_ref, present_ref, mid_ref, dshaped_ref, dmid_ref, grad_hops_ref, grad_out_ref,
        w_ref, w_mid_ref, w_out_ref, bias_ref, gain_rep, shift_rep, tab_a, tab_b, tab_e, tab_f, slopes_ref,
        table, table_near, table_far, t_total, s_near, s_far, s_total, e_near, e_far, e_total, c_near, c_far, c_total,
        part_mid, total_mid, part_rest, total_rest, stages_mid, stages_rest,
        t_sems, s_sems, e_sems, c_sems, d_sems, mid_sems, rest_sems, in_sems, out_sems, file_sems,
    ):
        spread_rows = feats * pieces * hops
        place = Place(groups, dps)
        barrier = pltpu.get_barrier_semaphore()
        for o in range(1, place.nears):
            pl.semaphore_signal(barrier, inc=1, device_id=place.near_peer(o)[1], device_id_type=MESH)
        for o in range(1, place.fars):
            pl.semaphore_signal(barrier, inc=1, device_id=place.far_peer(o)[1], device_id_type=MESH)

        def landing(ref, m):
            return ref.at[pl.ds(0, spread_rows), pl.ds(pl.multiple_of(m * LANES, LANES), LANES)]

        def x_copy(m):
            return pltpu.make_async_copy(x_in.at[m], landing(part_mid, m), in_sems.at[m])

        w_copy = pltpu.make_async_copy(w_in, landing(total_mid, 0), file_sems.at[1])
        w_mid_copy = pltpu.make_async_copy(w_mid_in, w_mid_ref, file_sems.at[2])
        w_copy.start()
        for m in range(batches):
            x_copy(m).start()
        w_mid_copy.start()

        stats = TableSum(place, table, table_near, table_far, t_total, t_sems[0:2], t_sems[2:4], t_sems[4:6])
        heads = SmallSum(place, s_near, s_far, s_total, s_sems[0:2], s_sems[2:4])
        backs = SmallSum(place, e_near, e_far, e_total, e_sems[0:2], e_sems[2:4])
        dots = TableSum(place, table, table_near, table_far, t_total, d_sems[0:2], d_sems[2:4], d_sems[4:6])
        amounts = SmallSum(place, c_near, c_far, c_total, c_sems[0:2], c_sems[2:4])
        mids = GradSum(place, part_mid, total_mid, stages_mid, mid_sems, MID_ORDERS)
        rests = GradSum(place, part_rest, total_rest, stages_rest, rest_sems, REST_ORDERS)

        def loop(first, last, body):
            def step(m, carry):
                body(m)
                return carry

            lax.fori_loop(first, last, step, 0)

        def at(m, when, body):
            pl.when(m == when)(body)

        spread[spread_rows:] = jnp.zeros((spread.shape[0] - spread_rows, LANES), F32)

        def hop_rows(k):
            parts = [spread[pl.ds(j * hops + k, HOT, stride=pieces * hops)] for j in range(pieces)]
            return jnp.concatenate(parts, axis=1)

        w_copy.wait()
        spread[:spread_rows] = landing(total_mid, 0)[...].astype(F32)
        for k in range(hops):
            w_ref[k] = jnp.concatenate([hop_rows(k), jnp.zeros((LANES - HOT, width), F32)], axis=0).astype(BF16)
            for g in range(groups):
                gain_rep[k * groups + g : k * groups + g + 1] = gain_ref[k : k + 1]
                shift_rep[k * groups + g : k * groups + g + 1] = shift_ref[k : k + 1]
        w_out_ref[...] = jnp.zeros_like(w_out_ref)
        w_out_ref[:classes] = w_out_in[...]
        bias_ref[...] = jnp.full(bias_ref.shape, -1e30, F32)
        bias_ref[0:1, :classes] = bias_in[...]
        bias_row = jnp.broadcast_to(bias_ref[0:1], (LANES, LANES))
        bias_ref[...] = jnp.transpose(bias_row)[: bias_ref.shape[0]]
        grad_hops_ref[...] = jnp.zeros_like(grad_hops_ref)
        grad_out_ref[...] = jnp.zeros_like(grad_out_ref)
        slopes_ref[...] = jnp.zeros_like(slopes_ref)

        def hot_rows(m):
            ids = lax.broadcasted_iota(jnp.int32, (LANES - HOT, nodes), 0)
            return (ids == bucket_ref[m]).astype(F32)

        def active_row(m, k):
            if k == 0:
                return jnp.ones((1, nodes), F32)
            return mask_ref[k - 1, pl.ds(m, 1)].astype(F32)

        which = lax.broadcasted_iota(jnp.int32, (groups, LANES), 1)
        amount = [jnp.zeros((groups, LANES), F32) for _ in range(hops)]
        for m in range(batches):
            hot = hot_rows(m)
            for k in range(hops):
                here = jnp.sum(hot * active_row(m, k), axis=1, keepdims=True)
                amount[k] = jnp.where(which == m, here[:groups], amount[k])
        for k in range(hops):
            c_near[0, place.near, k * groups : (k + 1) * groups] = amount[k]

        def by_node(row):
            return jnp.transpose(jnp.broadcast_to(row, (LANES, nodes)))

        def moments(m):
            x_copy(m).wait()
            spread[:spread_rows] = landing(part_mid, m)[...].astype(F32)
            hot_all = hot_rows(m)
            cat_ref[m] = by_node(bucket_ref[m].astype(F32)).astype(BF16)
            for k in range(hops):
                block = jnp.concatenate([hop_rows(k), hot_all], axis=0) * active_row(m, k)
                xt = block.astype(BF16)
                hot = xt[HOT:]
                xt_ref[m, k] = xt
                pre = dot(xt, w_ref[k], TN)
                u_ref[m, k] = pre
                square = (pre * pre).astype(BF16)
                second = dot(hot, square)
                sums = jnp.concatenate(split_high(dot(hot, xt, NT)), axis=1)
                first = dot(sums, jnp.concatenate([w_ref[k], w_ref[k]], axis=0))
                for j in range(pieces):
                    base = 2 * tables * j + k * groups
                    table[m, base : base + groups] = first[:groups, lane[j]]
                    table[m, base + tables : base + tables + groups] = second[:groups, lane[j]]

        def moments_step(m):
            moments(m)

            @pl.when(m == 0)
            def _():
                pl.semaphore_wait(barrier, place.nears + place.fars - 2)
                amounts.start(0)

            stats.start(m)
            at(m, 2, lambda: amounts.forward(0))
            pl.when(m >= 2)(lambda: stats.forward(m - 2))

        loop(0, batches, moments_step)
        stats.forward(final - 1)
        stats.back(0)
        stats.forward(final)
        stats.back(1)
        amounts.finish(0)
        w_mid_copy.wait()
        stats.finish(0)
        stats.back(final - 1)

        def counts_of(m):
            here = lax.broadcasted_iota(jnp.int32, (tables, LANES), 1) == m
            counts = jnp.sum(jnp.where(here, c_total[0], 0.0), axis=1, keepdims=True)
            return jnp.broadcast_to(counts, (tables, LANES))

        def bucket_tables(m):
            counts = counts_of(m)
            for j in range(pieces):
                base = 2 * tables * j
                mean = t_total[m, base : base + tables] / counts
                second = t_total[m, base + tables : base + 2 * tables] / counts
                inv = lax.rsqrt(second - mean * mean + EPSILON)
                a = 0.5 * gain_rep[:, lane[j]] * inv
                tab_a[m, :, lane[j]] = a
                tab_b[m, :, lane[j]] = 0.5 * shift_rep[:, lane[j]] - a * mean

        def choose(masks, values, k, j):
            result = values[k * groups + groups - 1 : k * groups + groups, lane[j]]
            for g in range(groups - 2, -1, -1):
                result = jnp.where(masks[g], values[k * groups + g : k * groups + g + 1, lane[j]], result)
            return result

        def masks_of(m, rows):
            cat = cat_ref[m, rows].astype(F32)
            return [cat == float(g) for g in range(groups - 1)]

        chunks = [slice(i * chunk, (i + 1) * chunk) for i in range(nodes // chunk)]

        def forward(m):
            bucket_tables(m)

            def product(k):
                middle = dot(join_ref[m, :, columns[k]], w_mid_ref[columns[k]])
                mid_ref[m] = middle if k == 0 else mid_ref[m] + middle

            for k in range(hops):
                if k:
                    product(k - 1)
                    present = present_ref.at[k % 2]
                    present[...] = by_node(active_row(m, k))
                for rows in chunks:
                    masks = masks_of(m, rows)
                    for j in range(pieces):
                        bend = 0.5 - 0.5 * slope_ref[k : k + 1, lane[j]]
                        bend_cat = 0.5 - 0.5 * slope_cat_ref[:, k * width + j * LANES : k * width + (j + 1) * LANES]
                        scale = choose(masks, tab_a.at[m], k, j)
                        offset = choose(masks, tab_b.at[m], k, j)
                        if k:
                            offset = offset * present[rows]
                        u = u_ref[m, k, rows, lane[j]] * scale + offset
                        u_ref[m, k, rows, lane[j]] = u
                        half = u - (bend * u) * (1.0 - jnp.tanh(u))
                        half = half - (bend_cat * half) * (1.0 - jnp.tanh(half))
                        join_ref[m, rows, k * width + j * LANES : k * width + (j + 1) * LANES] = half.astype(BF16)
            product(hops - 1)
            middle = mid_ref[m]
            first = jnp.sum(middle, axis=0, keepdims=True)
            second = jnp.sum(middle * middle, axis=0, keepdims=True)
            own = heads.own(m)
            for j in range(pieces):
                own[j : j + 1] = first[:, lane[j]]
                own[pieces + j : pieces + j + 1] = second[:, lane[j]]

        def row_of(ref, m, first):
            return jnp.concatenate([ref[m, first + j : first + j + 1] for j in range(pieces)], axis=1)

        def head_scale(m):
            mean = row_of(s_total, m, 0) * (1.0 / nodes_batch)
            second = row_of(s_total, m, pieces) * (1.0 / nodes_batch)
            inv = lax.rsqrt(4.0 * (second - mean * mean) + EPSILON)
            return mean, inv

        def head(m):
            heads.finish(m)
            mean, inv = head_scale(m)
            scale = gain_mid_ref[...] * inv
            offset = 0.5 * shift_mid_ref[...] - scale * mean
            slope = slope_mid_ref[...]
            u = mid_ref[m] * scale + offset
            mid_ref[m] = u
            tanh = jnp.tanh(u)
            gap = u * (1.0 - tanh)
            outer = (2.0 * u - (1.0 - slope) * gap).astype(BF16)
            logits = dot(w_out_ref[...], outer, NT) + bias_ref[:, 0:1]
            top = jnp.max(logits, axis=0, keepdims=True)
            powers = jnp.exp(logits - top)
            total = jnp.sum(powers, axis=0, keepdims=True)
            wanted = (lax.broadcasted_iota(jnp.int32, logits.shape, 0) == labels_ref[pl.ds(m, 1)]).astype(F32)
            loss = jnp.log(total) + top - jnp.sum(logits * wanted, axis=0, keepdims=True)
            dlogits = (powers / total - wanted) * (1.0 / total_nodes)
            low = dlogits.astype(BF16)
            grad_out_ref[...] += dot(low, outer)
            douter = dot(low, w_out_ref[...], TN)
            grad_slope = jnp.sum(douter * gap, axis=0, keepdims=True)
            dshaped = douter * (slope + (0.5 - 0.5 * slope) * (1.0 + tanh) * (1.0 + gap))
            dshaped_ref[m] = dshaped
            head_sum = jnp.sum(dshaped, axis=0, keepdims=True)
            head_dot = jnp.sum(dshaped * u, axis=0, keepdims=True)
            own = backs.own(m)
            for j in range(pieces):
                own[j : j + 1] = head_sum[:, lane[j]]
                own[pieces + j : pieces + j + 1] = head_dot[:, lane[j]]
                own[2 * pieces + j : 2 * pieces + j + 1] = grad_slope[:, lane[j]]
            folded = sum(dlogits[:, i * LANES : (i + 1) * LANES] for i in range(nodes // LANES))
            square = jnp.concatenate([folded, jnp.zeros((LANES - folded.shape[0], LANES), F32)], axis=0)
            own[3 * pieces : 3 * pieces + 1] = jnp.sum(jnp.transpose(square), axis=0, keepdims=True)
            own[3 * pieces + 1 : 3 * pieces + 2] = sum(
                loss[:, i * LANES : (i + 1) * LANES] for i in range(nodes // LANES)
            )
            own[3 * pieces + 2 :] = jnp.zeros((own.shape[0] - 3 * pieces - 2, LANES), F32)
            backs.start(m)

        def head_grads(m):
            inv = head_scale(m)[1]
            head_sum = row_of(e_total, m, 0)
            head_dot = (2.0 * row_of(e_total, m, pieces) - shift_mid_ref[...] * head_sum) / gain_mid_ref[...]
            return inv, head_sum, head_dot

        def back_head(m):
            backs.finish(m)
            inv, head_sum, head_dot = head_grads(m)
            scale = gain_mid_ref[...] * inv
            tilt = 2.0 * inv * head_dot * (1.0 / nodes_batch)
            level = scale * head_sum * (1.0 / nodes_batch) - 0.5 * shift_mid_ref[...] * tilt
            dmid_ref[m] = (scale * dshaped_ref[m] - level - mid_ref[m] * tilt).astype(BF16)

        gradients = [mid_ref.at[0], dshaped_ref.at[0]]

        def products(k):
            return (part_rest, total_rest)[k % 2].at[pl.ds(0, nodes)]

        def backward(m, which_hops, target, tick):
            def into(k):
                gradients[k % 2][...] = dot(dmid_ref[m], w_mid_ref[columns[k]], NT)

            def bucket_sums(k):
                hot = xt_ref[m, k, HOT:LANES]
                first = dot(hot, target(k)[...])
                second = dot(hot, products(k)[...])
                for j in range(pieces):
                    base = 2 * tables * j + k * groups
                    table[m, base : base + groups] = first[:groups, lane[j]]
                    table[m, base + tables : base + tables + groups] = second[:groups, lane[j]]

            into(which_hops[0])
            for k in which_hops:
                if k + 1 in which_hops:
                    into(k + 1)
                if k - 1 in which_hops:
                    bucket_sums(k - 1)
                slope_sums = [jnp.zeros((8, LANES), F32) for _ in range(2 * pieces)]
                result = target(k)
                for rows in chunks:
                    masks = masks_of(m, rows)
                    for j in range(pieces):
                        slope = slope_ref[k : k + 1, lane[j]]
                        slope_cat = slope_cat_ref[:, k * width + j * LANES : k * width + (j + 1) * LANES]
                        bend, bend_cat = 0.5 - 0.5 * slope, 0.5 - 0.5 * slope_cat
                        u = u_ref[m, k, rows, lane[j]]
                        tanh = jnp.tanh(u)
                        gap = (bend * u) * (1.0 - tanh)
                        half = u - gap
                        tanh_cat = jnp.tanh(half)
                        gap_cat = (bend_cat * half) * (1.0 - tanh_cat)
                        grad = gradients[k % 2][rows, lane[j]]
                        slope_sums[pieces + j] += jnp.sum((grad * gap_cat).reshape(-1, 8, LANES), axis=0)
                        grad = grad * (slope_cat + (1.0 + tanh_cat) * (bend_cat + gap_cat))
                        slope_sums[j] += jnp.sum((grad * gap).reshape(-1, 8, LANES), axis=0)
                        grad = grad * (slope + (1.0 + tanh) * (bend + gap))
                        grad = grad * choose(masks, tab_a.at[m], k, j)
                        result[rows, lane[j]] = grad.astype(BF16)
                        products(k)[rows, lane[j]] = (grad * u).astype(BF16)
                for j in range(pieces):
                    slope = slope_ref[k : k + 1, lane[j]]
                    slope_cat = slope_cat_ref[:, k * width + j * LANES : k * width + (j + 1) * LANES]
                    for s, values in enumerate((slope, slope_cat)):
                        grad_hops_ref[k, feats + s : feats + s + 1, lane[j]] += jnp.sum(
                            slope_sums[s * pieces + j], axis=0, keepdims=True
                        ) / (0.5 - 0.5 * values)
                if k == which_hops[-1]:
                    bucket_sums(k)
                tick(k)

        def first_target(k):
            return total_mid.at[pl.ds(k * nodes, nodes)]

        def first_copy(k):
            return pltpu.make_async_copy(first_target(k), join_ref.at[0, :, pl.ds(k * width, width)], in_sems.at[k])

        def no_tick(k):
            pass

        def forward_step(m):
            pl.when(m >= 1)(lambda: stats.finish(m))
            forward(m)
            heads.start(m)
            pl.when(m >= 1)(lambda: heads.forward(m - 1))
            at(m, 0, lambda: stats.back(final))
            at(m, 2, lambda: head(0))

        loop(0, batches, forward_step)
        backs.forward(0)

        def head_step(m):
            head(m)

            @pl.when(m == 1)
            def _():
                heads.forward(final)

            @pl.when(m == 2)
            def _():
                backs.forward(1)
                back_head(0)
                backward(0, [0, 1], first_target, no_tick)

        loop(1, batches, head_step)
        backs.forward(2)

        def late_tick(k):
            if k == hops - 1:
                backs.forward(final)

        backward(0, list(range(2, hops)), first_target, late_tick)
        dots.start(0)
        for m in range(1, final):
            back_head(m)

        held = [mid_ref.at[m] for m in range(final)] + [dshaped_ref.at[0]]
        for k in range(hops):
            held[k][...] = sum(dot(join_ref[m, :, columns[k]], dmid_ref[m], TN) for m in range(final))
        back_head(final)
        for k in range(hops):
            total = held[k][...] + dot(join_ref[final, :, columns[k]], dmid_ref[final], TN)
            part_mid[columns[k]] = (2.0 * total).astype(BF16)
        mids.start_down(0)
        for k in range(hops):
            first_copy(k).start()
        dots.forward(0)

        def backward_step(m):
            def tick(k):
                if k == 1:
                    at(m, 1, lambda: mids.advance(0))
                    at(m, 3, lambda: dots.back(1))
                if k == 2:
                    at(m, 1, lambda: dots.back(0))
                    at(m, 2, lambda: dots.forward(1))
                    at(m, 2, lambda: mids.advance(1))
                    at(m, 3, lambda: dots.forward(2))
                    at(m, 3, lambda: mids.advance(2))

            backward(m, list(range(hops)), lambda k: join_ref.at[m, :, columns[k]], tick)
            dots.start(m)

        loop(1, batches, backward_step)
        for k in range(hops):
            first_copy(k).wait()

        def last_tables(m):
            counts = counts_of(m)
            for j in range(pieces):
                base = 2 * tables * j
                a = tab_a[m, :, lane[j]]
                inv = 2.0 * a / gain_rep[:, lane[j]]
                shift = shift_rep[:, lane[j]]
                scaled = t_total[m, base : base + tables]
                bucket_sum = scaled / a
                bucket_dot = (2.0 * t_total[m, base + tables : base + 2 * tables] / a - shift * bucket_sum) / gain_rep[
                    :, lane[j]
                ]
                tilt = inv * bucket_dot / counts
                tab_f[:, lane[j]] = tilt
                tab_e[:, lane[j]] = scaled / counts - 0.5 * shift * tilt
                for k in range(hops):
                    here = slice(k * groups, (k + 1) * groups)
                    slopes_ref[k : k + 1, lane[j]] += jnp.sum(bucket_dot[here], axis=0, keepdims=True)
                    slopes_ref[hops + k : hops + k + 1, lane[j]] += jnp.sum(bucket_sum[here], axis=0, keepdims=True)

        def last(m):
            dots.finish(m)
            last_tables(m)

            def weights(k):
                grad_hops_ref[k, :HOT] += dot(xt_ref[m, k, :HOT], join_ref[m, :, columns[k]]) * 2.0

            for k in range(hops):
                if k:
                    weights(k - 1)
                for rows in chunks:
                    masks = masks_of(m, rows)
                    for j in range(pieces):
                        here = slice(k * width + j * LANES, k * width + (j + 1) * LANES)
                        grad = join_ref[m, rows, here].astype(F32) - choose(masks, tab_e, k, j)
                        grad = grad - choose(masks, tab_f, k, j) * u_ref[m, k, rows, lane[j]]
                        join_ref[m, rows, here] = grad.astype(BF16)
            weights(hops - 1)

        def features_copy(m):
            return pltpu.make_async_copy(spread.at[pl.ds(0, spread_rows)], out_features.at[m], out_sems.at[m])

        def features(m):
            pl.when(m >= 1)(lambda: features_copy(m - 1).wait())
            for k in range(hops):
                scale = active_row(m, k) * float(2 * total_nodes)
                values = dot(w_ref[k], join_ref[m, :, columns[k]], NT) * scale
                for j in range(pieces):
                    spread[pl.ds(j * hops + k, feats, stride=pieces * hops)] = values[:feats, lane[j]]
            features_copy(m).start()

        def start_rests():
            rows = grad_out_ref.shape[0] // hops
            for k in range(hops):
                grad_hops_ref[k, SPARE : SPARE + rows] = grad_out_ref[k * rows : (k + 1) * rows]
                part_rest[k * LANES : (k + 1) * LANES] = grad_hops_ref[k].astype(BF16)
            if part_rest.shape[0] > hops * LANES:
                part_rest[hops * LANES :] = jnp.zeros((part_rest.shape[0] - hops * LANES, width), BF16)
            rests.start_down(0)

        def last_step(m):
            last(m)
            at(m, 0, lambda: dots.back(2))
            at(m, 2, lambda: mids.advance(3))
            at(m, 3, start_rests)
            features(m)
            at(m, 0, lambda: dots.forward(final))
            at(m, 1, lambda: dots.back(final))

        loop(0, batches, last_step)
        rests.advance(0)
        mids.advance(4)

        grad_gain = jnp.zeros((1, width), F32)
        grad_shift = jnp.zeros((1, width), F32)
        grad_slope = jnp.zeros((1, width), F32)
        bias_loss = jnp.zeros((2, LANES), F32)
        for m in range(batches):
            _, head_sum, head_dot = head_grads(m)
            grad_gain = grad_gain + head_dot
            grad_shift = grad_shift + head_sum
            grad_slope = grad_slope + row_of(e_total, m, 2 * pieces)
            bias_loss = bias_loss + e_total[m, 3 * pieces : 3 * pieces + 2]
        out_small[: 2 * hops] = slopes_ref[...]
        loss = jnp.sum(bias_loss[1:2], axis=1, keepdims=True) * (1.0 / total_nodes)
        last_row = [bias_loss[0:1], jnp.broadcast_to(loss, (1, LANES)), jnp.zeros((1, width - 2 * LANES), F32)]
        for i, row in enumerate((grad_gain, grad_shift, grad_slope, jnp.concatenate(last_row, axis=1))):
            out_small[2 * hops + i : 2 * hops + i + 1] = row

        rests.advance(1)
        mids.advance(5)
        rests.advance(2)
        rests.advance(3)
        mids.advance(6)
        rests.advance(4)
        mids.advance(7)
        mid_file = pltpu.make_async_copy(total_mid, out_mid, file_sems.at[0])
        mid_file.start()
        rests.advance(5)
        rest_file = pltpu.make_async_copy(total_rest.at[pl.ds(0, hops * LANES)], out_rest, file_sems.at[1])
        rest_file.start()
        features_copy(final).wait()
        mid_file.wait()
        rest_file.wait()

    return kernel


def make_finish(dims):
    (groups, dps, batches, nodes, hops, feats, width, classes) = dims
    pieces = width // LANES
    spare = -(-classes // 16) * 16 // hops

    def kernel(
        features_in, mid_in, rest_in, small_in,
        features, mid, hops_grad, gain, shift, slope, cat, gain_mid, shift_mid, slope_mid, out_grad, bias, loss,
        low, wide, held, sems,
    ):
        in_copy = [pltpu.make_async_copy(features_in.at[m], held.at[m], sems.at[0, m]) for m in range(batches)]
        out_copy = [pltpu.make_async_copy(held.at[m], features.at[m], sems.at[3, m]) for m in range(batches)]
        low_copy = [pltpu.make_async_copy(mid_in.at[pl.ds(k * width, width)], low.at[k], sems.at[1, k]) for k in range(hops)]
        wide_copy = [pltpu.make_async_copy(wide.at[k], mid.at[pl.ds(k * width, width)], sems.at[2, k]) for k in range(hops)]
        for copy in low_copy + in_copy:
            copy.start()
        for k in range(hops):
            values = rest_in[k * LANES : (k + 1) * LANES].astype(F32)
            for j in range(pieces):
                hops_grad[pl.ds(j * hops + k, feats, stride=pieces * hops)] = values[
                    :feats, j * LANES : (j + 1) * LANES
                ]
            slope[k : k + 1] = values[feats : feats + 1]
            cat[:, k * width : (k + 1) * width] = values[feats + 1 : feats + 2]
            count = min(spare, classes - k * spare)
            out_grad[k * spare : k * spare + count] = values[SPARE : SPARE + count]
        gain[...] = small_in[:hops]
        shift[...] = small_in[hops : 2 * hops]
        gain_mid[...] = small_in[2 * hops : 2 * hops + 1]
        shift_mid[...] = small_in[2 * hops + 1 : 2 * hops + 2]
        slope_mid[...] = small_in[2 * hops + 2 : 2 * hops + 3]
        bias[...] = small_in[2 * hops + 3 : 2 * hops + 4, :classes]
        loss[...] = small_in[2 * hops + 3 : 2 * hops + 4, LANES : LANES + 1]
        for k in range(hops):
            low_copy[k].wait()
            wide[k] = low[k].astype(F32)
            wide_copy[k].start()
        for m in range(batches):
            in_copy[m].wait()
            out_copy[m].start()
        for copy in wide_copy + out_copy:
            copy.wait()

    return kernel


def by_piece(values):
    *lead, feats, hops, width = values.shape
    values = jnp.swapaxes(values.reshape(*lead, feats, hops, width // LANES, LANES), -3, -2)
    return values.reshape(*lead, feats * hops * width // LANES, LANES)


def by_hop(rows, hops, pieces):
    *lead, count, _ = rows.shape
    values = rows.reshape(*lead, count // (hops * pieces), pieces, hops, LANES)
    return jnp.swapaxes(values, -3, -2).reshape(*lead, count // (hops * pieces), hops, pieces * LANES)


def shards(
    features,
    buckets,
    hop_mask,
    labels,
    w_hops,
    gain_hops,
    shift_hops,
    slope_hops,
    slope_cat,
    w_mid,
    gain_mid,
    shift_mid,
    slope_mid,
    w_out,
    bias_out,
):
    batches, nodes, hops, feats = features.shape
    width, classes = w_out.shape
    groups, dps = lax.axis_size("bucket"), lax.axis_size("dp")
    dims = (groups, dps, batches, nodes, hops, feats, width, classes)
    pieces = width // LANES
    joined_width = hops * width
    tables = hops * groups
    padded = -(-classes // 16) * 16

    wide, low, high = groups // 2, dps // 4, 4
    sizes = {"wide": wide, "low": low, "high": high, "plane": wide * low}
    rows_rest = max(hops * LANES, 2 * wide * low * 16)
    mid_shapes = GradSum.stage_shapes(joined_width, width, MID_ORDERS, sizes)
    rest_shapes = GradSum.stage_shapes(rows_rest, width, REST_ORDERS, sizes)
    _, nears, fars = Place.group_sizes(groups, dps)
    table_rows = 2 * tables * pieces
    share = table_rows // nears
    sem = pltpu.SemaphoreType.DMA

    def small_scratch(rows, copies=batches):
        return [
            pltpu.VMEM((copies, nears, rows, LANES), F32),
            pltpu.VMEM((copies, fars, rows, LANES), F32),
            pltpu.VMEM((copies, rows, LANES), F32),
        ]

    vmem = pl.BlockSpec(memory_space=pltpu.VMEM)
    hbm = pl.BlockSpec(memory_space=pl.ANY)

    def real(*shape):
        return jax.ShapeDtypeStruct(shape, F32)

    outs = pl.pallas_call(
        make_kernel(dims),
        name="train_step",
        out_shape=(
            real(batches, feats * pieces * hops, LANES),
            jax.ShapeDtypeStruct((joined_width, width), BF16),
            jax.ShapeDtypeStruct((hops * LANES, width), BF16),
            real(2 * hops + 4, width),
        ),
        in_specs=[hbm] + [vmem] * 3 + [hbm] + [vmem] * 4 + [hbm] + [vmem] * 5,
        out_specs=(hbm, hbm, hbm, vmem),
        scratch_shapes=[
            pltpu.VMEM((HOT * pieces * hops, LANES), F32),
            pltpu.VMEM((batches, hops, nodes, width), F32),
            pltpu.VMEM((batches, nodes, joined_width), BF16),
            pltpu.VMEM((batches, hops, LANES, nodes), BF16),
            pltpu.VMEM((batches, nodes, LANES), BF16),
            pltpu.VMEM((2, nodes, LANES), F32),
            pltpu.VMEM((batches, nodes, width), F32),
            pltpu.VMEM((batches, nodes, width), F32),
            pltpu.VMEM((batches, nodes, width), BF16),
            pltpu.VMEM((hops, LANES, width), F32),
            pltpu.VMEM((padded, width), F32),
            pltpu.VMEM((hops, LANES, width), BF16),
            pltpu.VMEM((joined_width, width), BF16),
            pltpu.VMEM((padded, width), BF16),
            pltpu.VMEM((padded, LANES), F32),
            pltpu.VMEM((tables, width), F32),
            pltpu.VMEM((tables, width), F32),
        ]
        + [pltpu.VMEM((batches, tables, width), F32) for _ in range(2)]
        + [pltpu.VMEM((tables, width), F32) for _ in range(2)]
        + [pltpu.VMEM((2 * hops, width), F32)]
        + [pltpu.VMEM((batches, table_rows, LANES), F32)]
        + [pltpu.VMEM((batches, nears, share, LANES), F32), pltpu.VMEM((batches, fars, share, LANES), F32)]
        + [pltpu.VMEM((batches, table_rows, LANES), F32)]
        + small_scratch(8)
        + small_scratch(16)
        + small_scratch(tables, 1)
        + [
            pltpu.VMEM((joined_width, width), BF16),
            pltpu.VMEM((joined_width, width), BF16),
            pltpu.VMEM((rows_rest, width), BF16),
            pltpu.VMEM((rows_rest, width), BF16),
            [pltpu.VMEM(s, BF16) for s in mid_shapes],
            [pltpu.VMEM(s, BF16) for s in rest_shapes],
            [sem((batches,)) for _ in range(6)],
            [sem((batches,)) for _ in range(4)],
            [sem((batches,)) for _ in range(4)],
            [sem((1,)) for _ in range(4)],
            [sem((batches,)) for _ in range(6)],
            [sem((len(mid_shapes),)) for _ in range(4)],
            [sem((len(rest_shapes),)) for _ in range(4)],
            sem((max(batches, hops),)),
            sem((batches,)),
            sem((3,)),
        ],
        compiler_params=pltpu.CompilerParams(
            collective_id=0, has_side_effects=True, vmem_limit_bytes=int(63.9 * 2**20)
        ),
    )(
        by_piece(jnp.transpose(features, (0, 3, 2, 1))),
        jnp.transpose(buckets, (0, 2, 1)),
        jnp.transpose(hop_mask, (2, 0, 1)),
        labels,
        by_piece(jnp.transpose(w_hops, (1, 0, 2))),
        gain_hops,
        shift_hops,
        slope_hops,
        slope_cat[None],
        w_mid,
        gain_mid[None],
        shift_mid[None],
        slope_mid[None],
        w_out.T,
        bias_out[None],
    )
    outs = pl.pallas_call(
        make_finish(dims),
        name="finish",
        out_shape=(
            real(batches, feats * pieces * hops, LANES),
            real(joined_width, width),
            real(feats * pieces * hops, LANES),
            real(hops, width),
            real(hops, width),
            real(hops, width),
            real(1, joined_width),
            real(1, width),
            real(1, width),
            real(1, width),
            real(classes, width),
            real(1, classes),
            real(1, 1),
        ),
        in_specs=[hbm, hbm, vmem, vmem],
        out_specs=(hbm, hbm) + (vmem,) * 11,
        scratch_shapes=[
            pltpu.VMEM((hops, width, width), BF16),
            pltpu.VMEM((hops, width, width), F32),
            pltpu.VMEM((batches, feats * pieces * hops, LANES), F32),
            sem((4, max(batches, hops))),
        ],
        compiler_params=pltpu.CompilerParams(vmem_limit_bytes=int(63.9 * 2**20)),
    )(*outs)
    (features_grad, mid_grad, hops_grad, gain, shift, slope, cat, gain_m, shift_m, slope_m, out_grad, bias, loss) = outs
    return (
        loss[0, 0],
        jnp.transpose(by_hop(features_grad, hops, nodes // LANES), (0, 3, 2, 1)),
        jnp.transpose(by_hop(hops_grad, hops, pieces), (1, 0, 2)),
        gain,
        shift,
        slope,
        cat[0],
        mid_grad,
        gain_m[0],
        shift_m[0],
        slope_m[0],
        out_grad.T,
        bias[0],
    )


def solution(mesh):
    nodes_split = ("bucket", "dp")
    placed = (
        P(None, nodes_split, None, None),
        P(None, nodes_split, None),
        P(None, nodes_split, None),
        P(None, nodes_split),
    ) + (P(),) * 11
    return jax.shard_map(
        shards,
        mesh=mesh,
        in_specs=placed,
        out_specs=(P(), P(None, nodes_split, None, None)) + (P(),) * 11,
        check_vma=False,
    )
```

```python
import functools

import jax
import jax.numpy as jnp
from jax import lax
from jax.experimental import pallas as pl
from jax.experimental.pallas import tpu as pltpu
from jax.sharding import PartitionSpec as P

F32 = jnp.float32
BF16 = jnp.bfloat16
EPSILON = 1e-05
MESH = pl.DeviceIdType.MESH
LANES = 128
HOT = 112
SPARE = 104
MID_ORDERS = (("wide", "low", "high"), ("low", "wide", "high"))
REST_ORDERS = (("plane", "high"),)
NN, NT, TN = ((1,), (0,)), ((1,), (1,)), ((0,), (0,))


def dot(left, right, dims=NN):
    return lax.dot_general(left, right, (dims, ((), ())), preferred_element_type=F32)


def split_high(values):
    high = values.astype(BF16)
    return high, (values - high.astype(F32)).astype(BF16)


class Place:
    def __init__(self, groups, dps):
        self.groups, self.dps = groups, dps
        self.high = 4
        self.low = dps // self.high
        self.wide = groups // 2
        self.b = lax.axis_index("bucket")
        self.d = lax.axis_index("dp")
        self.core = lax.rem(self.b, 2)
        self.x = lax.div(self.b, 2)
        self.lo = lax.rem(self.d, self.low)
        self.hi = lax.div(self.d, self.low)
        self.fold, self.nears, self.fars = self.group_sizes(groups, dps)
        self.near = self.b * self.fold + lax.rem(self.d, self.fold)
        self.far = lax.div(self.d, self.fold)

    @staticmethod
    def group_sizes(groups, dps):
        low = dps // 4
        fold = low if groups * low <= 8 else 1
        return fold, groups * fold, dps // fold

    def at(self, b=None, d=None):
        return {"bucket": self.b if b is None else b, "dp": self.d if d is None else d}

    def near_peer(self, o):
        i = lax.rem(self.near + o, self.nears)
        b, lo = lax.div(i, self.fold), lax.rem(i, self.fold)
        return i, self.at(b=b, d=lax.div(self.d, self.fold) * self.fold + lo)

    def far_peer(self, o):
        i = lax.rem(self.far + o, self.fars)
        return i, self.at(d=i * self.fold + lax.rem(self.d, self.fold))

    def axis(self, name):
        if name == "core":
            return self.core, 2, lambda o: (1 - self.core, self.at(b=2 * self.x + 1 - self.core))
        if name == "wide":
            def peer(o):
                i = lax.rem(self.x + o, self.wide)
                return i, self.at(b=2 * i + self.core)
            return self.x, self.wide, peer
        if name == "low":
            def peer(o):
                i = lax.rem(self.lo + o, self.low)
                return i, self.at(d=self.hi * self.low + i)
            return self.lo, self.low, peer

        if name == "plane":
            own = self.x * self.low + self.lo

            def peer(o):
                i = lax.rem(own + o, self.wide * self.low)
                b = 2 * lax.div(i, self.low) + self.core
                return i, self.at(b=b, d=self.hi * self.low + lax.rem(i, self.low))
            return own, self.wide * self.low, peer

        def peer(o):
            i = lax.rem(self.hi + o, self.high)
            return i, self.at(d=i * self.low + self.lo)
        return self.hi, self.high, peer


def remote(src, dst, sems, index, device):
    send, recv = sems
    return pltpu.make_async_remote_copy(
        src_ref=src,
        dst_ref=dst,
        send_sem=send.at[index],
        recv_sem=recv.at[index],
        device_id=device,
        device_id_type=MESH,
    )


def wait_all(copied, sems, index, device):
    remote(copied, copied, sems, index, device).wait()


class SmallSum:
    def __init__(self, place, near, far, total, near_sems, far_sems):
        self.place, self.near, self.far, self.total = place, near, far, total
        self.near_sems, self.far_sems = near_sems, far_sems

    def own(self, m):
        return self.near.at[m, self.place.near]

    def near_copies(self, m):
        mine = self.near.at[m, self.place.near]
        return [
            remote(mine, mine, self.near_sems, m, self.place.near_peer(o)[1])
            for o in range(1, self.place.nears)
        ]

    def far_copies(self, m):
        mine = self.far.at[m, self.place.far]
        return [
            remote(mine, mine, self.far_sems, m, self.place.far_peer(o)[1])
            for o in range(1, self.place.fars)
        ]

    def start(self, m):
        for copy in self.near_copies(m):
            copy.start()

    def forward(self, m):
        place = self.place
        wait_all(self.near.at[m, pl.ds(0, place.nears - 1)], self.near_sems, m, place.near_peer(1)[1])
        self.far[m, self.place.far] = sum(self.near[m, i] for i in range(self.place.nears))
        for copy in self.far_copies(m):
            copy.start()

    def finish(self, m):
        place = self.place
        wait_all(self.far.at[m, pl.ds(0, place.fars - 1)], self.far_sems, m, place.far_peer(1)[1])
        self.total[m] = sum(self.far[m, i] for i in range(self.place.fars))


class TableSum:
    def __init__(self, place, table, near, far, total, near_sems, far_sems, back_sems):
        self.place, self.table, self.near, self.far, self.total = place, table, near, far, total
        self.near_sems, self.far_sems, self.back_sems = near_sems, far_sems, back_sems
        self.rows = table.shape[1] // place.nears

    def share(self, i):
        return pl.ds(pl.multiple_of(i * self.rows, 8), self.rows)

    def near_copies(self, m):
        mine = self.near.at[m, self.place.near]
        copies = []
        for o in range(1, self.place.nears):
            i, device = self.place.near_peer(o)
            copies.append(remote(self.table.at[m, self.share(i)], mine, self.near_sems, m, device))
        return copies

    def far_copies(self, m):
        mine = self.far.at[m, self.place.far]
        return [
            remote(mine, mine, self.far_sems, m, self.place.far_peer(o)[1])
            for o in range(1, self.place.fars)
        ]

    def back_copies(self, m):
        mine = self.total.at[m, self.share(self.place.near)]
        return [
            remote(mine, mine, self.back_sems, m, self.place.near_peer(o)[1])
            for o in range(1, self.place.nears)
        ]

    def start(self, m):
        for copy in self.near_copies(m):
            copy.start()
        self.near[m, self.place.near] = self.table[m, self.share(self.place.near)]

    def forward(self, m):
        place = self.place
        wait_all(self.near.at[m, pl.ds(0, place.nears - 1)], self.near_sems, m, place.near_peer(1)[1])
        self.far[m, self.place.far] = sum(self.near[m, i] for i in range(self.place.nears))
        for copy in self.far_copies(m):
            copy.start()

    def back(self, m):
        place = self.place
        wait_all(self.far.at[m, pl.ds(0, place.fars - 1)], self.far_sems, m, place.far_peer(1)[1])
        self.total[m, self.share(self.place.near)] = sum(self.far[m, i] for i in range(self.place.fars))
        for copy in self.back_copies(m):
            copy.start()

    def finish(self, m):
        place = self.place
        rows = self.total.at[m, pl.ds(0, (place.nears - 1) * self.rows)]
        wait_all(rows, self.back_sems, m, place.near_peer(1)[1])


class GradSum:
    def __init__(self, place, part, total, stages, sems, orders):
        self.part, self.total, self.stages, self.sems = part, total, stages, sems
        half = part.shape[0] // 2
        core = place.axis("core")
        self.steps = [[(core, 0, half, 0)]] + [[] for _ in orders[0]]
        slot = 1
        for h, order in enumerate(orders):
            size = half // len(orders)
            start = core[0] * half + h * size
            for i, name in enumerate(order):
                axis = place.axis(name)
                self.shared = i == len(order) - 1 and size % (16 * axis[1]) != 0
                if not self.shared:
                    size = size // axis[1]
                self.steps[i + 1].append((axis, start, size, slot))
                start = start + axis[0] * size
                slot += 1

    @staticmethod
    def stage_shapes(rows, columns, orders, sizes):
        shapes = [(1, rows // 2, columns)]
        for order in orders:
            size = rows // 2 // len(orders)
            for i, name in enumerate(order):
                n = sizes[name]
                if i == len(order) - 1 and size % (16 * n):
                    shapes.append((n, size, columns))
                else:
                    size //= n
                    shapes.append((n - 1, size, columns))
            assert size % 16 == 0
        return shapes

    def rows(self, base, size, index):
        return pl.ds(pl.multiple_of(base + index * size, 16), size)

    def whole(self, step):
        return self.shared and step == len(self.steps) - 1

    def down(self, step):
        copies = []
        for (own, n, peer), base, size, slot in self.steps[step]:
            for o in range(1, n):
                i, device = peer(o)
                if self.whole(step):
                    src, dst = self.part.at[self.rows(base, size, 0)], self.stages[slot].at[own]
                else:
                    src, dst = self.part.at[self.rows(base, size, i)], self.stages[slot].at[o - 1]
                copies.append(remote(src, dst, self.sems[:2], slot, device))
        return copies

    def up(self, step):
        copies = []
        for (own, n, peer), base, size, slot in [] if self.whole(step) else self.steps[step]:
            mine = self.total.at[self.rows(base, size, own)]
            for o in range(1, n):
                copies.append(remote(mine, mine, self.sems[2:], slot, peer(o)[1]))
        return copies

    def start_down(self, step):
        for copy in self.down(step):
            copy.start()

    def end_down(self, step, less=None):
        last = step == len(self.steps) - 1
        for (own, n, peer), base, size, slot in self.steps[step]:
            wait_all(self.stages[slot].at[pl.ds(0, n - 1)], self.sems[:2], slot, peer(1)[1])
            piece = min(size, 64)
            if self.whole(step):
                rows = self.rows(base, size, 0)
                self.stages[slot][own] = self.part[rows]
                self.total[rows] = sum(self.stages[slot][i].astype(F32) for i in range(n)).astype(BF16)
                continue

            def add(i, carry):
                rows = pl.ds(pl.multiple_of(base + own * size + i * piece, 16), piece)
                there = pl.ds(pl.multiple_of(i * piece, 16), piece)
                total = self.part[rows].astype(F32)
                for o in range(1, n):
                    total = total + self.stages[slot][o - 1, there].astype(F32)
                if less is not None:
                    total = total - less
                (self.total if last else self.part)[rows] = total.astype(BF16)
                return carry

            lax.fori_loop(0, size // piece, add, 0)

    def start_up(self, step):
        for copy in self.up(step):
            copy.start()

    def end_up(self, step):
        for (own, n, peer), base, size, slot in [] if self.whole(step) else self.steps[step]:
            rows = self.total.at[pl.ds(pl.multiple_of(base, 16), (n - 1) * size)]
            wait_all(rows, self.sems[2:], slot, peer(1)[1])

    def advance(self, stage, less=None):
        last = len(self.steps) - 1
        if stage <= last:
            self.end_down(stage, less if stage == last else None)
            if stage < last:
                self.start_down(stage + 1)
            else:
                self.start_up(last)
        else:
            step = 2 * last + 1 - stage
            self.end_up(step)
            if step:
                self.start_up(step - 1)


def plan(groups, dps, hops, width):
    wide, low, high = groups // 2, dps // 4, 4
    early = groups * LANES == width and 2 * wide * low * high * 16 == hops * LANES
    parts = 2 if hops % 2 == 0 and hops * width % (2 * 4 * wide * low * high * 16) == 0 else 1
    return early, parts


def make_kernel(dims):
    (groups, dps, batches, nodes, hops, feats, width, classes) = dims
    pieces = width // LANES
    tables = hops * groups
    nodes_batch = nodes * groups * dps
    total_nodes = batches * nodes_batch
    chunk = 32
    final = batches - 1
    early, mid_parts = plan(groups, dps, hops, width)
    bands = LANES // 16
    lane = [slice(j * LANES, (j + 1) * LANES) for j in range(pieces)]
    columns = [slice(k * width, (k + 1) * width) for k in range(hops)]

    def kernel(
        x_in, bucket_ref, mask_ref, labels_ref, w_in, gain_ref, shift_ref, slope_ref, slope_cat_ref, w_mid_in,
        gain_mid_ref, shift_mid_ref, slope_mid_ref, w_out_in, bias_in,
        out_features, out_mid, out_rest, out_small,
        spread, u_ref, join_ref, xt_ref, cat_ref, present_ref, mid_ref, dshaped_ref, dmid_ref, grad_hops_ref, grad_out_ref,
        w_ref, w_mid_ref, w_out_ref, bias_ref, gain_rep, shift_rep, tab_a, tab_b, tab_e, tab_f, slopes_ref,
        table, table_near, table_far, t_total, s_near, s_far, s_total, e_near, e_far, e_total, c_near, c_far, c_total,
        part_mid, total_mid, part_rest, total_rest, stages_mid, stages_rest, gram_own, scale_own, level_own, stages_gram,
        t_sems, s_sems, e_sems, c_sems, d_sems, mid_sems, rest_sems, gram_sems, in_sems, out_sems, file_sems,
    ):
        spread_rows = feats * pieces * hops
        place = Place(groups, dps)
        barrier = pltpu.get_barrier_semaphore()
        for o in range(1, place.nears):
            pl.semaphore_signal(barrier, inc=1, device_id=place.near_peer(o)[1], device_id_type=MESH)
        for o in range(1, place.fars):
            pl.semaphore_signal(barrier, inc=1, device_id=place.far_peer(o)[1], device_id_type=MESH)

        def landing(ref, m):
            return ref.at[pl.ds(0, spread_rows), pl.ds(pl.multiple_of(m * LANES, LANES), LANES)]

        def x_copy(m):
            return pltpu.make_async_copy(x_in.at[m], landing(part_mid, m), in_sems.at[m])

        w_copy = pltpu.make_async_copy(w_in, landing(total_mid, 0), file_sems.at[1])
        w_mid_copy = pltpu.make_async_copy(w_mid_in, w_mid_ref, file_sems.at[2])
        w_copy.start()
        for m in range(batches):
            x_copy(m).start()
        w_mid_copy.start()

        stats = TableSum(place, table, table_near, table_far, t_total, t_sems[0:2], t_sems[2:4], t_sems[4:6])
        heads = SmallSum(place, s_near, s_far, s_total, s_sems[0:2], s_sems[2:4])
        backs = SmallSum(place, e_near, e_far, e_total, e_sems[0:2], e_sems[2:4])
        dots = TableSum(place, table, table_near, table_far, t_total, d_sems[0:2], d_sems[2:4], d_sems[4:6])
        amounts = SmallSum(place, c_near, c_far, c_total, c_sems[0:2], c_sems[2:4])
        mid_rows = [pl.ds(i * hops * width // mid_parts, hops * width // mid_parts) for i in range(mid_parts)]
        mids = [
            GradSum(place, part_mid.at[rows], total_mid.at[rows], stages_mid[i], mid_sems[i], MID_ORDERS)
            for i, rows in enumerate(mid_rows)
        ]
        if early:
            gram_rows = [pl.ds(m * hops * LANES, hops * LANES) for m in range(batches)]
            grams = [
                GradSum(place, part_mid.at[rows], part_mid.at[rows], stages_gram[m], gram_sems[m], REST_ORDERS)
                for m, rows in enumerate(gram_rows)
            ]
            owned = (place.core * place.wide * place.low + place.axis("plane")[0]) * place.high + place.hi
            owned_hop = lax.div(owned, bands)

        def mid_step(i, stage):
            if i < mid_parts:
                mids[i].advance(stage)
        rests = GradSum(place, part_rest, total_rest, stages_rest, rest_sems, REST_ORDERS)

        def loop(first, last, body):
            def step(m, carry):
                body(m)
                return carry

            lax.fori_loop(first, last, step, 0)

        def at(m, when, body):
            pl.when(m == when)(body)

        spread[spread_rows:] = jnp.zeros((spread.shape[0] - spread_rows, LANES), F32)

        def hop_rows(k):
            parts = [spread[pl.ds(j * hops + k, HOT, stride=pieces * hops)] for j in range(pieces)]
            return jnp.concatenate(parts, axis=1)

        w_copy.wait()
        spread[:spread_rows] = landing(total_mid, 0)[...].astype(F32)
        for k in range(hops):
            w_ref[k] = jnp.concatenate([hop_rows(k), jnp.zeros((LANES - HOT, width), F32)], axis=0).astype(BF16)
            for g in range(groups):
                gain_rep[k * groups + g : k * groups + g + 1] = gain_ref[k : k + 1]
                shift_rep[k * groups + g : k * groups + g + 1] = shift_ref[k : k + 1]
        w_out_ref[...] = jnp.zeros_like(w_out_ref)
        w_out_ref[:classes] = w_out_in[...]
        bias_ref[...] = jnp.full(bias_ref.shape, -1e30, F32)
        bias_ref[0:1, :classes] = bias_in[...]
        bias_row = jnp.broadcast_to(bias_ref[0:1], (LANES, LANES))
        bias_ref[...] = jnp.transpose(bias_row)[: bias_ref.shape[0]]
        grad_hops_ref[...] = jnp.zeros_like(grad_hops_ref)
        grad_out_ref[...] = jnp.zeros_like(grad_out_ref)
        slopes_ref[...] = jnp.zeros_like(slopes_ref)

        def hot_rows(m):
            ids = lax.broadcasted_iota(jnp.int32, (LANES - HOT, nodes), 0)
            return (ids == bucket_ref[m]).astype(F32)

        def active_row(m, k):
            if k == 0:
                return jnp.ones((1, nodes), F32)
            return mask_ref[k - 1, pl.ds(m, 1)].astype(F32)

        which = lax.broadcasted_iota(jnp.int32, (groups, LANES), 1)
        amount = [jnp.zeros((groups, LANES), F32) for _ in range(hops)]
        for m in range(batches):
            hot = hot_rows(m)
            for k in range(hops):
                here = jnp.sum(hot * active_row(m, k), axis=1, keepdims=True)
                amount[k] = jnp.where(which == m, here[:groups], amount[k])
        for k in range(hops):
            c_near[0, place.near, k * groups : (k + 1) * groups] = amount[k]

        def by_node(row):
            return jnp.transpose(jnp.broadcast_to(row, (LANES, nodes)))

        def moments(m):
            x_copy(m).wait()
            spread[:spread_rows] = landing(part_mid, m)[...].astype(F32)
            hot_all = hot_rows(m)
            cat_ref[m] = by_node(bucket_ref[m].astype(F32)).astype(BF16)
            for k in range(hops):
                block = jnp.concatenate([hop_rows(k), hot_all], axis=0) * active_row(m, k)
                xt = block.astype(BF16)
                hot = xt[HOT:]
                xt_ref[m, k] = xt
                pre = dot(xt, w_ref[k], TN)
                u_ref[m, k] = pre
                square = (pre * pre).astype(BF16)
                second = dot(hot, square)
                sums = jnp.concatenate(split_high(dot(hot, xt, NT)), axis=1)
                first = dot(sums, jnp.concatenate([w_ref[k], w_ref[k]], axis=0))
                for j in range(pieces):
                    base = 2 * tables * j + k * groups
                    table[m, base : base + groups] = first[:groups, lane[j]]
                    table[m, base + tables : base + tables + groups] = second[:groups, lane[j]]

        def moments_step(m):
            moments(m)

            @pl.when(m == 0)
            def _():
                pl.semaphore_wait(barrier, place.nears + place.fars - 2)
                amounts.start(0)

            stats.start(m)
            at(m, 2, lambda: amounts.forward(0))
            pl.when(m >= 2)(lambda: stats.forward(m - 2))

        loop(0, batches, moments_step)

        def gram(m):
            for k in range(hops):
                xt = xt_ref[m, k]
                masked = [xt * xt[HOT + g : HOT + g + 1] for g in range(groups)]
                here = dot(jnp.concatenate(masked, axis=0), xt, NT)
                by_bucket = [here[g * LANES : g * LANES + HOT] for g in range(groups)]
                block = jnp.concatenate(by_bucket, axis=1)
                block = jnp.concatenate([block, jnp.zeros((LANES - HOT, width), F32)], axis=0)
                start = pl.multiple_of((m * hops + k) * LANES, LANES)
                part_mid[pl.ds(start, LANES)] = block.astype(BF16)

        def end_gram(m):
            grams[m].end_down(2)
            rows = pl.multiple_of(m * hops * LANES + owned * 16, 16)
            gram_own[m * 16 : (m + 1) * 16] = part_mid[pl.ds(rows, 16)]

        def gram_step(m):
            if early:
                gram(m)
                for i in range(batches):
                    at(m, i, lambda i=i: grams[i].start_down(0))

            @pl.when(m == 0)
            def _():
                stats.forward(final - 1)
                stats.back(0)

            @pl.when(m == 1)
            def _():
                stats.forward(final)
                stats.back(1)

        loop(0, batches, gram_step)
        if early:
            grams[0].advance(0)
        amounts.finish(0)
        w_mid_copy.wait()
        stats.back(final - 1)
        stats.finish(0)

        def counts_of(m):
            here = lax.broadcasted_iota(jnp.int32, (tables, LANES), 1) == m
            counts = jnp.sum(jnp.where(here, c_total[0], 0.0), axis=1, keepdims=True)
            return jnp.broadcast_to(counts, (tables, LANES))

        def bucket_tables(m):
            counts = counts_of(m)
            for j in range(pieces):
                base = 2 * tables * j
                mean = t_total[m, base : base + tables] / counts
                second = t_total[m, base + tables : base + 2 * tables] / counts
                inv = lax.rsqrt(second - mean * mean + EPSILON)
                a = 0.5 * gain_rep[:, lane[j]] * inv
                tab_a[m, :, lane[j]] = a
                tab_b[m, :, lane[j]] = 0.5 * shift_rep[:, lane[j]] - a * mean

        def choose(masks, values, k, j):
            result = values[k * groups + groups - 1 : k * groups + groups, lane[j]]
            for g in range(groups - 2, -1, -1):
                result = jnp.where(masks[g], values[k * groups + g : k * groups + g + 1, lane[j]], result)
            return result

        def masks_of(m, rows):
            cat = cat_ref[m, rows].astype(F32)
            return [cat == float(g) for g in range(groups - 1)]

        chunks = [slice(i * chunk, (i + 1) * chunk) for i in range(nodes // chunk)]

        def forward(m):
            bucket_tables(m)

            def product(k):
                middle = dot(join_ref[m, :, columns[k]], w_mid_ref[columns[k]])
                mid_ref[m] = middle if k == 0 else mid_ref[m] + middle

            for k in range(hops):
                if k:
                    product(k - 1)
                    present = present_ref.at[k % 2]
                    present[...] = by_node(active_row(m, k))
                for rows in chunks:
                    masks = masks_of(m, rows)
                    for j in range(pieces):
                        bend = 0.5 - 0.5 * slope_ref[k : k + 1, lane[j]]
                        bend_cat = 0.5 - 0.5 * slope_cat_ref[:, k * width + j * LANES : k * width + (j + 1) * LANES]
                        scale = choose(masks, tab_a.at[m], k, j)
                        offset = choose(masks, tab_b.at[m], k, j)
                        if k:
                            offset = offset * present[rows]
                        u = u_ref[m, k, rows, lane[j]] * scale + offset
                        u_ref[m, k, rows, lane[j]] = u
                        half = u - (bend * u) * (1.0 - jnp.tanh(u))
                        half = half - (bend_cat * half) * (1.0 - jnp.tanh(half))
                        join_ref[m, rows, k * width + j * LANES : k * width + (j + 1) * LANES] = half.astype(BF16)
            product(hops - 1)
            middle = mid_ref[m]
            first = jnp.sum(middle, axis=0, keepdims=True)
            second = jnp.sum(middle * middle, axis=0, keepdims=True)
            own = heads.own(m)
            for j in range(pieces):
                own[j : j + 1] = first[:, lane[j]]
                own[pieces + j : pieces + j + 1] = second[:, lane[j]]

        def row_of(ref, m, first):
            return jnp.concatenate([ref[m, first + j : first + j + 1] for j in range(pieces)], axis=1)

        def head_scale(m):
            mean = row_of(s_total, m, 0) * (1.0 / nodes_batch)
            second = row_of(s_total, m, pieces) * (1.0 / nodes_batch)
            inv = lax.rsqrt(4.0 * (second - mean * mean) + EPSILON)
            return mean, inv

        def head(m):
            heads.finish(m)
            mean, inv = head_scale(m)
            scale = gain_mid_ref[...] * inv
            offset = 0.5 * shift_mid_ref[...] - scale * mean
            slope = slope_mid_ref[...]
            u = mid_ref[m] * scale + offset
            mid_ref[m] = u
            tanh = jnp.tanh(u)
            gap = u * (1.0 - tanh)
            outer = (2.0 * u - (1.0 - slope) * gap).astype(BF16)
            logits = dot(w_out_ref[...], outer, NT) + bias_ref[:, 0:1]
            top = jnp.max(logits, axis=0, keepdims=True)
            powers = jnp.exp(logits - top)
            total = jnp.sum(powers, axis=0, keepdims=True)
            wanted = (lax.broadcasted_iota(jnp.int32, logits.shape, 0) == labels_ref[pl.ds(m, 1)]).astype(F32)
            loss = jnp.log(total) + top - jnp.sum(logits * wanted, axis=0, keepdims=True)
            dlogits = (powers / total - wanted) * (1.0 / total_nodes)
            low = dlogits.astype(BF16)
            grad_out_ref[...] += dot(low, outer)
            douter = dot(low, w_out_ref[...], TN)
            grad_slope = jnp.sum(douter * gap, axis=0, keepdims=True)
            dshaped = douter * (slope + (0.5 - 0.5 * slope) * (1.0 + tanh) * (1.0 + gap))
            dshaped_ref[m] = dshaped
            head_sum = jnp.sum(dshaped, axis=0, keepdims=True)
            head_dot = jnp.sum(dshaped * u, axis=0, keepdims=True)
            own = backs.own(m)
            for j in range(pieces):
                own[j : j + 1] = head_sum[:, lane[j]]
                own[pieces + j : pieces + j + 1] = head_dot[:, lane[j]]
                own[2 * pieces + j : 2 * pieces + j + 1] = grad_slope[:, lane[j]]
            folded = sum(dlogits[:, i * LANES : (i + 1) * LANES] for i in range(nodes // LANES))
            square = jnp.concatenate([folded, jnp.zeros((LANES - folded.shape[0], LANES), F32)], axis=0)
            own[3 * pieces : 3 * pieces + 1] = jnp.sum(jnp.transpose(square), axis=0, keepdims=True)
            own[3 * pieces + 1 : 3 * pieces + 2] = sum(
                loss[:, i * LANES : (i + 1) * LANES] for i in range(nodes // LANES)
            )
            own[3 * pieces + 2 :] = jnp.zeros((own.shape[0] - 3 * pieces - 2, LANES), F32)
            backs.start(m)

        def head_grads(m):
            inv = head_scale(m)[1]
            head_sum = row_of(e_total, m, 0)
            head_dot = (2.0 * row_of(e_total, m, pieces) - shift_mid_ref[...] * head_sum) / gain_mid_ref[...]
            return inv, head_sum, head_dot

        def back_head(m):
            backs.finish(m)
            inv, head_sum, head_dot = head_grads(m)
            scale = gain_mid_ref[...] * inv
            tilt = 2.0 * inv * head_dot * (1.0 / nodes_batch)
            level = scale * head_sum * (1.0 / nodes_batch) - 0.5 * shift_mid_ref[...] * tilt
            dmid_ref[m] = (scale * dshaped_ref[m] - level - mid_ref[m] * tilt).astype(BF16)

        gradients = [mid_ref.at[0], dshaped_ref.at[0]]

        def products(k):
            return (part_rest, total_rest)[k % 2].at[pl.ds(0, nodes)]

        def backward(m, which_hops, target, tick):
            def into(k):
                gradients[k % 2][...] = dot(dmid_ref[m], w_mid_ref[columns[k]], NT)

            def bucket_sums(k):
                hot = xt_ref[m, k, HOT:LANES]
                if early:
                    both = dot(xt_ref[m, k], target(k)[...])
                    grad_hops_ref[k, :HOT] += 2.0 * both[:HOT]
                    first = both[HOT:]
                else:
                    first = dot(hot, target(k)[...])
                second = dot(hot, products(k)[...])
                for j in range(pieces):
                    base = 2 * tables * j + k * groups
                    table[m, base : base + groups] = first[:groups, lane[j]]
                    table[m, base + tables : base + tables + groups] = second[:groups, lane[j]]

            into(which_hops[0])
            for k in which_hops:
                if k + 1 in which_hops:
                    into(k + 1)
                if k - 1 in which_hops:
                    bucket_sums(k - 1)
                slope_sums = [jnp.zeros((8, LANES), F32) for _ in range(2 * pieces)]
                result = target(k)
                for rows in chunks:
                    masks = masks_of(m, rows)
                    for j in range(pieces):
                        slope = slope_ref[k : k + 1, lane[j]]
                        slope_cat = slope_cat_ref[:, k * width + j * LANES : k * width + (j + 1) * LANES]
                        bend, bend_cat = 0.5 - 0.5 * slope, 0.5 - 0.5 * slope_cat
                        u = u_ref[m, k, rows, lane[j]]
                        tanh = jnp.tanh(u)
                        gap = (bend * u) * (1.0 - tanh)
                        half = u - gap
                        tanh_cat = jnp.tanh(half)
                        gap_cat = (bend_cat * half) * (1.0 - tanh_cat)
                        grad = gradients[k % 2][rows, lane[j]]
                        slope_sums[pieces + j] += jnp.sum((grad * gap_cat).reshape(-1, 8, LANES), axis=0)
                        grad = grad * (slope_cat + (1.0 + tanh_cat) * (bend_cat + gap_cat))
                        slope_sums[j] += jnp.sum((grad * gap).reshape(-1, 8, LANES), axis=0)
                        grad = grad * (slope + (1.0 + tanh) * (bend + gap))
                        grad = grad * choose(masks, tab_a.at[m], k, j)
                        result[rows, lane[j]] = grad.astype(BF16)
                        products(k)[rows, lane[j]] = (grad * u).astype(BF16)
                for j in range(pieces):
                    slope = slope_ref[k : k + 1, lane[j]]
                    slope_cat = slope_cat_ref[:, k * width + j * LANES : k * width + (j + 1) * LANES]
                    for s, values in enumerate((slope, slope_cat)):
                        grad_hops_ref[k, feats + s : feats + s + 1, lane[j]] += jnp.sum(
                            slope_sums[s * pieces + j], axis=0, keepdims=True
                        ) / (0.5 - 0.5 * values)
                if k == which_hops[-1]:
                    bucket_sums(k)
                tick(k)

        def first_target(k):
            return total_mid.at[pl.ds(k * nodes, nodes)]

        def first_copy(k):
            return pltpu.make_async_copy(first_target(k), join_ref.at[0, :, pl.ds(k * width, width)], in_sems.at[k])

        def no_tick(k):
            pass

        def forward_step(m):
            pl.when(m >= 1)(lambda: stats.finish(m))
            forward(m)
            heads.start(m)
            pl.when(m >= 1)(lambda: heads.forward(m - 1))
            at(m, 0, lambda: stats.back(final))
            if early:
                for i in range(batches):
                    if i >= 1:
                        at(m, i, lambda i=i: end_gram(i - 1))
                    at(m, i, lambda i=i: grams[i].advance(1))
                    if i < final:
                        at(m, i, lambda i=i: grams[i + 1].advance(0))
            at(m, 2, lambda: head(0))

        loop(0, batches, forward_step)
        backs.forward(0)

        def head_step(m):
            head(m)

            @pl.when(m == 1)
            def _():
                heads.forward(final)

            @pl.when(m == 2)
            def _():
                backs.forward(1)
                back_head(0)
                backward(0, [0, 1], first_target, no_tick)

        loop(1, batches, head_step)
        backs.forward(2)
        if early:
            end_gram(final)

        def late_tick(k):
            if k == hops - 1:
                backs.forward(final)

        backward(0, list(range(2, hops)), first_target, late_tick)
        dots.start(0)
        for m in range(1, final):
            back_head(m)

        held = [mid_ref.at[m] for m in range(final)] + [dshaped_ref.at[0]]
        for k in range(hops):
            held[k][...] = sum(dot(join_ref[m, :, columns[k]], dmid_ref[m], TN) for m in range(final))
        back_head(final)
        for k in range(hops):
            total = held[k][...] + dot(join_ref[final, :, columns[k]], dmid_ref[final], TN)
            part_mid[columns[k]] = (2.0 * total).astype(BF16)
            if (k + 1) * mid_parts % hops == 0:
                mids[(k + 1) * mid_parts // hops - 1].start_down(0)
        for k in range(hops):
            first_copy(k).start()
        dots.forward(0)

        def wait_first():
            for k in range(hops):
                first_copy(k).wait()

        ticks = {
            (1, 0): [wait_first],
            (1, 1): [lambda: mid_step(0, 0)],
            (1, 2): [lambda: mid_step(1, 0), lambda: dots.back(0)],
            (2, 0): [lambda: mid_step(0, 1)],
            (2, 1): [lambda: mid_step(1, 1)],
            (2, 2): [lambda: dots.forward(1)],
            (2, 3): [lambda: mid_step(0, 2)],
            (3, 0): [lambda: mid_step(1, 2)],
            (3, 1): [lambda: dots.back(1)],
            (3, 2): [lambda: dots.forward(2)],
            (3, 3): [lambda: mid_step(0, 3)],
        }

        def backward_step(m):
            def tick(k):
                for when, bodies in ticks.items():
                    if when[1] == k:
                        for body in bodies:
                            at(m, when[0], body)

            backward(m, list(range(hops)), lambda k: join_ref.at[m, :, columns[k]], tick)
            dots.start(m)

        loop(1, batches, backward_step)

        def last_tables(m):
            counts = counts_of(m)
            for j in range(pieces):
                base = 2 * tables * j
                a = tab_a[m, :, lane[j]]
                inv = 2.0 * a / gain_rep[:, lane[j]]
                shift = shift_rep[:, lane[j]]
                scaled = t_total[m, base : base + tables]
                bucket_sum = scaled / a
                bucket_dot = (2.0 * t_total[m, base + tables : base + 2 * tables] / a - shift * bucket_sum) / gain_rep[
                    :, lane[j]
                ]
                tilt = inv * bucket_dot / counts
                tab_f[:, lane[j]] = tilt
                tab_e[:, lane[j]] = scaled / counts - 0.5 * shift * tilt
                for k in range(hops):
                    here = slice(k * groups, (k + 1) * groups)
                    slopes_ref[k : k + 1, lane[j]] += jnp.sum(bucket_dot[here], axis=0, keepdims=True)
                    slopes_ref[hops + k : hops + k + 1, lane[j]] += jnp.sum(bucket_sum[here], axis=0, keepdims=True)

        def own_tables(m):
            for k in range(hops):
                rows = slice(k * groups, (k + 1) * groups)

                @pl.when(owned_hop == k)
                def _(rows=rows):
                    tilt = tab_f[rows]
                    scale_own[m] = tilt * tab_a[m, rows]
                    level_own[m] = tab_e[rows] + tilt * tab_b[m, rows]

        def last(m):
            dots.finish(m)
            last_tables(m)
            if early:
                own_tables(m)

            def weights(k):
                grad_hops_ref[k, :HOT] += dot(xt_ref[m, k, :HOT], join_ref[m, :, columns[k]]) * 2.0

            for k in range(hops):
                if k and not early:
                    weights(k - 1)
                for rows in chunks:
                    masks = masks_of(m, rows)
                    for j in range(pieces):
                        here = slice(k * width + j * LANES, k * width + (j + 1) * LANES)
                        grad = join_ref[m, rows, here].astype(F32) - choose(masks, tab_e, k, j)
                        grad = grad - choose(masks, tab_f, k, j) * u_ref[m, k, rows, lane[j]]
                        join_ref[m, rows, here] = grad.astype(BF16)
            if not early:
                weights(hops - 1)

        def correction():
            total = jnp.zeros((16, width), F32)
            weights = w_ref[owned_hop].astype(F32)
            row = lax.broadcasted_iota(jnp.int32, (LANES, width), 0)
            for m in range(batches):
                scaled = [
                    jnp.where(row == HOT + g, level_own[m, g : g + 1], weights * scale_own[m, g : g + 1]).astype(BF16)
                    for g in range(groups)
                ]
                total = total + dot(gram_own[m * 16 : (m + 1) * 16], jnp.concatenate(scaled, axis=0))
            return 2.0 * total

        def features_copy(m):
            return pltpu.make_async_copy(spread.at[pl.ds(0, spread_rows)], out_features.at[m], out_sems.at[m])

        def features(m):
            pl.when(m >= 1)(lambda: features_copy(m - 1).wait())
            for k in range(hops):
                scale = active_row(m, k) * float(2 * total_nodes)
                values = dot(w_ref[k], join_ref[m, :, columns[k]], NT) * scale
                for j in range(pieces):
                    spread[pl.ds(j * hops + k, feats, stride=pieces * hops)] = values[:feats, lane[j]]
            features_copy(m).start()

        def start_rests():
            rows = grad_out_ref.shape[0] // hops
            for k in range(hops):
                grad_hops_ref[k, SPARE : SPARE + rows] = grad_out_ref[k * rows : (k + 1) * rows]
                part_rest[k * LANES : (k + 1) * LANES] = grad_hops_ref[k].astype(BF16)
            if part_rest.shape[0] > hops * LANES:
                part_rest[hops * LANES :] = jnp.zeros((part_rest.shape[0] - hops * LANES, width), BF16)
            rests.start_down(0)

        def last_step(m):
            last(m)

            @pl.when(m == 0)
            def _():
                if early:
                    rests.advance(0)
                dots.back(2)
                mid_step(1, 3)

            at(m, 1, lambda: mid_step(0, 4))
            at(m, 2, lambda: mid_step(0, 5))

            @pl.when(m == 3)
            def _():
                if early:
                    rests.advance(2, correction())
                else:
                    start_rests()

            features(m)
            at(m, 0, lambda: dots.forward(final))

            @pl.when(m == 1)
            def _():
                dots.back(final)
                if early:
                    rests.advance(1)
                mid_step(1, 4)

            at(m, 2, lambda: mid_step(1, 5))
            at(m, 3, lambda: mid_step(0, 6))

        if early:
            start_rests()
        loop(0, batches, last_step)
        if not early:
            for stage in range(3):
                rests.advance(stage)

        grad_gain = jnp.zeros((1, width), F32)
        grad_shift = jnp.zeros((1, width), F32)
        grad_slope = jnp.zeros((1, width), F32)
        bias_loss = jnp.zeros((2, LANES), F32)
        for m in range(batches):
            _, head_sum, head_dot = head_grads(m)
            grad_gain = grad_gain + head_dot
            grad_shift = grad_shift + head_sum
            grad_slope = grad_slope + row_of(e_total, m, 2 * pieces)
            bias_loss = bias_loss + e_total[m, 3 * pieces : 3 * pieces + 2]
        out_small[: 2 * hops] = slopes_ref[...]
        loss = jnp.sum(bias_loss[1:2], axis=1, keepdims=True) * (1.0 / total_nodes)
        last_row = [bias_loss[0:1], jnp.broadcast_to(loss, (1, LANES)), jnp.zeros((1, width - 2 * LANES), F32)]
        for i, row in enumerate((grad_gain, grad_shift, grad_slope, jnp.concatenate(last_row, axis=1))):
            out_small[2 * hops + i : 2 * hops + i + 1] = row

        mid_step(1, 6)
        rests.advance(3)
        mid_step(0, 7)
        rests.advance(4)
        mid_step(1, 7)
        mid_file = pltpu.make_async_copy(total_mid, out_mid, file_sems.at[0])
        mid_file.start()
        rests.advance(5)
        rest_file = pltpu.make_async_copy(total_rest.at[pl.ds(0, hops * LANES)], out_rest, file_sems.at[1])
        rest_file.start()
        features_copy(final).wait()
        mid_file.wait()
        rest_file.wait()

    return kernel


def make_finish(dims):
    (groups, dps, batches, nodes, hops, feats, width, classes) = dims
    pieces = width // LANES
    spare = -(-classes // 16) * 16 // hops

    def kernel(
        features_in, mid_in, rest_in, small_in,
        features, mid, hops_grad, gain, shift, slope, cat, gain_mid, shift_mid, slope_mid, out_grad, bias, loss,
        low, wide, held, sems,
    ):
        in_copy = [pltpu.make_async_copy(features_in.at[m], held.at[m], sems.at[0, m]) for m in range(batches)]
        out_copy = [pltpu.make_async_copy(held.at[m], features.at[m], sems.at[3, m]) for m in range(batches)]
        low_copy = [pltpu.make_async_copy(mid_in.at[pl.ds(k * width, width)], low.at[k], sems.at[1, k]) for k in range(hops)]
        wide_copy = [pltpu.make_async_copy(wide.at[k], mid.at[pl.ds(k * width, width)], sems.at[2, k]) for k in range(hops)]
        for copy in low_copy + in_copy:
            copy.start()
        for k in range(hops):
            values = rest_in[k * LANES : (k + 1) * LANES].astype(F32)
            for j in range(pieces):
                hops_grad[pl.ds(j * hops + k, feats, stride=pieces * hops)] = values[
                    :feats, j * LANES : (j + 1) * LANES
                ]
            slope[k : k + 1] = values[feats : feats + 1]
            cat[:, k * width : (k + 1) * width] = values[feats + 1 : feats + 2]
            count = min(spare, classes - k * spare)
            out_grad[k * spare : k * spare + count] = values[SPARE : SPARE + count]
        gain[...] = small_in[:hops]
        shift[...] = small_in[hops : 2 * hops]
        gain_mid[...] = small_in[2 * hops : 2 * hops + 1]
        shift_mid[...] = small_in[2 * hops + 1 : 2 * hops + 2]
        slope_mid[...] = small_in[2 * hops + 2 : 2 * hops + 3]
        bias[...] = small_in[2 * hops + 3 : 2 * hops + 4, :classes]
        loss[...] = small_in[2 * hops + 3 : 2 * hops + 4, LANES : LANES + 1]
        for k in range(hops):
            low_copy[k].wait()
            wide[k] = low[k].astype(F32)
            wide_copy[k].start()
        for m in range(batches):
            in_copy[m].wait()
            out_copy[m].start()
        for copy in wide_copy + out_copy:
            copy.wait()

    return kernel


def by_piece(values):
    *lead, feats, hops, width = values.shape
    values = jnp.swapaxes(values.reshape(*lead, feats, hops, width // LANES, LANES), -3, -2)
    return values.reshape(*lead, feats * hops * width // LANES, LANES)


def by_hop(rows, hops, pieces):
    *lead, count, _ = rows.shape
    values = rows.reshape(*lead, count // (hops * pieces), pieces, hops, LANES)
    return jnp.swapaxes(values, -3, -2).reshape(*lead, count // (hops * pieces), hops, pieces * LANES)


def shards(
    features,
    buckets,
    hop_mask,
    labels,
    w_hops,
    gain_hops,
    shift_hops,
    slope_hops,
    slope_cat,
    w_mid,
    gain_mid,
    shift_mid,
    slope_mid,
    w_out,
    bias_out,
):
    batches, nodes, hops, feats = features.shape
    width, classes = w_out.shape
    groups, dps = lax.axis_size("bucket"), lax.axis_size("dp")
    dims = (groups, dps, batches, nodes, hops, feats, width, classes)
    pieces = width // LANES
    joined_width = hops * width
    tables = hops * groups
    padded = -(-classes // 16) * 16

    wide, low, high = groups // 2, dps // 4, 4
    sizes = {"wide": wide, "low": low, "high": high, "plane": wide * low}
    rows_rest = max(hops * LANES, 2 * wide * low * 16)
    early, mid_parts = plan(groups, dps, hops, width)
    mid_shapes = GradSum.stage_shapes(joined_width // mid_parts, width, MID_ORDERS, sizes)
    gram_count = batches if early else 0
    own_rows = 16 * batches if early else 16
    rest_shapes = GradSum.stage_shapes(rows_rest, width, REST_ORDERS, sizes)
    _, nears, fars = Place.group_sizes(groups, dps)
    table_rows = 2 * tables * pieces
    share = table_rows // nears
    sem = pltpu.SemaphoreType.DMA

    def small_scratch(rows, copies=batches):
        return [
            pltpu.VMEM((copies, nears, rows, LANES), F32),
            pltpu.VMEM((copies, fars, rows, LANES), F32),
            pltpu.VMEM((copies, rows, LANES), F32),
        ]

    vmem = pl.BlockSpec(memory_space=pltpu.VMEM)
    hbm = pl.BlockSpec(memory_space=pl.ANY)

    def real(*shape):
        return jax.ShapeDtypeStruct(shape, F32)

    outs = pl.pallas_call(
        make_kernel(dims),
        name="train_step",
        out_shape=(
            real(batches, feats * pieces * hops, LANES),
            jax.ShapeDtypeStruct((joined_width, width), BF16),
            jax.ShapeDtypeStruct((hops * LANES, width), BF16),
            real(2 * hops + 4, width),
        ),
        in_specs=[hbm] + [vmem] * 3 + [hbm] + [vmem] * 4 + [hbm] + [vmem] * 5,
        out_specs=(hbm, hbm, hbm, vmem),
        scratch_shapes=[
            pltpu.VMEM((HOT * pieces * hops, LANES), F32),
            pltpu.VMEM((batches, hops, nodes, width), F32),
            pltpu.VMEM((batches, nodes, joined_width), BF16),
            pltpu.VMEM((batches, hops, LANES, nodes), BF16),
            pltpu.VMEM((batches, nodes, LANES), BF16),
            pltpu.VMEM((2, nodes, LANES), F32),
            pltpu.VMEM((batches, nodes, width), F32),
            pltpu.VMEM((batches, nodes, width), F32),
            pltpu.VMEM((batches, nodes, width), BF16),
            pltpu.VMEM((hops, LANES, width), F32),
            pltpu.VMEM((padded, width), F32),
            pltpu.VMEM((hops, LANES, width), BF16),
            pltpu.VMEM((joined_width, width), BF16),
            pltpu.VMEM((padded, width), BF16),
            pltpu.VMEM((padded, LANES), F32),
            pltpu.VMEM((tables, width), F32),
            pltpu.VMEM((tables, width), F32),
        ]
        + [pltpu.VMEM((batches, tables, width), F32) for _ in range(2)]
        + [pltpu.VMEM((tables, width), F32) for _ in range(2)]
        + [pltpu.VMEM((2 * hops, width), F32)]
        + [pltpu.VMEM((batches, table_rows, LANES), F32)]
        + [pltpu.VMEM((batches, nears, share, LANES), F32), pltpu.VMEM((batches, fars, share, LANES), F32)]
        + [pltpu.VMEM((batches, table_rows, LANES), F32)]
        + small_scratch(8)
        + small_scratch(16)
        + small_scratch(tables, 1)
        + [
            pltpu.VMEM((joined_width, width), BF16),
            pltpu.VMEM((joined_width, width), BF16),
            pltpu.VMEM((rows_rest, width), BF16),
            pltpu.VMEM((rows_rest, width), BF16),
            [[pltpu.VMEM(s, BF16) for s in mid_shapes] for _ in range(mid_parts)],
            [pltpu.VMEM(s, BF16) for s in rest_shapes],
            pltpu.VMEM((own_rows, width), BF16),
            pltpu.VMEM((batches, groups, width), F32),
            pltpu.VMEM((batches, groups, width), F32),
            [[pltpu.VMEM(s, BF16) for s in rest_shapes] for _ in range(gram_count)],
            [sem((batches,)) for _ in range(6)],
            [sem((batches,)) for _ in range(4)],
            [sem((batches,)) for _ in range(4)],
            [sem((1,)) for _ in range(4)],
            [sem((batches,)) for _ in range(6)],
            [[sem((len(mid_shapes),)) for _ in range(4)] for _ in range(mid_parts)],
            [sem((len(rest_shapes),)) for _ in range(4)],
            [[sem((len(rest_shapes),)) for _ in range(4)] for _ in range(gram_count)],
            sem((max(batches, hops),)),
            sem((batches,)),
            sem((3,)),
        ],
        compiler_params=pltpu.CompilerParams(
            collective_id=0, has_side_effects=True, vmem_limit_bytes=int(63.9 * 2**20)
        ),
    )(
        by_piece(jnp.transpose(features, (0, 3, 2, 1))),
        jnp.transpose(buckets, (0, 2, 1)),
        jnp.transpose(hop_mask, (2, 0, 1)),
        labels,
        by_piece(jnp.transpose(w_hops, (1, 0, 2))),
        gain_hops,
        shift_hops,
        slope_hops,
        slope_cat[None],
        w_mid,
        gain_mid[None],
        shift_mid[None],
        slope_mid[None],
        w_out.T,
        bias_out[None],
    )
    outs = pl.pallas_call(
        make_finish(dims),
        name="finish",
        out_shape=(
            real(batches, feats * pieces * hops, LANES),
            real(joined_width, width),
            real(feats * pieces * hops, LANES),
            real(hops, width),
            real(hops, width),
            real(hops, width),
            real(1, joined_width),
            real(1, width),
            real(1, width),
            real(1, width),
            real(classes, width),
            real(1, classes),
            real(1, 1),
        ),
        in_specs=[hbm, hbm, vmem, vmem],
        out_specs=(hbm, hbm) + (vmem,) * 11,
        scratch_shapes=[
            pltpu.VMEM((hops, width, width), BF16),
            pltpu.VMEM((hops, width, width), F32),
            pltpu.VMEM((batches, feats * pieces * hops, LANES), F32),
            sem((4, max(batches, hops))),
        ],
        compiler_params=pltpu.CompilerParams(vmem_limit_bytes=int(63.9 * 2**20)),
    )(*outs)
    (features_grad, mid_grad, hops_grad, gain, shift, slope, cat, gain_m, shift_m, slope_m, out_grad, bias, loss) = outs
    return (
        loss[0, 0],
        jnp.transpose(by_hop(features_grad, hops, nodes // LANES), (0, 3, 2, 1)),
        jnp.transpose(by_hop(hops_grad, hops, pieces), (1, 0, 2)),
        gain,
        shift,
        slope,
        cat[0],
        mid_grad,
        gain_m[0],
        shift_m[0],
        slope_m[0],
        out_grad.T,
        bias[0],
    )


def solution(mesh):
    nodes_split = ("bucket", "dp")
    placed = (
        P(None, nodes_split, None, None),
        P(None, nodes_split, None),
        P(None, nodes_split, None),
        P(None, nodes_split),
    ) + (P(),) * 11
    return jax.shard_map(
        shards,
        mesh=mesh,
        in_specs=placed,
        out_specs=(P(), P(None, nodes_split, None, None)) + (P(),) * 11,
        check_vma=False,
    )
```

```python
import functools

import jax
import jax.numpy as jnp
from jax import lax
from jax.experimental import pallas as pl
from jax.experimental.pallas import tpu as pltpu
from jax.sharding import PartitionSpec as P

F32 = jnp.float32
BF16 = jnp.bfloat16
EPSILON = 1e-05
MESH = pl.DeviceIdType.MESH
LANES = 128
HOT = 112
SPARE = 104
MID_ORDERS = (("wide", "low", "high"), ("low", "wide", "high"))
REST_ORDERS = (("plane", "high"),)
NN, NT, TN = ((1,), (0,)), ((1,), (1,)), ((0,), (0,))


def dot(left, right, dims=NN):
    return lax.dot_general(left, right, (dims, ((), ())), preferred_element_type=F32)


def split_high(values):
    high = values.astype(BF16)
    return high, (values - high.astype(F32)).astype(BF16)


class Place:
    def __init__(self, groups, dps):
        self.groups, self.dps = groups, dps
        self.high = 4
        self.low = dps // self.high
        self.wide = groups // 2
        self.b = lax.axis_index("bucket")
        self.d = lax.axis_index("dp")
        self.core = lax.rem(self.b, 2)
        self.x = lax.div(self.b, 2)
        self.lo = lax.rem(self.d, self.low)
        self.hi = lax.div(self.d, self.low)
        self.fold, self.nears, self.fars = self.group_sizes(groups, dps)
        self.near = self.b * self.fold + lax.rem(self.d, self.fold)
        self.far = lax.div(self.d, self.fold)

    @staticmethod
    def group_sizes(groups, dps):
        low = dps // 4
        fold = low if groups * low <= 8 else 1
        return fold, groups * fold, dps // fold

    def at(self, b=None, d=None):
        return {"bucket": self.b if b is None else b, "dp": self.d if d is None else d}

    def near_peer(self, o):
        i = lax.rem(self.near + o, self.nears)
        b, lo = lax.div(i, self.fold), lax.rem(i, self.fold)
        return i, self.at(b=b, d=lax.div(self.d, self.fold) * self.fold + lo)

    def far_peer(self, o):
        i = lax.rem(self.far + o, self.fars)
        return i, self.at(d=i * self.fold + lax.rem(self.d, self.fold))

    def axis(self, name):
        if name == "core":
            return self.core, 2, lambda o: (1 - self.core, self.at(b=2 * self.x + 1 - self.core))
        if name == "wide":
            def peer(o):
                i = lax.rem(self.x + o, self.wide)
                return i, self.at(b=2 * i + self.core)
            return self.x, self.wide, peer
        if name == "low":
            def peer(o):
                i = lax.rem(self.lo + o, self.low)
                return i, self.at(d=self.hi * self.low + i)
            return self.lo, self.low, peer

        if name == "plane":
            own = self.x * self.low + self.lo

            def peer(o):
                i = lax.rem(own + o, self.wide * self.low)
                b = 2 * lax.div(i, self.low) + self.core
                return i, self.at(b=b, d=self.hi * self.low + lax.rem(i, self.low))
            return own, self.wide * self.low, peer

        def peer(o):
            i = lax.rem(self.hi + o, self.high)
            return i, self.at(d=i * self.low + self.lo)
        return self.hi, self.high, peer


def remote(src, dst, sems, index, device):
    send, recv = sems
    return pltpu.make_async_remote_copy(
        src_ref=src,
        dst_ref=dst,
        send_sem=send.at[index],
        recv_sem=recv.at[index],
        device_id=device,
        device_id_type=MESH,
    )


def wait_all(copied, sems, index, device):
    remote(copied, copied, sems, index, device).wait()


class SmallSum:
    def __init__(self, place, near, far, total, near_sems, far_sems):
        self.place, self.near, self.far, self.total = place, near, far, total
        self.near_sems, self.far_sems = near_sems, far_sems

    def own(self, m):
        return self.near.at[m, self.place.near]

    def near_copies(self, m):
        mine = self.near.at[m, self.place.near]
        return [
            remote(mine, mine, self.near_sems, m, self.place.near_peer(o)[1])
            for o in range(1, self.place.nears)
        ]

    def far_copies(self, m):
        mine = self.far.at[m, self.place.far]
        return [
            remote(mine, mine, self.far_sems, m, self.place.far_peer(o)[1])
            for o in range(1, self.place.fars)
        ]

    def start(self, m):
        for copy in self.near_copies(m):
            copy.start()

    def forward(self, m):
        place = self.place
        wait_all(self.near.at[m, pl.ds(0, place.nears - 1)], self.near_sems, m, place.near_peer(1)[1])
        self.far[m, self.place.far] = sum(self.near[m, i] for i in range(self.place.nears))
        for copy in self.far_copies(m):
            copy.start()

    def finish(self, m):
        place = self.place
        wait_all(self.far.at[m, pl.ds(0, place.fars - 1)], self.far_sems, m, place.far_peer(1)[1])
        self.total[m] = sum(self.far[m, i] for i in range(self.place.fars))


class TableSum:
    def __init__(self, place, table, near, far, total, near_sems, far_sems, back_sems):
        self.place, self.table, self.near, self.far, self.total = place, table, near, far, total
        self.near_sems, self.far_sems, self.back_sems = near_sems, far_sems, back_sems
        self.rows = table.shape[1] // place.nears

    def share(self, i):
        return pl.ds(pl.multiple_of(i * self.rows, 8), self.rows)

    def near_copies(self, m):
        mine = self.near.at[m, self.place.near]
        copies = []
        for o in range(1, self.place.nears):
            i, device = self.place.near_peer(o)
            copies.append(remote(self.table.at[m, self.share(i)], mine, self.near_sems, m, device))
        return copies

    def far_copies(self, m):
        mine = self.far.at[m, self.place.far]
        return [
            remote(mine, mine, self.far_sems, m, self.place.far_peer(o)[1])
            for o in range(1, self.place.fars)
        ]

    def back_copies(self, m):
        mine = self.total.at[m, self.share(self.place.near)]
        return [
            remote(mine, mine, self.back_sems, m, self.place.near_peer(o)[1])
            for o in range(1, self.place.nears)
        ]

    def start(self, m):
        for copy in self.near_copies(m):
            copy.start()
        self.near[m, self.place.near] = self.table[m, self.share(self.place.near)]

    def forward(self, m):
        place = self.place
        wait_all(self.near.at[m, pl.ds(0, place.nears - 1)], self.near_sems, m, place.near_peer(1)[1])
        self.far[m, self.place.far] = sum(self.near[m, i] for i in range(self.place.nears))
        for copy in self.far_copies(m):
            copy.start()

    def back(self, m):
        place = self.place
        wait_all(self.far.at[m, pl.ds(0, place.fars - 1)], self.far_sems, m, place.far_peer(1)[1])
        self.total[m, self.share(self.place.near)] = sum(self.far[m, i] for i in range(self.place.fars))
        for copy in self.back_copies(m):
            copy.start()

    def finish(self, m):
        place = self.place
        rows = self.total.at[m, pl.ds(0, (place.nears - 1) * self.rows)]
        wait_all(rows, self.back_sems, m, place.near_peer(1)[1])


class GradSum:
    def __init__(self, place, part, total, stages, sems, orders):
        self.part, self.total, self.stages, self.sems = part, total, stages, sems
        half = part.shape[0] // 2
        core = place.axis("core")
        self.steps = [[(core, 0, half, 0)]] + [[] for _ in orders[0]]
        slot = 1
        for h, order in enumerate(orders):
            size = half // len(orders)
            start = core[0] * half + h * size
            for i, name in enumerate(order):
                axis = place.axis(name)
                self.shared = i == len(order) - 1 and size % (16 * axis[1]) != 0
                if not self.shared:
                    size = size // axis[1]
                self.steps[i + 1].append((axis, start, size, slot))
                start = start + axis[0] * size
                slot += 1

    @staticmethod
    def stage_shapes(rows, columns, orders, sizes):
        shapes = [(1, rows // 2, columns)]
        for order in orders:
            size = rows // 2 // len(orders)
            for i, name in enumerate(order):
                n = sizes[name]
                if i == len(order) - 1 and size % (16 * n):
                    shapes.append((n, size, columns))
                else:
                    size //= n
                    shapes.append((n - 1, size, columns))
            assert size % 16 == 0
        return shapes

    def rows(self, base, size, index):
        return pl.ds(pl.multiple_of(base + index * size, 16), size)

    def whole(self, step):
        return self.shared and step == len(self.steps) - 1

    def down(self, step):
        copies = []
        for (own, n, peer), base, size, slot in self.steps[step]:
            for o in range(1, n):
                i, device = peer(o)
                if self.whole(step):
                    src, dst = self.part.at[self.rows(base, size, 0)], self.stages[slot].at[own]
                else:
                    src, dst = self.part.at[self.rows(base, size, i)], self.stages[slot].at[o - 1]
                copies.append(remote(src, dst, self.sems[:2], slot, device))
        return copies

    def up(self, step):
        copies = []
        for (own, n, peer), base, size, slot in [] if self.whole(step) else self.steps[step]:
            mine = self.total.at[self.rows(base, size, own)]
            for o in range(1, n):
                copies.append(remote(mine, mine, self.sems[2:], slot, peer(o)[1]))
        return copies

    def start_down(self, step):
        for copy in self.down(step):
            copy.start()

    def end_down(self, step, less=None):
        last = step == len(self.steps) - 1
        for (own, n, peer), base, size, slot in self.steps[step]:
            wait_all(self.stages[slot].at[pl.ds(0, n - 1)], self.sems[:2], slot, peer(1)[1])
            piece = min(size, 64)
            if self.whole(step):
                rows = self.rows(base, size, 0)
                self.stages[slot][own] = self.part[rows]
                self.total[rows] = sum(self.stages[slot][i].astype(F32) for i in range(n)).astype(BF16)
                continue

            def add(i, carry):
                rows = pl.ds(pl.multiple_of(base + own * size + i * piece, 16), piece)
                there = pl.ds(pl.multiple_of(i * piece, 16), piece)
                total = self.part[rows].astype(F32)
                for o in range(1, n):
                    total = total + self.stages[slot][o - 1, there].astype(F32)
                if less is not None:
                    total = total - less
                (self.total if last else self.part)[rows] = total.astype(BF16)
                return carry

            lax.fori_loop(0, size // piece, add, 0)

    def start_up(self, step):
        for copy in self.up(step):
            copy.start()

    def end_up(self, step):
        for (own, n, peer), base, size, slot in [] if self.whole(step) else self.steps[step]:
            rows = self.total.at[pl.ds(pl.multiple_of(base, 16), (n - 1) * size)]
            wait_all(rows, self.sems[2:], slot, peer(1)[1])

    def advance(self, stage, less=None):
        last = len(self.steps) - 1
        if stage <= last:
            self.end_down(stage, less if stage == last else None)
            if stage < last:
                self.start_down(stage + 1)
            else:
                self.start_up(last)
        else:
            step = 2 * last + 1 - stage
            self.end_up(step)
            if step:
                self.start_up(step - 1)


def plan(groups, dps, hops, width):
    wide, low, high = groups // 2, dps // 4, 4
    early = groups * LANES == width and 2 * wide * low * high * 16 == hops * LANES
    parts = 2 if hops % 2 == 0 and hops * width % (2 * 4 * wide * low * high * 16) == 0 else 1
    return early, parts


def make_kernel(dims):
    (groups, dps, batches, nodes, hops, feats, width, classes) = dims
    pieces = width // LANES
    tables = hops * groups
    nodes_batch = nodes * groups * dps
    total_nodes = batches * nodes_batch
    chunk = 64
    final = batches - 1
    early, mid_parts = plan(groups, dps, hops, width)
    bands = LANES // 16
    lane = [slice(j * LANES, (j + 1) * LANES) for j in range(pieces)]
    columns = [slice(k * width, (k + 1) * width) for k in range(hops)]

    def kernel(
        x_in, bucket_ref, mask_ref, labels_ref, w_in, gain_ref, shift_ref, slope_ref, slope_cat_ref, w_mid_in,
        gain_mid_ref, shift_mid_ref, slope_mid_ref, w_out_in, bias_in,
        out_features, out_mid, out_rest, out_small,
        spread, u_ref, join_ref, xt_ref, cat_ref, w_shift_ref, mid_ref, dshaped_ref, dmid_ref, grad_hops_ref, grad_out_ref,
        w_ref, w_mid_ref, w_out_ref, bias_ref, gain_rep, shift_rep, tab_a, tab_b, tab_e, tab_f, slopes_ref,
        table, table_near, table_far, t_total, s_near, s_far, s_total, e_near, e_far, e_total, c_near, c_far, c_total,
        part_mid, total_mid, part_rest, total_rest, stages_mid, stages_rest, gram_own, scale_own, level_own, stages_gram,
        t_sems, s_sems, e_sems, c_sems, d_sems, mid_sems, rest_sems, gram_sems, in_sems, out_sems, file_sems,
    ):
        spread_rows = feats * pieces * hops
        place = Place(groups, dps)
        barrier = pltpu.get_barrier_semaphore()
        for o in range(1, place.nears):
            pl.semaphore_signal(barrier, inc=1, device_id=place.near_peer(o)[1], device_id_type=MESH)
        for o in range(1, place.fars):
            pl.semaphore_signal(barrier, inc=1, device_id=place.far_peer(o)[1], device_id_type=MESH)

        def landing(ref, m):
            return ref.at[pl.ds(0, spread_rows), pl.ds(pl.multiple_of(m * LANES, LANES), LANES)]

        def x_copy(m):
            return pltpu.make_async_copy(x_in.at[m], landing(part_mid, m), in_sems.at[m])

        w_copy = pltpu.make_async_copy(w_in, landing(total_mid, 0), file_sems.at[1])
        w_mid_copy = pltpu.make_async_copy(w_mid_in, w_mid_ref, file_sems.at[2])
        w_copy.start()
        for m in range(batches):
            x_copy(m).start()
        w_mid_copy.start()

        stats = TableSum(place, table, table_near, table_far, t_total, t_sems[0:2], t_sems[2:4], t_sems[4:6])
        heads = SmallSum(place, s_near, s_far, s_total, s_sems[0:2], s_sems[2:4])
        backs = SmallSum(place, e_near, e_far, e_total, e_sems[0:2], e_sems[2:4])
        dots = TableSum(place, table, table_near, table_far, t_total, d_sems[0:2], d_sems[2:4], d_sems[4:6])
        amounts = SmallSum(place, c_near, c_far, c_total, c_sems[0:2], c_sems[2:4])
        mid_rows = [pl.ds(i * hops * width // mid_parts, hops * width // mid_parts) for i in range(mid_parts)]
        mids = [
            GradSum(place, part_mid.at[rows], total_mid.at[rows], stages_mid[i], mid_sems[i], MID_ORDERS)
            for i, rows in enumerate(mid_rows)
        ]
        if early:
            gram_rows = [pl.ds(m * hops * LANES, hops * LANES) for m in range(batches)]
            grams = [
                GradSum(place, part_mid.at[rows], part_mid.at[rows], stages_gram[m], gram_sems[m], REST_ORDERS)
                for m, rows in enumerate(gram_rows)
            ]
            owned = (place.core * place.wide * place.low + place.axis("plane")[0]) * place.high + place.hi
            owned_hop = lax.div(owned, bands)

        def mid_step(i, stage):
            if i < mid_parts:
                mids[i].advance(stage)
        rests = GradSum(place, part_rest, total_rest, stages_rest, rest_sems, REST_ORDERS)

        def loop(first, last, body):
            def step(m, carry):
                body(m)
                return carry

            lax.fori_loop(first, last, step, 0)

        def at(m, when, body):
            pl.when(m == when)(body)

        spread[spread_rows:] = jnp.zeros((spread.shape[0] - spread_rows, LANES), F32)

        def hop_rows(k):
            parts = [spread[pl.ds(j * hops + k, HOT, stride=pieces * hops)] for j in range(pieces)]
            return jnp.concatenate(parts, axis=1)

        w_copy.wait()
        spread[:spread_rows] = landing(total_mid, 0)[...].astype(F32)
        for k in range(hops):
            w_ref[k] = jnp.concatenate([hop_rows(k), jnp.zeros((LANES - HOT, width), F32)], axis=0).astype(BF16)
            w_shift_ref[k] = w_ref[k]
            for g in range(groups):
                gain_rep[k * groups + g : k * groups + g + 1] = gain_ref[k : k + 1]
                shift_rep[k * groups + g : k * groups + g + 1] = shift_ref[k : k + 1]
        w_out_ref[...] = jnp.zeros_like(w_out_ref)
        w_out_ref[:classes] = w_out_in[...]
        bias_ref[...] = jnp.full(bias_ref.shape, -1e30, F32)
        bias_ref[0:1, :classes] = bias_in[...]
        bias_row = jnp.broadcast_to(bias_ref[0:1], (LANES, LANES))
        bias_ref[...] = jnp.transpose(bias_row)[: bias_ref.shape[0]]
        grad_hops_ref[...] = jnp.zeros_like(grad_hops_ref)
        grad_out_ref[...] = jnp.zeros_like(grad_out_ref)
        slopes_ref[...] = jnp.zeros_like(slopes_ref)

        def hot_rows(m):
            ids = lax.rem(lax.broadcasted_iota(jnp.int32, (LANES - HOT, nodes), 0), 8)
            return (ids == bucket_ref[m]).astype(F32)

        def active_row(m, k):
            if k == 0:
                return jnp.ones((1, nodes), F32)
            return mask_ref[k - 1, pl.ds(m, 1)].astype(F32)

        which = lax.broadcasted_iota(jnp.int32, (groups, LANES), 1)
        amount = [jnp.zeros((groups, LANES), F32) for _ in range(hops)]
        for m in range(batches):
            hot = hot_rows(m)
            for k in range(hops):
                here = jnp.sum(hot * active_row(m, k), axis=1, keepdims=True)
                amount[k] = jnp.where(which == m, here[:groups], amount[k])
        for k in range(hops):
            c_near[0, place.near, k * groups : (k + 1) * groups] = amount[k]

        def by_node(row):
            return jnp.transpose(jnp.broadcast_to(row, (LANES, nodes)))

        def moments(m):
            x_copy(m).wait()
            spread[:spread_rows] = landing(part_mid, m)[...].astype(F32)
            hot_all = hot_rows(m)
            cat_ref[m] = by_node(bucket_ref[m].astype(F32)).astype(BF16)
            for k in range(hops):
                block = jnp.concatenate([hop_rows(k), hot_all], axis=0) * active_row(m, k)
                xt = block.astype(BF16)
                hot = xt[HOT:]
                xt_ref[m, k] = xt
                pre = dot(xt, w_ref[k], TN)
                square = (pre * pre).astype(BF16)
                second = dot(hot, square)
                sums = jnp.concatenate(split_high(dot(hot, xt, NT)), axis=1)
                first = dot(sums, jnp.concatenate([w_ref[k], w_ref[k]], axis=0))
                for j in range(pieces):
                    base = 2 * tables * j + k * groups
                    table[m, base : base + groups] = first[:groups, lane[j]]
                    table[m, base + tables : base + tables + groups] = second[:groups, lane[j]]

        def moments_step(m):
            moments(m)

            @pl.when(m == 0)
            def _():
                pl.semaphore_wait(barrier, place.nears + place.fars - 2)
                amounts.start(0)

            stats.start(m)
            at(m, 2, lambda: amounts.forward(0))
            pl.when(m >= 2)(lambda: stats.forward(m - 2))

        loop(0, batches, moments_step)

        def gram(m):
            for k in range(hops):
                xt = xt_ref[m, k]
                masked = [xt * xt[HOT + g : HOT + g + 1] for g in range(groups)]
                here = dot(jnp.concatenate(masked, axis=0), xt, NT)
                by_bucket = [here[g * LANES : g * LANES + HOT] for g in range(groups)]
                block = jnp.concatenate(by_bucket, axis=1)
                block = jnp.concatenate([block, jnp.zeros((LANES - HOT, width), F32)], axis=0)
                start = pl.multiple_of((m * hops + k) * LANES, LANES)
                part_mid[pl.ds(start, LANES)] = block.astype(BF16)

        def end_gram(m):
            grams[m].end_down(2)
            rows = pl.multiple_of(m * hops * LANES + owned * 16, 16)
            gram_own[m * 16 : (m + 1) * 16] = part_mid[pl.ds(rows, 16)]

        def gram_step(m):
            if early:
                gram(m)
                for i in range(batches):
                    at(m, i, lambda i=i: grams[i].start_down(0))

            @pl.when(m == 0)
            def _():
                stats.forward(final - 1)
                stats.back(0)

            @pl.when(m == 1)
            def _():
                stats.forward(final)
                stats.back(1)

        loop(0, batches, gram_step)
        if early:
            grams[0].advance(0)
        amounts.finish(0)
        w_mid_copy.wait()
        stats.back(final - 1)
        stats.finish(0)

        def counts_of(m):
            here = lax.broadcasted_iota(jnp.int32, (tables, LANES), 1) == m
            counts = jnp.sum(jnp.where(here, c_total[0], 0.0), axis=1, keepdims=True)
            return jnp.broadcast_to(counts, (tables, LANES))

        def bucket_tables(m):
            counts = counts_of(m)
            for j in range(pieces):
                base = 2 * tables * j
                mean = t_total[m, base : base + tables] / counts
                second = t_total[m, base + tables : base + 2 * tables] / counts
                inv = lax.rsqrt(second - mean * mean + EPSILON)
                a = 0.5 * gain_rep[:, lane[j]] * inv
                tab_a[m, :, lane[j]] = a
                tab_b[m, :, lane[j]] = 0.5 * shift_rep[:, lane[j]] - a * mean
                high, low = split_high(0.5 * shift_rep[:, lane[j]] / a - mean)
                for k in range(hops):
                    rows = slice(k * groups, (k + 1) * groups)
                    parts = []
                    for part in (high, low):
                        parts.append(part[rows].astype(F32))
                        if groups < 8:
                            parts.append(jnp.zeros((8 - groups, LANES), F32))
                    w_shift_ref[k, HOT:, lane[j]] = jnp.concatenate(parts, axis=0).astype(BF16)

        def choose(masks, values, k, j):
            result = values[k * groups + groups - 1 : k * groups + groups, lane[j]]
            for g in range(groups - 2, -1, -1):
                result = jnp.where(masks[g], values[k * groups + g : k * groups + g + 1, lane[j]], result)
            return result

        def masks_of(m, rows):
            cat = cat_ref[m, rows].astype(F32)
            return [cat == float(g) for g in range(groups - 1)]

        projected = [dshaped_ref.at[final], dshaped_ref.at[final - 1]]

        halves = [slice(0, nodes // 2), slice(nodes // 2, nodes)]
        chunks = [slice(i * chunk, (i + 1) * chunk) for i in range(nodes // chunk)]

        def put_beside(beside, i):
            for n, body in enumerate(beside):
                if i == n * len(chunks) // len(beside):
                    body()

        def forward(m):
            bucket_tables(m)

            def projection(k, rows):
                projected[k % 2][rows] = dot(xt_ref[m, k, :, rows], w_shift_ref[k], TN)

            def product(k, rows):
                middle = dot(join_ref[m, rows, columns[k]], w_mid_ref[columns[k]])
                mid_ref[m, rows] = middle if k == 0 else mid_ref[m, rows] + middle

            for rows in halves:
                projection(0, rows)
            for k in range(hops):
                beside = [functools.partial(projection, k + 1, rows) for rows in halves] if k + 1 < hops else []
                beside += [functools.partial(product, k - 1, rows) for rows in halves] if k else []
                for i, rows in enumerate(chunks):
                    put_beside(beside, i)
                    masks = masks_of(m, rows)
                    for j in range(pieces):
                        bend = 0.5 - 0.5 * slope_ref[k : k + 1, lane[j]]
                        bend_cat = 0.5 - 0.5 * slope_cat_ref[:, k * width + j * LANES : k * width + (j + 1) * LANES]
                        scale = choose(masks, tab_a.at[m], k, j)
                        u = projected[k % 2][rows, lane[j]] * scale
                        u_ref[m, k, rows, lane[j]] = u
                        half = u - (bend * u) * (1.0 - jnp.tanh(u))
                        half = half - (bend_cat * half) * (1.0 - jnp.tanh(half))
                        join_ref[m, rows, k * width + j * LANES : k * width + (j + 1) * LANES] = half.astype(BF16)
            for rows in halves:
                product(hops - 1, rows)
            middle = mid_ref[m]
            first = jnp.sum(middle, axis=0, keepdims=True)
            second = jnp.sum(middle * middle, axis=0, keepdims=True)
            own = heads.own(m)
            for j in range(pieces):
                own[j : j + 1] = first[:, lane[j]]
                own[pieces + j : pieces + j + 1] = second[:, lane[j]]

        def row_of(ref, m, first):
            return jnp.concatenate([ref[m, first + j : first + j + 1] for j in range(pieces)], axis=1)

        def head_scale(m):
            mean = row_of(s_total, m, 0) * (1.0 / nodes_batch)
            second = row_of(s_total, m, pieces) * (1.0 / nodes_batch)
            inv = lax.rsqrt(4.0 * (second - mean * mean) + EPSILON)
            return mean, inv

        def head(m):
            heads.finish(m)
            mean, inv = head_scale(m)
            scale = gain_mid_ref[...] * inv
            offset = 0.5 * shift_mid_ref[...] - scale * mean
            slope = slope_mid_ref[...]
            u = mid_ref[m] * scale + offset
            mid_ref[m] = u
            tanh = jnp.tanh(u)
            gap = u * (1.0 - tanh)
            outer = (2.0 * u - (1.0 - slope) * gap).astype(BF16)
            logits = dot(w_out_ref[...], outer, NT) + bias_ref[:, 0:1]
            top = jnp.max(logits, axis=0, keepdims=True)
            powers = jnp.exp(logits - top)
            total = jnp.sum(powers, axis=0, keepdims=True)
            wanted = (lax.broadcasted_iota(jnp.int32, logits.shape, 0) == labels_ref[pl.ds(m, 1)]).astype(F32)
            loss = jnp.log(total) + top - jnp.sum(logits * wanted, axis=0, keepdims=True)
            dlogits = (powers / total - wanted) * (1.0 / total_nodes)
            low = dlogits.astype(BF16)
            grad_out_ref[...] += dot(low, outer)
            douter = dot(low, w_out_ref[...], TN)
            grad_slope = jnp.sum(douter * gap, axis=0, keepdims=True)
            dshaped = douter * (slope + (0.5 - 0.5 * slope) * (1.0 + tanh) * (1.0 + gap))
            dshaped_ref[m] = dshaped
            head_sum = jnp.sum(dshaped, axis=0, keepdims=True)
            head_dot = jnp.sum(dshaped * u, axis=0, keepdims=True)
            own = backs.own(m)
            for j in range(pieces):
                own[j : j + 1] = head_sum[:, lane[j]]
                own[pieces + j : pieces + j + 1] = head_dot[:, lane[j]]
                own[2 * pieces + j : 2 * pieces + j + 1] = grad_slope[:, lane[j]]
            folded = sum(dlogits[:, i * LANES : (i + 1) * LANES] for i in range(nodes // LANES))
            square = jnp.concatenate([folded, jnp.zeros((LANES - folded.shape[0], LANES), F32)], axis=0)
            own[3 * pieces : 3 * pieces + 1] = jnp.sum(jnp.transpose(square), axis=0, keepdims=True)
            own[3 * pieces + 1 : 3 * pieces + 2] = sum(
                loss[:, i * LANES : (i + 1) * LANES] for i in range(nodes // LANES)
            )
            own[3 * pieces + 2 :] = jnp.zeros((own.shape[0] - 3 * pieces - 2, LANES), F32)
            backs.start(m)

        def head_grads(m):
            inv = head_scale(m)[1]
            head_sum = row_of(e_total, m, 0)
            head_dot = (2.0 * row_of(e_total, m, pieces) - shift_mid_ref[...] * head_sum) / gain_mid_ref[...]
            return inv, head_sum, head_dot

        def back_head(m):
            backs.finish(m)
            inv, head_sum, head_dot = head_grads(m)
            scale = gain_mid_ref[...] * inv
            tilt = 2.0 * inv * head_dot * (1.0 / nodes_batch)
            level = scale * head_sum * (1.0 / nodes_batch) - 0.5 * shift_mid_ref[...] * tilt
            dmid_ref[m] = (scale * dshaped_ref[m] - level - mid_ref[m] * tilt).astype(BF16)

        gradients = [mid_ref.at[0], dshaped_ref.at[0]]

        def products(k):
            return (part_rest, total_rest)[k % 2].at[pl.ds(0, nodes)]

        def backward(m, which_hops, target, tick):
            def into(k, rows):
                gradients[k % 2][rows] = dot(dmid_ref[m, rows], w_mid_ref[columns[k]], NT)

            def bucket_sums(k):
                first_sums(k)
                second_sums(k)

            def first_sums(k):
                hot = xt_ref[m, k, HOT:LANES]
                if early:
                    both = dot(xt_ref[m, k], target(k)[...])
                    grad_hops_ref[k, :HOT] += 2.0 * both[:HOT]
                    first = both[HOT:]
                else:
                    first = dot(hot, target(k)[...])
                for j in range(pieces):
                    base = 2 * tables * j + k * groups
                    table[m, base : base + groups] = first[:groups, lane[j]]

            def second_sums(k):
                second = dot(xt_ref[m, k, HOT:LANES], products(k)[...])
                for j in range(pieces):
                    base = 2 * tables * j + k * groups
                    table[m, base + tables : base + tables + groups] = second[:groups, lane[j]]

            for rows in halves:
                into(which_hops[0], rows)
            for k in which_hops:
                beside = [functools.partial(into, k + 1, rows) for rows in halves] if k + 1 in which_hops else []
                beside += [functools.partial(f, k - 1) for f in (first_sums, second_sums)] if k - 1 in which_hops else []
                slope_sums = [jnp.zeros((8, LANES), F32) for _ in range(2 * pieces)]
                result = target(k)
                for i, rows in enumerate(chunks):
                    put_beside(beside, i)
                    masks = masks_of(m, rows)
                    for j in range(pieces):
                        slope = slope_ref[k : k + 1, lane[j]]
                        slope_cat = slope_cat_ref[:, k * width + j * LANES : k * width + (j + 1) * LANES]
                        bend, bend_cat = 0.5 - 0.5 * slope, 0.5 - 0.5 * slope_cat
                        u = u_ref[m, k, rows, lane[j]]
                        tanh = jnp.tanh(u)
                        gap = (bend * u) * (1.0 - tanh)
                        half = u - gap
                        tanh_cat = jnp.tanh(half)
                        gap_cat = (bend_cat * half) * (1.0 - tanh_cat)
                        grad = gradients[k % 2][rows, lane[j]]
                        slope_sums[pieces + j] += jnp.sum((grad * gap_cat).reshape(-1, 8, LANES), axis=0)
                        grad = grad * (slope_cat + (1.0 + tanh_cat) * (bend_cat + gap_cat))
                        slope_sums[j] += jnp.sum((grad * gap).reshape(-1, 8, LANES), axis=0)
                        grad = grad * (slope + (1.0 + tanh) * (bend + gap))
                        grad = grad * choose(masks, tab_a.at[m], k, j)
                        result[rows, lane[j]] = grad.astype(BF16)
                        products(k)[rows, lane[j]] = (grad * u).astype(BF16)
                for j in range(pieces):
                    slope = slope_ref[k : k + 1, lane[j]]
                    slope_cat = slope_cat_ref[:, k * width + j * LANES : k * width + (j + 1) * LANES]
                    for s, values in enumerate((slope, slope_cat)):
                        grad_hops_ref[k, feats + s : feats + s + 1, lane[j]] += jnp.sum(
                            slope_sums[s * pieces + j], axis=0, keepdims=True
                        ) / (0.5 - 0.5 * values)
                if k == which_hops[-1]:
                    bucket_sums(k)
                tick(k)

        def first_target(k):
            return total_mid.at[pl.ds(k * nodes, nodes)]

        def first_copy(k):
            return pltpu.make_async_copy(first_target(k), join_ref.at[0, :, pl.ds(k * width, width)], in_sems.at[k])

        def no_tick(k):
            pass

        def forward_step(m):
            pl.when(m >= 1)(lambda: stats.finish(m))
            forward(m)
            heads.start(m)
            pl.when(m >= 1)(lambda: heads.forward(m - 1))
            at(m, 0, lambda: stats.back(final))
            if early:
                at(m, 2, lambda: end_gram(0))
                for i in range(1, final + 1):
                    at(m, i, lambda i=i: grams[i - 1].advance(1))
                    at(m, i - 1, lambda i=i: grams[i].advance(0))
            at(m, 2, lambda: head(0))

        loop(0, batches, forward_step)
        backs.forward(0)

        def head_step(m):
            head(m)

            @pl.when(m == 1)
            def _():
                heads.forward(final)
                if early:
                    end_gram(1)

            @pl.when(m == 2)
            def _():
                backs.forward(1)
                back_head(0)
                backward(0, [0, 1], first_target, no_tick)
                if early:
                    grams[final].advance(1)
                    end_gram(2)

        loop(1, batches, head_step)
        backs.forward(2)
        if early:
            end_gram(final)

        def late_tick(k):
            if k == hops - 1:
                backs.forward(final)

        backward(0, list(range(2, hops)), first_target, late_tick)
        dots.start(0)
        for m in range(1, final):
            back_head(m)

        held = [mid_ref.at[m] for m in range(final)] + [dshaped_ref.at[0]]
        for k in range(hops):
            held[k][...] = sum(dot(join_ref[m, :, columns[k]], dmid_ref[m], TN) for m in range(final))
        back_head(final)
        for k in range(hops):
            total = held[k][...] + dot(join_ref[final, :, columns[k]], dmid_ref[final], TN)
            part_mid[columns[k]] = (2.0 * total).astype(BF16)
            if (k + 1) * mid_parts % hops == 0:
                mids[(k + 1) * mid_parts // hops - 1].start_down(0)
        for k in range(hops):
            first_copy(k).start()
        dots.forward(0)

        def wait_first():
            for k in range(hops):
                first_copy(k).wait()

        ticks = {
            (1, 0): [wait_first],
            (1, 1): [lambda: mid_step(0, 0)],
            (1, 2): [lambda: mid_step(1, 0), lambda: dots.back(0)],
            (2, 0): [lambda: mid_step(0, 1)],
            (2, 1): [lambda: mid_step(1, 1)],
            (2, 2): [lambda: dots.forward(1)],
            (2, 3): [lambda: mid_step(0, 2)],
            (3, 0): [lambda: mid_step(1, 2)],
            (3, 1): [lambda: dots.back(1)],
            (3, 2): [lambda: dots.forward(2)],
            (3, 3): [lambda: mid_step(0, 3)],
        }

        def backward_step(m):
            def tick(k):
                for when, bodies in ticks.items():
                    if when[1] == k:
                        for body in bodies:
                            at(m, when[0], body)

            backward(m, list(range(hops)), lambda k: join_ref.at[m, :, columns[k]], tick)
            dots.start(m)

        loop(1, batches, backward_step)

        def last_tables(m):
            counts = counts_of(m)
            for j in range(pieces):
                base = 2 * tables * j
                a = tab_a[m, :, lane[j]]
                inv = 2.0 * a / gain_rep[:, lane[j]]
                shift = shift_rep[:, lane[j]]
                scaled = t_total[m, base : base + tables]
                bucket_sum = scaled / a
                bucket_dot = (2.0 * t_total[m, base + tables : base + 2 * tables] / a - shift * bucket_sum) / gain_rep[
                    :, lane[j]
                ]
                tilt = inv * bucket_dot / counts
                tab_f[:, lane[j]] = tilt
                tab_e[:, lane[j]] = scaled / counts - 0.5 * shift * tilt
                for k in range(hops):
                    here = slice(k * groups, (k + 1) * groups)
                    slopes_ref[k : k + 1, lane[j]] += jnp.sum(bucket_dot[here], axis=0, keepdims=True)
                    slopes_ref[hops + k : hops + k + 1, lane[j]] += jnp.sum(bucket_sum[here], axis=0, keepdims=True)

        def own_tables(m):
            for k in range(hops):
                rows = slice(k * groups, (k + 1) * groups)

                @pl.when(owned_hop == k)
                def _(rows=rows):
                    tilt = tab_f[rows]
                    scale_own[m] = tilt * tab_a[m, rows]
                    level_own[m] = tab_e[rows] + tilt * tab_b[m, rows]

        def last(m):
            dots.finish(m)
            last_tables(m)
            if early:
                own_tables(m)
                at(m, final, lambda: rests.advance(2, correction()))

            def weights(k):
                grad_hops_ref[k, :HOT] += dot(xt_ref[m, k, :HOT], join_ref[m, :, columns[k]]) * 2.0

            for k in range(hops):
                if k and not early:
                    weights(k - 1)
                for rows in chunks:
                    masks = masks_of(m, rows)
                    for j in range(pieces):
                        here = slice(k * width + j * LANES, k * width + (j + 1) * LANES)
                        grad = join_ref[m, rows, here].astype(F32) - choose(masks, tab_e, k, j)
                        grad = grad - choose(masks, tab_f, k, j) * u_ref[m, k, rows, lane[j]]
                        join_ref[m, rows, here] = grad.astype(BF16)
            if not early:
                weights(hops - 1)

        def correction():
            total = jnp.zeros((16, width), F32)
            weights = w_ref[owned_hop].astype(F32)
            row = lax.broadcasted_iota(jnp.int32, (LANES, width), 0)
            for m in range(batches):
                scaled = [
                    jnp.where(row == HOT + g, level_own[m, g : g + 1], weights * scale_own[m, g : g + 1]).astype(BF16)
                    for g in range(groups)
                ]
                total = total + dot(gram_own[m * 16 : (m + 1) * 16], jnp.concatenate(scaled, axis=0))
            return 2.0 * total

        def features_copy(m):
            return pltpu.make_async_copy(spread.at[pl.ds(0, spread_rows)], out_features.at[m], out_sems.at[m])

        def features(m):
            pl.when(m >= 1)(lambda: features_copy(m - 1).wait())
            for k in range(hops):
                scale = active_row(m, k) * float(2 * total_nodes)
                values = dot(w_ref[k], join_ref[m, :, columns[k]], NT) * scale
                for j in range(pieces):
                    spread[pl.ds(j * hops + k, feats, stride=pieces * hops)] = values[:feats, lane[j]]
            features_copy(m).start()

        def start_rests():
            rows = grad_out_ref.shape[0] // hops
            for k in range(hops):
                grad_hops_ref[k, SPARE : SPARE + rows] = grad_out_ref[k * rows : (k + 1) * rows]
                part_rest[k * LANES : (k + 1) * LANES] = grad_hops_ref[k].astype(BF16)
            if part_rest.shape[0] > hops * LANES:
                part_rest[hops * LANES :] = jnp.zeros((part_rest.shape[0] - hops * LANES, width), BF16)
            rests.start_down(0)

        def last_step(m):
            last(m)

            @pl.when(m == 0)
            def _():
                if early:
                    rests.advance(0)
                dots.back(2)
                mid_step(1, 3)

            at(m, 1, lambda: mid_step(0, 4))
            at(m, 2, lambda: mid_step(0, 5))

            @pl.when(m == 3)
            def _():
                if not early:
                    start_rests()

            features(m)
            at(m, 0, lambda: dots.forward(final))

            @pl.when(m == 1)
            def _():
                dots.back(final)
                if early:
                    rests.advance(1)
                mid_step(1, 4)

            at(m, 2, lambda: mid_step(1, 5))
            at(m, 3, lambda: mid_step(0, 6))

        if early:
            start_rests()
        loop(0, batches, last_step)
        if not early:
            for stage in range(3):
                rests.advance(stage)

        grad_gain = jnp.zeros((1, width), F32)
        grad_shift = jnp.zeros((1, width), F32)
        grad_slope = jnp.zeros((1, width), F32)
        bias_loss = jnp.zeros((2, LANES), F32)
        for m in range(batches):
            _, head_sum, head_dot = head_grads(m)
            grad_gain = grad_gain + head_dot
            grad_shift = grad_shift + head_sum
            grad_slope = grad_slope + row_of(e_total, m, 2 * pieces)
            bias_loss = bias_loss + e_total[m, 3 * pieces : 3 * pieces + 2]
        out_small[: 2 * hops] = slopes_ref[...]
        loss = jnp.sum(bias_loss[1:2], axis=1, keepdims=True) * (1.0 / total_nodes)
        last_row = [bias_loss[0:1], jnp.broadcast_to(loss, (1, LANES)), jnp.zeros((1, width - 2 * LANES), F32)]
        for i, row in enumerate((grad_gain, grad_shift, grad_slope, jnp.concatenate(last_row, axis=1))):
            out_small[2 * hops + i : 2 * hops + i + 1] = row

        rests.advance(3)
        mid_step(1, 6)
        mid_step(0, 7)
        rests.advance(4)
        mid_step(1, 7)
        mid_file = pltpu.make_async_copy(total_mid, out_mid, file_sems.at[0])
        mid_file.start()
        rests.advance(5)
        rest_file = pltpu.make_async_copy(total_rest.at[pl.ds(0, hops * LANES)], out_rest, file_sems.at[1])
        rest_file.start()
        features_copy(final).wait()
        mid_file.wait()
        rest_file.wait()

    return kernel


def make_finish(dims):
    (groups, dps, batches, nodes, hops, feats, width, classes) = dims
    pieces = width // LANES
    spare = -(-classes // 16) * 16 // hops

    def kernel(
        features_in, mid_in, rest_in, small_in,
        features, mid, hops_grad, gain, shift, slope, cat, gain_mid, shift_mid, slope_mid, out_grad, bias, loss,
        low, wide, held, rest, spread, sems,
    ):
        rest_copy = pltpu.make_async_copy(rest_in, rest, sems.at[4, 0])
        spread_copy = pltpu.make_async_copy(spread, hops_grad, sems.at[4, 1])
        in_copy = [pltpu.make_async_copy(features_in.at[m], held.at[m], sems.at[0, m]) for m in range(batches)]
        out_copy = [pltpu.make_async_copy(held.at[m], features.at[m], sems.at[3, m]) for m in range(batches)]
        low_copy = [pltpu.make_async_copy(mid_in.at[pl.ds(k * width, width)], low.at[k], sems.at[1, k]) for k in range(hops)]
        wide_copy = [pltpu.make_async_copy(wide.at[k], mid.at[pl.ds(k * width, width)], sems.at[2, k]) for k in range(hops)]
        for copy in [rest_copy] + [c for pair in zip(in_copy, low_copy) for c in pair]:
            copy.start()
        rest_copy.wait()
        for k in range(hops):
            values = rest[k * LANES : (k + 1) * LANES].astype(F32)
            for j in range(pieces):
                spread[pl.ds(j * hops + k, feats, stride=pieces * hops)] = values[:feats, j * LANES : (j + 1) * LANES]
            slope[k : k + 1] = values[feats : feats + 1]
            cat[:, k * width : (k + 1) * width] = values[feats + 1 : feats + 2]
            count = min(spare, classes - k * spare)
            out_grad[k * spare : k * spare + count] = values[SPARE : SPARE + count]
        spread_copy.start()
        gain[...] = small_in[:hops]
        shift[...] = small_in[hops : 2 * hops]
        gain_mid[...] = small_in[2 * hops : 2 * hops + 1]
        shift_mid[...] = small_in[2 * hops + 1 : 2 * hops + 2]
        slope_mid[...] = small_in[2 * hops + 2 : 2 * hops + 3]
        bias[...] = small_in[2 * hops + 3 : 2 * hops + 4, :classes]
        loss[...] = small_in[2 * hops + 3 : 2 * hops + 4, LANES : LANES + 1]
        for i in range(max(batches, hops)):
            if i < batches:
                in_copy[i].wait()
                out_copy[i].start()
            if i < hops:
                low_copy[i].wait()
                wide[i] = low[i].astype(F32)
                wide_copy[i].start()
        for copy in wide_copy + out_copy + [spread_copy]:
            copy.wait()

    return kernel


def by_piece(values):
    *lead, feats, hops, width = values.shape
    values = jnp.swapaxes(values.reshape(*lead, feats, hops, width // LANES, LANES), -3, -2)
    return values.reshape(*lead, feats * hops * width // LANES, LANES)


def by_hop(rows, hops, pieces):
    *lead, count, _ = rows.shape
    values = rows.reshape(*lead, count // (hops * pieces), pieces, hops, LANES)
    return jnp.swapaxes(values, -3, -2).reshape(*lead, count // (hops * pieces), hops, pieces * LANES)


def shards(
    features,
    buckets,
    hop_mask,
    labels,
    w_hops,
    gain_hops,
    shift_hops,
    slope_hops,
    slope_cat,
    w_mid,
    gain_mid,
    shift_mid,
    slope_mid,
    w_out,
    bias_out,
):
    batches, nodes, hops, feats = features.shape
    width, classes = w_out.shape
    groups, dps = lax.axis_size("bucket"), lax.axis_size("dp")
    dims = (groups, dps, batches, nodes, hops, feats, width, classes)
    pieces = width // LANES
    joined_width = hops * width
    tables = hops * groups
    padded = -(-classes // 16) * 16

    wide, low, high = groups // 2, dps // 4, 4
    sizes = {"wide": wide, "low": low, "high": high, "plane": wide * low}
    rows_rest = max(hops * LANES, 2 * wide * low * 16)
    early, mid_parts = plan(groups, dps, hops, width)
    mid_shapes = GradSum.stage_shapes(joined_width // mid_parts, width, MID_ORDERS, sizes)
    gram_count = batches if early else 0
    own_rows = 16 * batches if early else 16
    rest_shapes = GradSum.stage_shapes(rows_rest, width, REST_ORDERS, sizes)
    _, nears, fars = Place.group_sizes(groups, dps)
    table_rows = 2 * tables * pieces
    share = table_rows // nears
    sem = pltpu.SemaphoreType.DMA

    def small_scratch(rows, copies=batches):
        return [
            pltpu.VMEM((copies, nears, rows, LANES), F32),
            pltpu.VMEM((copies, fars, rows, LANES), F32),
            pltpu.VMEM((copies, rows, LANES), F32),
        ]

    vmem = pl.BlockSpec(memory_space=pltpu.VMEM)
    hbm = pl.BlockSpec(memory_space=pl.ANY)

    def real(*shape):
        return jax.ShapeDtypeStruct(shape, F32)

    outs = pl.pallas_call(
        make_kernel(dims),
        name="train_step",
        out_shape=(
            real(batches, feats * pieces * hops, LANES),
            jax.ShapeDtypeStruct((joined_width, width), BF16),
            jax.ShapeDtypeStruct((hops * LANES, width), BF16),
            real(2 * hops + 4, width),
        ),
        in_specs=[hbm] + [vmem] * 3 + [hbm] + [vmem] * 4 + [hbm] + [vmem] * 5,
        out_specs=(hbm, hbm, hbm, vmem),
        scratch_shapes=[
            pltpu.VMEM((HOT * pieces * hops, LANES), F32),
            pltpu.VMEM((batches, hops, nodes, width), F32),
            pltpu.VMEM((batches, nodes, joined_width), BF16),
            pltpu.VMEM((batches, hops, LANES, nodes), BF16),
            pltpu.VMEM((batches, nodes, LANES), BF16),
            pltpu.VMEM((hops, LANES, width), BF16),
            pltpu.VMEM((batches, nodes, width), F32),
            pltpu.VMEM((batches, nodes, width), F32),
            pltpu.VMEM((batches, nodes, width), BF16),
            pltpu.VMEM((hops, LANES, width), F32),
            pltpu.VMEM((padded, width), F32),
            pltpu.VMEM((hops, LANES, width), BF16),
            pltpu.VMEM((joined_width, width), BF16),
            pltpu.VMEM((padded, width), BF16),
            pltpu.VMEM((padded, LANES), F32),
            pltpu.VMEM((tables, width), F32),
            pltpu.VMEM((tables, width), F32),
        ]
        + [pltpu.VMEM((batches, tables, width), F32) for _ in range(2)]
        + [pltpu.VMEM((tables, width), F32) for _ in range(2)]
        + [pltpu.VMEM((2 * hops, width), F32)]
        + [pltpu.VMEM((batches, table_rows, LANES), F32)]
        + [pltpu.VMEM((batches, nears, share, LANES), F32), pltpu.VMEM((batches, fars, share, LANES), F32)]
        + [pltpu.VMEM((batches, table_rows, LANES), F32)]
        + small_scratch(8)
        + small_scratch(16)
        + small_scratch(tables, 1)
        + [
            pltpu.VMEM((joined_width, width), BF16),
            pltpu.VMEM((joined_width, width), BF16),
            pltpu.VMEM((rows_rest, width), BF16),
            pltpu.VMEM((rows_rest, width), BF16),
            [[pltpu.VMEM(s, BF16) for s in mid_shapes] for _ in range(mid_parts)],
            [pltpu.VMEM(s, BF16) for s in rest_shapes],
            pltpu.VMEM((own_rows, width), BF16),
            pltpu.VMEM((batches, groups, width), F32),
            pltpu.VMEM((batches, groups, width), F32),
            [[pltpu.VMEM(s, BF16) for s in rest_shapes] for _ in range(gram_count)],
            [sem((batches,)) for _ in range(6)],
            [sem((batches,)) for _ in range(4)],
            [sem((batches,)) for _ in range(4)],
            [sem((1,)) for _ in range(4)],
            [sem((batches,)) for _ in range(6)],
            [[sem((len(mid_shapes),)) for _ in range(4)] for _ in range(mid_parts)],
            [sem((len(rest_shapes),)) for _ in range(4)],
            [[sem((len(rest_shapes),)) for _ in range(4)] for _ in range(gram_count)],
            sem((max(batches, hops),)),
            sem((batches,)),
            sem((3,)),
        ],
        compiler_params=pltpu.CompilerParams(
            collective_id=0, has_side_effects=True, vmem_limit_bytes=int(63.9 * 2**20)
        ),
    )(
        by_piece(jnp.transpose(features, (0, 3, 2, 1))),
        jnp.transpose(buckets, (0, 2, 1)),
        jnp.transpose(hop_mask, (2, 0, 1)),
        labels,
        by_piece(jnp.transpose(w_hops, (1, 0, 2))),
        gain_hops,
        shift_hops,
        slope_hops,
        slope_cat[None],
        w_mid,
        gain_mid[None],
        shift_mid[None],
        slope_mid[None],
        w_out.T,
        bias_out[None],
    )
    outs = pl.pallas_call(
        make_finish(dims),
        name="finish",
        out_shape=(
            real(batches, feats * pieces * hops, LANES),
            real(joined_width, width),
            real(feats * pieces * hops, LANES),
            real(hops, width),
            real(hops, width),
            real(hops, width),
            real(1, joined_width),
            real(1, width),
            real(1, width),
            real(1, width),
            real(classes, width),
            real(1, classes),
            real(1, 1),
        ),
        in_specs=[hbm, hbm, hbm, vmem],
        out_specs=(hbm, hbm, hbm) + (vmem,) * 10,
        scratch_shapes=[
            pltpu.VMEM((hops, width, width), BF16),
            pltpu.VMEM((hops, width, width), F32),
            pltpu.VMEM((batches, feats * pieces * hops, LANES), F32),
            pltpu.VMEM((hops * LANES, width), BF16),
            pltpu.VMEM((feats * pieces * hops, LANES), F32),
            sem((5, max(batches, hops))),
        ],
        compiler_params=pltpu.CompilerParams(vmem_limit_bytes=int(63.9 * 2**20)),
    )(*outs)
    (features_grad, mid_grad, hops_grad, gain, shift, slope, cat, gain_m, shift_m, slope_m, out_grad, bias, loss) = outs
    return (
        loss[0, 0],
        jnp.transpose(by_hop(features_grad, hops, nodes // LANES), (0, 3, 2, 1)),
        jnp.transpose(by_hop(hops_grad, hops, pieces), (1, 0, 2)),
        gain,
        shift,
        slope,
        cat[0],
        mid_grad,
        gain_m[0],
        shift_m[0],
        slope_m[0],
        out_grad.T,
        bias[0],
    )


def solution(mesh):
    nodes_split = ("bucket", "dp")
    placed = (
        P(None, nodes_split, None, None),
        P(None, nodes_split, None),
        P(None, nodes_split, None),
        P(None, nodes_split),
    ) + (P(),) * 11
    return jax.shard_map(
        shards,
        mesh=mesh,
        in_specs=placed,
        out_specs=(P(), P(None, nodes_split, None, None)) + (P(),) * 11,
        check_vma=False,
    )
```

```python
import functools

import jax
import jax.numpy as jnp
from jax import lax
from jax.experimental import pallas as pl
from jax.experimental.pallas import tpu as pltpu
from jax.sharding import PartitionSpec as P

F32 = jnp.float32
BF16 = jnp.bfloat16
EPSILON = 1e-05
MESH = pl.DeviceIdType.MESH
LANES = 128
HOT = 112
SPARE = 104
MID_ORDERS = (("wide", "low", "high"), ("low", "wide", "high"))
REST_ORDERS = (("plane", "high"),)
NN, NT, TN = ((1,), (0,)), ((1,), (1,)), ((0,), (0,))


def dot(left, right, dims=NN):
    return lax.dot_general(left, right, (dims, ((), ())), preferred_element_type=F32)


def split_high(values):
    high = values.astype(BF16)
    return high, (values - high.astype(F32)).astype(BF16)


class Place:
    def __init__(self, groups, dps):
        self.groups, self.dps = groups, dps
        self.high = 4
        self.low = dps // self.high
        self.wide = groups // 2
        self.b = lax.axis_index("bucket")
        self.d = lax.axis_index("dp")
        self.core = lax.rem(self.b, 2)
        self.x = lax.div(self.b, 2)
        self.lo = lax.rem(self.d, self.low)
        self.hi = lax.div(self.d, self.low)
        self.fold, self.nears, self.fars = self.group_sizes(groups, dps)
        self.near = self.b * self.fold + lax.rem(self.d, self.fold)
        self.far = lax.div(self.d, self.fold)

    @staticmethod
    def group_sizes(groups, dps):
        low = dps // 4
        fold = low if groups * low <= 8 else 1
        return fold, groups * fold, dps // fold

    def at(self, b=None, d=None):
        return {"bucket": self.b if b is None else b, "dp": self.d if d is None else d}

    def near_peer(self, o):
        i = lax.rem(self.near + o, self.nears)
        b, lo = lax.div(i, self.fold), lax.rem(i, self.fold)
        return i, self.at(b=b, d=lax.div(self.d, self.fold) * self.fold + lo)

    def far_peer(self, o):
        i = lax.rem(self.far + o, self.fars)
        return i, self.at(d=i * self.fold + lax.rem(self.d, self.fold))

    def axis(self, name):
        if name == "core":
            return self.core, 2, lambda o: (1 - self.core, self.at(b=2 * self.x + 1 - self.core))
        if name == "wide":
            def peer(o):
                i = lax.rem(self.x + o, self.wide)
                return i, self.at(b=2 * i + self.core)
            return self.x, self.wide, peer
        if name == "low":
            def peer(o):
                i = lax.rem(self.lo + o, self.low)
                return i, self.at(d=self.hi * self.low + i)
            return self.lo, self.low, peer

        if name == "plane":
            own = self.x * self.low + self.lo

            def peer(o):
                i = lax.rem(own + o, self.wide * self.low)
                b = 2 * lax.div(i, self.low) + self.core
                return i, self.at(b=b, d=self.hi * self.low + lax.rem(i, self.low))
            return own, self.wide * self.low, peer

        def peer(o):
            i = lax.rem(self.hi + o, self.high)
            return i, self.at(d=i * self.low + self.lo)
        return self.hi, self.high, peer


def remote(src, dst, sems, index, device):
    send, recv = sems
    return pltpu.make_async_remote_copy(
        src_ref=src,
        dst_ref=dst,
        send_sem=send.at[index],
        recv_sem=recv.at[index],
        device_id=device,
        device_id_type=MESH,
    )


def wait_all(copied, sems, index, device):
    remote(copied, copied, sems, index, device).wait()


class SmallSum:
    def __init__(self, place, near, far, total, near_sems, far_sems):
        self.place, self.near, self.far, self.total = place, near, far, total
        self.near_sems, self.far_sems = near_sems, far_sems

    def own(self, m):
        return self.near.at[m, self.place.near]

    def near_copies(self, m):
        mine = self.near.at[m, self.place.near]
        return [
            remote(mine, mine, self.near_sems, m, self.place.near_peer(o)[1])
            for o in range(1, self.place.nears)
        ]

    def far_copies(self, m):
        mine = self.far.at[m, self.place.far]
        return [
            remote(mine, mine, self.far_sems, m, self.place.far_peer(o)[1])
            for o in range(1, self.place.fars)
        ]

    def start(self, m):
        for copy in self.near_copies(m):
            copy.start()

    def forward(self, m):
        place = self.place
        wait_all(self.near.at[m, pl.ds(0, place.nears - 1)], self.near_sems, m, place.near_peer(1)[1])
        self.far[m, self.place.far] = sum(self.near[m, i] for i in range(self.place.nears))
        for copy in self.far_copies(m):
            copy.start()

    def finish(self, m):
        place = self.place
        wait_all(self.far.at[m, pl.ds(0, place.fars - 1)], self.far_sems, m, place.far_peer(1)[1])
        self.total[m] = sum(self.far[m, i] for i in range(self.place.fars))


class TableSum:
    def __init__(self, place, table, near, far, total, near_sems, far_sems, back_sems):
        self.place, self.table, self.near, self.far, self.total = place, table, near, far, total
        self.near_sems, self.far_sems, self.back_sems = near_sems, far_sems, back_sems
        self.rows = table.shape[1] // place.nears

    def share(self, i):
        return pl.ds(pl.multiple_of(i * self.rows, 8), self.rows)

    def near_copies(self, m):
        mine = self.near.at[m, self.place.near]
        copies = []
        for o in range(1, self.place.nears):
            i, device = self.place.near_peer(o)
            copies.append(remote(self.table.at[m, self.share(i)], mine, self.near_sems, m, device))
        return copies

    def far_copies(self, m):
        mine = self.far.at[m, self.place.far]
        return [
            remote(mine, mine, self.far_sems, m, self.place.far_peer(o)[1])
            for o in range(1, self.place.fars)
        ]

    def back_copies(self, m):
        mine = self.total.at[m, self.share(self.place.near)]
        return [
            remote(mine, mine, self.back_sems, m, self.place.near_peer(o)[1])
            for o in range(1, self.place.nears)
        ]

    def start(self, m):
        for copy in self.near_copies(m):
            copy.start()
        self.near[m, self.place.near] = self.table[m, self.share(self.place.near)]

    def forward(self, m):
        place = self.place
        wait_all(self.near.at[m, pl.ds(0, place.nears - 1)], self.near_sems, m, place.near_peer(1)[1])
        self.far[m, self.place.far] = sum(self.near[m, i] for i in range(self.place.nears))
        for copy in self.far_copies(m):
            copy.start()

    def back(self, m):
        place = self.place
        wait_all(self.far.at[m, pl.ds(0, place.fars - 1)], self.far_sems, m, place.far_peer(1)[1])
        self.total[m, self.share(self.place.near)] = sum(self.far[m, i] for i in range(self.place.fars))
        for copy in self.back_copies(m):
            copy.start()

    def finish(self, m):
        place = self.place
        rows = self.total.at[m, pl.ds(0, (place.nears - 1) * self.rows)]
        wait_all(rows, self.back_sems, m, place.near_peer(1)[1])


class GradSum:
    def __init__(self, place, part, total, stages, sems, orders):
        self.part, self.total, self.stages, self.sems = part, total, stages, sems
        half = part.shape[0] // 2
        core = place.axis("core")
        self.steps = [[(core, 0, half, 0)]] + [[] for _ in orders[0]]
        slot = 1
        for h, order in enumerate(orders):
            size = half // len(orders)
            start = core[0] * half + h * size
            for i, name in enumerate(order):
                axis = place.axis(name)
                self.shared = i == len(order) - 1 and size % (16 * axis[1]) != 0
                if not self.shared:
                    size = size // axis[1]
                self.steps[i + 1].append((axis, start, size, slot))
                start = start + axis[0] * size
                slot += 1

    @staticmethod
    def stage_shapes(rows, columns, orders, sizes):
        shapes = [(1, rows // 2, columns)]
        for order in orders:
            size = rows // 2 // len(orders)
            for i, name in enumerate(order):
                n = sizes[name]
                if i == len(order) - 1 and size % (16 * n):
                    shapes.append((n, size, columns))
                else:
                    size //= n
                    shapes.append((n - 1, size, columns))
            assert size % 16 == 0
        return shapes

    def rows(self, base, size, index):
        return pl.ds(pl.multiple_of(base + index * size, 16), size)

    def whole(self, step):
        return self.shared and step == len(self.steps) - 1

    def down(self, step):
        copies = []
        for (own, n, peer), base, size, slot in self.steps[step]:
            for o in range(1, n):
                i, device = peer(o)
                if self.whole(step):
                    src, dst = self.part.at[self.rows(base, size, 0)], self.stages[slot].at[own]
                else:
                    src, dst = self.part.at[self.rows(base, size, i)], self.stages[slot].at[o - 1]
                copies.append(remote(src, dst, self.sems[:2], slot, device))
        return copies

    def up(self, step):
        copies = []
        for (own, n, peer), base, size, slot in [] if self.whole(step) else self.steps[step]:
            mine = self.total.at[self.rows(base, size, own)]
            for o in range(1, n):
                copies.append(remote(mine, mine, self.sems[2:], slot, peer(o)[1]))
        return copies

    def start_down(self, step):
        for copy in self.down(step):
            copy.start()

    def end_down(self, step, less=None):
        last = step == len(self.steps) - 1
        for (own, n, peer), base, size, slot in self.steps[step]:
            wait_all(self.stages[slot].at[pl.ds(0, n - 1)], self.sems[:2], slot, peer(1)[1])
            piece = min(size, 64)
            if self.whole(step):
                rows = self.rows(base, size, 0)
                self.stages[slot][own] = self.part[rows]
                self.total[rows] = sum(self.stages[slot][i].astype(F32) for i in range(n)).astype(BF16)
                continue

            def add(i, carry):
                rows = pl.ds(pl.multiple_of(base + own * size + i * piece, 16), piece)
                there = pl.ds(pl.multiple_of(i * piece, 16), piece)
                total = self.part[rows].astype(F32)
                for o in range(1, n):
                    total = total + self.stages[slot][o - 1, there].astype(F32)
                if less is not None:
                    total = total - less
                (self.total if last else self.part)[rows] = total.astype(BF16)
                return carry

            lax.fori_loop(0, size // piece, add, 0)

    def start_up(self, step):
        for copy in self.up(step):
            copy.start()

    def end_up(self, step):
        for (own, n, peer), base, size, slot in [] if self.whole(step) else self.steps[step]:
            rows = self.total.at[pl.ds(pl.multiple_of(base, 16), (n - 1) * size)]
            wait_all(rows, self.sems[2:], slot, peer(1)[1])

    def advance(self, stage, less=None):
        last = len(self.steps) - 1
        if stage <= last:
            self.end_down(stage, less if stage == last else None)
            if stage < last:
                self.start_down(stage + 1)
            else:
                self.start_up(last)
        else:
            step = 2 * last + 1 - stage
            self.end_up(step)
            if step:
                self.start_up(step - 1)


def plan(groups, dps, hops, width):
    wide, low, high = groups // 2, dps // 4, 4
    early = groups * LANES == width and 2 * wide * low * high * 16 == hops * LANES
    parts = 2 if hops % 2 == 0 and hops * width % (2 * 4 * wide * low * high * 16) == 0 else 1
    return early, parts


def make_kernel(dims):
    (groups, dps, batches, nodes, hops, feats, width, classes) = dims
    pieces = width // LANES
    tables = hops * groups
    nodes_batch = nodes * groups * dps
    total_nodes = batches * nodes_batch
    chunk = 64
    final = batches - 1
    early, mid_parts = plan(groups, dps, hops, width)
    bands = LANES // 16
    lane = [slice(j * LANES, (j + 1) * LANES) for j in range(pieces)]
    columns = [slice(k * width, (k + 1) * width) for k in range(hops)]

    def kernel(
        x_in, bucket_ref, mask_ref, labels_ref, w_in, gain_ref, shift_ref, slope_ref, slope_cat_ref, w_mid_in,
        gain_mid_ref, shift_mid_ref, slope_mid_ref, w_out_in, bias_in,
        out_features, out_mid, out_rest, out_small,
        spread, u_ref, join_ref, xt_ref, cat_ref, w_shift_ref, mid_ref, dshaped_ref, dmid_ref, grad_hops_ref, grad_out_ref,
        w_ref, w_mid_ref, w_out_ref, bias_ref, gain_rep, shift_rep, tab_a, tab_b, tab_e, tab_f, slopes_ref,
        table, table_near, table_far, t_total, s_near, s_far, s_total, e_near, e_far, e_total, c_near, c_far, c_total,
        part_mid, total_mid, part_rest, total_rest, stages_mid, stages_rest, gram_own, scale_own, level_own, stages_gram,
        t_sems, s_sems, e_sems, c_sems, d_sems, mid_sems, rest_sems, gram_sems, in_sems, out_sems, file_sems,
    ):
        spread_rows = feats * pieces * hops
        place = Place(groups, dps)
        barrier = pltpu.get_barrier_semaphore()
        for o in range(1, place.nears):
            pl.semaphore_signal(barrier, inc=1, device_id=place.near_peer(o)[1], device_id_type=MESH)
        for o in range(1, place.fars):
            pl.semaphore_signal(barrier, inc=1, device_id=place.far_peer(o)[1], device_id_type=MESH)

        def landing(ref, m):
            return ref.at[pl.ds(0, spread_rows), pl.ds(pl.multiple_of(m * LANES, LANES), LANES)]

        def x_copy(m):
            return pltpu.make_async_copy(x_in.at[m], landing(part_mid, m), in_sems.at[m])

        w_copy = pltpu.make_async_copy(w_in, landing(total_mid, 0), file_sems.at[1])
        w_mid_copy = pltpu.make_async_copy(w_mid_in, w_mid_ref, file_sems.at[2])
        w_copy.start()
        for m in range(batches):
            x_copy(m).start()
        w_mid_copy.start()

        stats = TableSum(place, table, table_near, table_far, t_total, t_sems[0:2], t_sems[2:4], t_sems[4:6])
        heads = SmallSum(place, s_near, s_far, s_total, s_sems[0:2], s_sems[2:4])
        backs = SmallSum(place, e_near, e_far, e_total, e_sems[0:2], e_sems[2:4])
        dots = TableSum(place, table, table_near, table_far, t_total, d_sems[0:2], d_sems[2:4], d_sems[4:6])
        amounts = SmallSum(place, c_near, c_far, c_total, c_sems[0:2], c_sems[2:4])
        mid_rows = [pl.ds(i * hops * width // mid_parts, hops * width // mid_parts) for i in range(mid_parts)]
        mids = [
            GradSum(place, part_mid.at[rows], total_mid.at[rows], stages_mid[i], mid_sems[i], MID_ORDERS)
            for i, rows in enumerate(mid_rows)
        ]
        if early:
            gram_rows = [pl.ds(m * hops * LANES, hops * LANES) for m in range(batches)]
            grams = [
                GradSum(place, part_mid.at[rows], part_mid.at[rows], stages_gram[m], gram_sems[m], REST_ORDERS)
                for m, rows in enumerate(gram_rows)
            ]
            owned = (place.core * place.wide * place.low + place.axis("plane")[0]) * place.high + place.hi
            owned_hop = lax.div(owned, bands)

        def mid_step(i, stage):
            if i < mid_parts:
                mids[i].advance(stage)
        rests = GradSum(place, part_rest, total_rest, stages_rest, rest_sems, REST_ORDERS)

        def loop(first, last, body):
            def step(m, carry):
                body(m)
                return carry

            lax.fori_loop(first, last, step, 0)

        def at(m, when, body):
            pl.when(m == when)(body)

        spread[spread_rows:] = jnp.zeros((spread.shape[0] - spread_rows, LANES), F32)

        def hop_rows(k):
            parts = [spread[pl.ds(j * hops + k, HOT, stride=pieces * hops)] for j in range(pieces)]
            return jnp.concatenate(parts, axis=1)

        w_copy.wait()
        spread[:spread_rows] = landing(total_mid, 0)[...].astype(F32)
        for k in range(hops):
            w_ref[k] = jnp.concatenate([hop_rows(k), jnp.zeros((LANES - HOT, width), F32)], axis=0).astype(BF16)
            w_shift_ref[k] = w_ref[k]
            for g in range(groups):
                gain_rep[k * groups + g : k * groups + g + 1] = gain_ref[k : k + 1]
                shift_rep[k * groups + g : k * groups + g + 1] = shift_ref[k : k + 1]
        grad_out_ref[...] = jnp.zeros_like(grad_out_ref)
        grad_out_ref[:classes] = w_out_in[...].astype(F32)
        w_out_ref[...] = grad_out_ref[...].astype(BF16)
        bias_ref[...] = jnp.full(bias_ref.shape, -1e30, F32)
        bias_ref[0:1, :classes] = bias_in[...]
        bias_row = jnp.broadcast_to(bias_ref[0:1], (LANES, LANES))
        bias_ref[...] = jnp.transpose(bias_row)[: bias_ref.shape[0]]
        grad_hops_ref[...] = jnp.zeros_like(grad_hops_ref)
        grad_out_ref[...] = jnp.zeros_like(grad_out_ref)
        slopes_ref[...] = jnp.zeros_like(slopes_ref)

        def hot_rows(m):
            ids = lax.rem(lax.broadcasted_iota(jnp.int32, (LANES - HOT, nodes), 0), 8)
            return (ids == bucket_ref[m]).astype(F32)

        def active_row(m, k):
            if k == 0:
                return jnp.ones((1, nodes), F32)
            return mask_ref[k - 1, pl.ds(m, 1)].astype(F32)

        which = lax.broadcasted_iota(jnp.int32, (groups, LANES), 1)
        amount = [jnp.zeros((groups, LANES), F32) for _ in range(hops)]
        for m in range(batches):
            hot = hot_rows(m)
            for k in range(hops):
                here = jnp.sum(hot * active_row(m, k), axis=1, keepdims=True)
                amount[k] = jnp.where(which == m, here[:groups], amount[k])
        for k in range(hops):
            c_near[0, place.near, k * groups : (k + 1) * groups] = amount[k]

        def by_node(row):
            return jnp.transpose(jnp.broadcast_to(row, (LANES, nodes)))

        def moments(m):
            x_copy(m).wait()
            spread[:spread_rows] = landing(part_mid, m)[...].astype(F32)
            hot_all = hot_rows(m)
            cat_ref[m] = by_node(bucket_ref[m].astype(F32)).astype(BF16)
            for k in range(hops):
                block = jnp.concatenate([hop_rows(k), hot_all], axis=0) * active_row(m, k)
                xt = block.astype(BF16)
                hot = xt[HOT:]
                xt_ref[m, k] = xt
                pre = dot(xt, w_ref[k], TN)
                square = (pre * pre).astype(BF16)
                second = dot(hot, square)
                sums = jnp.concatenate(split_high(dot(hot, xt, NT)), axis=1)
                first = dot(sums, jnp.concatenate([w_ref[k], w_ref[k]], axis=0))
                for j in range(pieces):
                    base = 2 * tables * j + k * groups
                    table[m, base : base + groups] = first[:groups, lane[j]]
                    table[m, base + tables : base + tables + groups] = second[:groups, lane[j]]

        def moments_step(m):
            moments(m)

            @pl.when(m == 0)
            def _():
                pl.semaphore_wait(barrier, place.nears + place.fars - 2)
                amounts.start(0)

            stats.start(m)
            at(m, 2, lambda: amounts.forward(0))
            pl.when(m >= 2)(lambda: stats.forward(m - 2))

        loop(0, batches, moments_step)

        def gram(m):
            for k in range(hops):
                xt = xt_ref[m, k]
                masked = [xt * xt[HOT + g : HOT + g + 1] for g in range(groups)]
                here = dot(jnp.concatenate(masked, axis=0), xt, NT)
                by_bucket = [here[g * LANES : g * LANES + HOT] for g in range(groups)]
                block = jnp.concatenate(by_bucket, axis=1)
                block = jnp.concatenate([block, jnp.zeros((LANES - HOT, width), F32)], axis=0)
                start = pl.multiple_of((m * hops + k) * LANES, LANES)
                part_mid[pl.ds(start, LANES)] = block.astype(BF16)

        def end_gram(m):
            grams[m].end_down(2)
            rows = pl.multiple_of(m * hops * LANES + owned * 16, 16)
            gram_own[m * 16 : (m + 1) * 16] = part_mid[pl.ds(rows, 16)]

        def gram_step(m):
            if early:
                gram(m)
                for i in range(batches):
                    at(m, i, lambda i=i: grams[i].start_down(0))

            @pl.when(m == 0)
            def _():
                stats.forward(final - 1)
                stats.back(0)

            @pl.when(m == 1)
            def _():
                stats.forward(final)
                stats.back(1)

        loop(0, batches, gram_step)
        if early:
            grams[0].advance(0)
        amounts.finish(0)
        w_mid_copy.wait()
        stats.back(final - 1)
        stats.finish(0)

        def counts_of(m):
            here = lax.broadcasted_iota(jnp.int32, (tables, LANES), 1) == m
            counts = jnp.sum(jnp.where(here, c_total[0], 0.0), axis=1, keepdims=True)
            return jnp.broadcast_to(counts, (tables, LANES))

        def bucket_tables(m):
            counts = counts_of(m)
            for j in range(pieces):
                base = 2 * tables * j
                mean = t_total[m, base : base + tables] / counts
                second = t_total[m, base + tables : base + 2 * tables] / counts
                inv = lax.rsqrt(second - mean * mean + EPSILON)
                a = 0.5 * gain_rep[:, lane[j]] * inv
                tab_a[m, :, lane[j]] = a
                tab_b[m, :, lane[j]] = 0.5 * shift_rep[:, lane[j]] - a * mean
                high, low = split_high(0.5 * shift_rep[:, lane[j]] / a - mean)
                for k in range(hops):
                    rows = slice(k * groups, (k + 1) * groups)
                    parts = []
                    for part in (high, low):
                        parts.append(part[rows].astype(F32))
                        if groups < 8:
                            parts.append(jnp.zeros((8 - groups, LANES), F32))
                    w_shift_ref[k, HOT:, lane[j]] = jnp.concatenate(parts, axis=0).astype(BF16)

        def choose(masks, values, k, j):
            result = values[k * groups + groups - 1 : k * groups + groups, lane[j]]
            for g in range(groups - 2, -1, -1):
                result = jnp.where(masks[g], values[k * groups + g : k * groups + g + 1, lane[j]], result)
            return result

        def masks_of(m, rows):
            cat = cat_ref[m, rows].astype(F32)
            return [cat == float(g) for g in range(groups - 1)]

        projected = [dshaped_ref.at[final], dshaped_ref.at[final - 1]]

        halves = [slice(0, nodes // 2), slice(nodes // 2, nodes)]
        chunks = [slice(i * chunk, (i + 1) * chunk) for i in range(nodes // chunk)]

        def put_beside(beside, i):
            for n, body in enumerate(beside):
                if i == n * len(chunks) // len(beside):
                    body()

        def forward(m):
            bucket_tables(m)

            def projection(k, rows):
                projected[k % 2][rows] = dot(xt_ref[m, k, :, rows], w_shift_ref[k], TN)

            def product(k, rows):
                middle = dot(join_ref[m, rows, columns[k]], w_mid_ref[columns[k]])
                mid_ref[m, rows] = middle if k == 0 else mid_ref[m, rows] + middle

            for rows in halves:
                projection(0, rows)
            for k in range(hops):
                beside = [functools.partial(projection, k + 1, rows) for rows in halves] if k + 1 < hops else []
                beside += [functools.partial(product, k - 1, rows) for rows in halves] if k else []
                for i, rows in enumerate(chunks):
                    put_beside(beside, i)
                    masks = masks_of(m, rows)
                    for j in range(pieces):
                        bend = 0.5 - 0.5 * slope_ref[k : k + 1, lane[j]]
                        bend_cat = 0.5 - 0.5 * slope_cat_ref[:, k * width + j * LANES : k * width + (j + 1) * LANES]
                        scale = choose(masks, tab_a.at[m], k, j)
                        u = projected[k % 2][rows, lane[j]] * scale
                        u_ref[m, k, rows, lane[j]] = u
                        half = u - (bend * u) * (1.0 - jnp.tanh(u))
                        half = half - (bend_cat * half) * (1.0 - jnp.tanh(half))
                        join_ref[m, rows, k * width + j * LANES : k * width + (j + 1) * LANES] = half.astype(BF16)
            for rows in halves:
                product(hops - 1, rows)
            middle = mid_ref[m]
            first = jnp.sum(middle, axis=0, keepdims=True)
            second = jnp.sum(middle * middle, axis=0, keepdims=True)
            own = heads.own(m)
            for j in range(pieces):
                own[j : j + 1] = first[:, lane[j]]
                own[pieces + j : pieces + j + 1] = second[:, lane[j]]

        def row_of(ref, m, first):
            return jnp.concatenate([ref[m, first + j : first + j + 1] for j in range(pieces)], axis=1)

        def head_scale(m):
            mean = row_of(s_total, m, 0) * (1.0 / nodes_batch)
            second = row_of(s_total, m, pieces) * (1.0 / nodes_batch)
            inv = lax.rsqrt(4.0 * (second - mean * mean) + EPSILON)
            return mean, inv

        def head(m):
            heads.finish(m)
            mean, inv = head_scale(m)
            scale = gain_mid_ref[...] * inv
            offset = 0.5 * shift_mid_ref[...] - scale * mean
            slope = slope_mid_ref[...]
            u = mid_ref[m] * scale + offset
            mid_ref[m] = u
            tanh = jnp.tanh(u)
            gap = u * (1.0 - tanh)
            outer = (2.0 * u - (1.0 - slope) * gap).astype(BF16)
            logits = dot(w_out_ref[...], outer, NT) + bias_ref[:, 0:1]
            top = jnp.max(logits, axis=0, keepdims=True)
            powers = jnp.exp(logits - top)
            total = jnp.sum(powers, axis=0, keepdims=True)
            wanted = (lax.broadcasted_iota(jnp.int32, logits.shape, 0) == labels_ref[pl.ds(m, 1)]).astype(F32)
            loss = jnp.log(total) + top - jnp.sum(logits * wanted, axis=0, keepdims=True)
            dlogits = (powers / total - wanted) * (1.0 / total_nodes)
            low = dlogits.astype(BF16)
            grad_out_ref[...] += dot(low, outer)
            douter = dot(low, w_out_ref[...], TN)
            grad_slope = jnp.sum(douter * gap, axis=0, keepdims=True)
            dshaped = douter * (slope + (0.5 - 0.5 * slope) * (1.0 + tanh) * (1.0 + gap))
            dshaped_ref[m] = dshaped
            head_sum = jnp.sum(dshaped, axis=0, keepdims=True)
            head_dot = jnp.sum(dshaped * u, axis=0, keepdims=True)
            own = backs.own(m)
            for j in range(pieces):
                own[j : j + 1] = head_sum[:, lane[j]]
                own[pieces + j : pieces + j + 1] = head_dot[:, lane[j]]
                own[2 * pieces + j : 2 * pieces + j + 1] = grad_slope[:, lane[j]]
            folded = sum(dlogits[:, i * LANES : (i + 1) * LANES] for i in range(nodes // LANES))
            square = jnp.concatenate([folded, jnp.zeros((LANES - folded.shape[0], LANES), F32)], axis=0)
            own[3 * pieces : 3 * pieces + 1] = jnp.sum(jnp.transpose(square), axis=0, keepdims=True)
            own[3 * pieces + 1 : 3 * pieces + 2] = sum(
                loss[:, i * LANES : (i + 1) * LANES] for i in range(nodes // LANES)
            )
            own[3 * pieces + 2 :] = jnp.zeros((own.shape[0] - 3 * pieces - 2, LANES), F32)
            backs.start(m)

        def head_grads(m):
            inv = head_scale(m)[1]
            head_sum = row_of(e_total, m, 0)
            head_dot = (2.0 * row_of(e_total, m, pieces) - shift_mid_ref[...] * head_sum) / gain_mid_ref[...]
            return inv, head_sum, head_dot

        def back_head(m):
            backs.finish(m)
            inv, head_sum, head_dot = head_grads(m)
            scale = gain_mid_ref[...] * inv
            tilt = 2.0 * inv * head_dot * (1.0 / nodes_batch)
            level = scale * head_sum * (1.0 / nodes_batch) - 0.5 * shift_mid_ref[...] * tilt
            dmid_ref[m] = (scale * dshaped_ref[m] - level - mid_ref[m] * tilt).astype(BF16)

        gradients = [mid_ref.at[0], dshaped_ref.at[0]]

        def products(k):
            return (part_rest, total_rest)[k % 2].at[pl.ds(0, nodes)]

        def backward(m, which_hops, target, tick):
            def into(k, rows):
                gradients[k % 2][rows] = dot(dmid_ref[m, rows], w_mid_ref[columns[k]], NT)

            def bucket_sums(k):
                first_sums(k)
                second_sums(k)

            def first_sums(k):
                hot = xt_ref[m, k, HOT:LANES]
                if early:
                    both = dot(xt_ref[m, k], target(k)[...])
                    grad_hops_ref[k, :HOT] += 2.0 * both[:HOT]
                    first = both[HOT:]
                else:
                    first = dot(hot, target(k)[...])
                for j in range(pieces):
                    base = 2 * tables * j + k * groups
                    table[m, base : base + groups] = first[:groups, lane[j]]

            def second_sums(k):
                second = dot(xt_ref[m, k, HOT:LANES], products(k)[...])
                for j in range(pieces):
                    base = 2 * tables * j + k * groups
                    table[m, base + tables : base + tables + groups] = second[:groups, lane[j]]

            for rows in halves:
                into(which_hops[0], rows)
            for k in which_hops:
                beside = [functools.partial(into, k + 1, rows) for rows in halves] if k + 1 in which_hops else []
                beside += [functools.partial(f, k - 1) for f in (first_sums, second_sums)] if k - 1 in which_hops else []
                slope_sums = [jnp.zeros((8, LANES), F32) for _ in range(2 * pieces)]
                result = target(k)
                for i, rows in enumerate(chunks):
                    put_beside(beside, i)
                    masks = masks_of(m, rows)
                    for j in range(pieces):
                        slope = slope_ref[k : k + 1, lane[j]]
                        slope_cat = slope_cat_ref[:, k * width + j * LANES : k * width + (j + 1) * LANES]
                        bend, bend_cat = 0.5 - 0.5 * slope, 0.5 - 0.5 * slope_cat
                        u = u_ref[m, k, rows, lane[j]]
                        tanh = jnp.tanh(u)
                        gap = (bend * u) * (1.0 - tanh)
                        half = u - gap
                        tanh_cat = jnp.tanh(half)
                        gap_cat = (bend_cat * half) * (1.0 - tanh_cat)
                        grad = gradients[k % 2][rows, lane[j]]
                        slope_sums[pieces + j] += jnp.sum((grad * gap_cat).reshape(-1, 8, LANES), axis=0)
                        grad = grad * (slope_cat + (1.0 + tanh_cat) * (bend_cat + gap_cat))
                        slope_sums[j] += jnp.sum((grad * gap).reshape(-1, 8, LANES), axis=0)
                        grad = grad * (slope + (1.0 + tanh) * (bend + gap))
                        grad = grad * choose(masks, tab_a.at[m], k, j)
                        result[rows, lane[j]] = grad.astype(BF16)
                        products(k)[rows, lane[j]] = (grad * u).astype(BF16)
                for j in range(pieces):
                    slope = slope_ref[k : k + 1, lane[j]]
                    slope_cat = slope_cat_ref[:, k * width + j * LANES : k * width + (j + 1) * LANES]
                    for s, values in enumerate((slope, slope_cat)):
                        grad_hops_ref[k, feats + s : feats + s + 1, lane[j]] += jnp.sum(
                            slope_sums[s * pieces + j], axis=0, keepdims=True
                        ) / (0.5 - 0.5 * values)
                if k == which_hops[-1]:
                    bucket_sums(k)
                tick(k)

        def first_target(k):
            return total_mid.at[pl.ds(k * nodes, nodes)]

        def first_copy(k):
            return pltpu.make_async_copy(first_target(k), join_ref.at[0, :, pl.ds(k * width, width)], in_sems.at[k])

        def no_tick(k):
            pass

        def forward_step(m):
            pl.when(m >= 1)(lambda: stats.finish(m))
            forward(m)
            heads.start(m)
            pl.when(m >= 1)(lambda: heads.forward(m - 1))
            at(m, 0, lambda: stats.back(final))
            if early:
                at(m, 3, lambda: end_gram(0))
                for i in range(2, final + 1):
                    at(m, i, lambda i=i: grams[i - 2].advance(1))
                for i in range(1, final + 1):
                    at(m, i - 1, lambda i=i: grams[i].advance(0))
            at(m, 2, lambda: head(0))

        loop(0, batches, forward_step)
        backs.forward(0)

        def head_step(m):
            head(m)

            @pl.when(m == 1)
            def _():
                heads.forward(final)
                if early:
                    grams[2].advance(1)
                    end_gram(1)

            @pl.when(m == 2)
            def _():
                backs.forward(1)
                back_head(0)
                backward(0, [0, 1], first_target, no_tick)
                if early:
                    grams[final].advance(1)
                    end_gram(2)

        loop(1, batches, head_step)
        backs.forward(2)
        if early:
            end_gram(final)

        def late_tick(k):
            if k == hops - 1:
                backs.forward(final)

        backward(0, list(range(2, hops)), first_target, late_tick)
        dots.start(0)
        for m in range(1, final):
            back_head(m)

        held = [mid_ref.at[m] for m in range(final)] + [dshaped_ref.at[0]]
        for k in range(hops):
            held[k][...] = sum(dot(join_ref[m, :, columns[k]], dmid_ref[m], TN) for m in range(final))
        back_head(final)
        for k in range(hops):
            total = held[k][...] + dot(join_ref[final, :, columns[k]], dmid_ref[final], TN)
            part_mid[columns[k]] = (2.0 * total).astype(BF16)
            if (k + 1) * mid_parts % hops == 0:
                mids[(k + 1) * mid_parts // hops - 1].start_down(0)
        for k in range(hops):
            first_copy(k).start()
        dots.forward(0)

        def wait_first():
            for k in range(hops):
                first_copy(k).wait()

        ticks = {
            (1, 0): [wait_first],
            (1, 1): [lambda: mid_step(0, 0)],
            (1, 2): [lambda: mid_step(1, 0), lambda: dots.back(0)],
            (2, 0): [lambda: mid_step(0, 1)],
            (2, 1): [lambda: mid_step(1, 1)],
            (2, 2): [lambda: dots.forward(1)],
            (2, 3): [lambda: mid_step(0, 2)],
            (3, 0): [lambda: mid_step(1, 2)],
            (3, 1): [lambda: dots.back(1)],
            (3, 2): [lambda: dots.forward(2)],
            (3, 3): [lambda: mid_step(0, 3)],
        }

        def backward_step(m):
            def tick(k):
                for when, bodies in ticks.items():
                    if when[1] == k:
                        for body in bodies:
                            at(m, when[0], body)

            backward(m, list(range(hops)), lambda k: join_ref.at[m, :, columns[k]], tick)
            dots.start(m)

        loop(1, batches, backward_step)

        def last_tables(m):
            counts = counts_of(m)
            for j in range(pieces):
                base = 2 * tables * j
                a = tab_a[m, :, lane[j]]
                inv = 2.0 * a / gain_rep[:, lane[j]]
                shift = shift_rep[:, lane[j]]
                scaled = t_total[m, base : base + tables]
                bucket_sum = scaled / a
                bucket_dot = (2.0 * t_total[m, base + tables : base + 2 * tables] / a - shift * bucket_sum) / gain_rep[
                    :, lane[j]
                ]
                tilt = inv * bucket_dot / counts
                tab_f[:, lane[j]] = tilt
                tab_e[:, lane[j]] = scaled / counts - 0.5 * shift * tilt
                for k in range(hops):
                    here = slice(k * groups, (k + 1) * groups)
                    slopes_ref[k : k + 1, lane[j]] += jnp.sum(bucket_dot[here], axis=0, keepdims=True)
                    slopes_ref[hops + k : hops + k + 1, lane[j]] += jnp.sum(bucket_sum[here], axis=0, keepdims=True)

        def own_tables(m):
            for k in range(hops):
                rows = slice(k * groups, (k + 1) * groups)

                @pl.when(owned_hop == k)
                def _(rows=rows):
                    tilt = tab_f[rows]
                    scale_own[m] = tilt * tab_a[m, rows]
                    level_own[m] = tab_e[rows] + tilt * tab_b[m, rows]

        def last(m):
            dots.finish(m)
            last_tables(m)
            if early:
                own_tables(m)
                at(m, final, lambda: rests.advance(2, correction()))

            def weights(k):
                grad_hops_ref[k, :HOT] += dot(xt_ref[m, k, :HOT], join_ref[m, :, columns[k]]) * 2.0

            for k in range(hops):
                if k and not early:
                    weights(k - 1)
                for rows in chunks:
                    masks = masks_of(m, rows)
                    for j in range(pieces):
                        here = slice(k * width + j * LANES, k * width + (j + 1) * LANES)
                        grad = join_ref[m, rows, here].astype(F32) - choose(masks, tab_e, k, j)
                        grad = grad - choose(masks, tab_f, k, j) * u_ref[m, k, rows, lane[j]]
                        join_ref[m, rows, here] = grad.astype(BF16)
            if not early:
                weights(hops - 1)

        def correction():
            total = jnp.zeros((16, width), F32)
            weights = w_ref[owned_hop].astype(F32)
            row = lax.broadcasted_iota(jnp.int32, (LANES, width), 0)
            for m in range(batches):
                scaled = [
                    jnp.where(row == HOT + g, level_own[m, g : g + 1], weights * scale_own[m, g : g + 1]).astype(BF16)
                    for g in range(groups)
                ]
                total = total + dot(gram_own[m * 16 : (m + 1) * 16], jnp.concatenate(scaled, axis=0))
            return 2.0 * total

        def features_copy(m):
            return pltpu.make_async_copy(spread.at[pl.ds(0, spread_rows)], out_features.at[m], out_sems.at[m])

        def features(m):
            pl.when(m >= 1)(lambda: features_copy(m - 1).wait())
            for k in range(hops):
                scale = active_row(m, k) * float(2 * total_nodes)
                values = dot(w_ref[k], join_ref[m, :, columns[k]], NT) * scale
                for j in range(pieces):
                    spread[pl.ds(j * hops + k, feats, stride=pieces * hops)] = values[:feats, lane[j]]
            features_copy(m).start()

        def start_rests():
            rows = grad_out_ref.shape[0] // hops
            for k in range(hops):
                grad_hops_ref[k, SPARE : SPARE + rows] = grad_out_ref[k * rows : (k + 1) * rows]
                part_rest[k * LANES : (k + 1) * LANES] = grad_hops_ref[k].astype(BF16)
            if part_rest.shape[0] > hops * LANES:
                part_rest[hops * LANES :] = jnp.zeros((part_rest.shape[0] - hops * LANES, width), BF16)
            rests.start_down(0)

        def last_step(m):
            last(m)

            @pl.when(m == 0)
            def _():
                if early:
                    rests.advance(0)
                dots.back(2)
                mid_step(1, 3)

            at(m, 1, lambda: mid_step(0, 4))
            at(m, 2, lambda: mid_step(0, 5))

            @pl.when(m == 3)
            def _():
                if not early:
                    start_rests()

            features(m)
            at(m, 0, lambda: dots.forward(final))

            @pl.when(m == 1)
            def _():
                dots.back(final)
                if early:
                    rests.advance(1)
                mid_step(1, 4)

            at(m, 2, lambda: mid_step(1, 5))
            at(m, 3, lambda: mid_step(0, 6))

        if early:
            start_rests()
        loop(0, batches, last_step)
        if not early:
            for stage in range(3):
                rests.advance(stage)

        grad_gain = jnp.zeros((1, width), F32)
        grad_shift = jnp.zeros((1, width), F32)
        grad_slope = jnp.zeros((1, width), F32)
        bias_loss = jnp.zeros((2, LANES), F32)
        for m in range(batches):
            _, head_sum, head_dot = head_grads(m)
            grad_gain = grad_gain + head_dot
            grad_shift = grad_shift + head_sum
            grad_slope = grad_slope + row_of(e_total, m, 2 * pieces)
            bias_loss = bias_loss + e_total[m, 3 * pieces : 3 * pieces + 2]
        out_small[: 2 * hops] = slopes_ref[...]
        loss = jnp.sum(bias_loss[1:2], axis=1, keepdims=True) * (1.0 / total_nodes)
        last_row = [bias_loss[0:1], jnp.broadcast_to(loss, (1, LANES)), jnp.zeros((1, width - 2 * LANES), F32)]
        for i, row in enumerate((grad_gain, grad_shift, grad_slope, jnp.concatenate(last_row, axis=1))):
            out_small[2 * hops + i : 2 * hops + i + 1] = row

        rests.advance(3)
        mid_step(1, 6)
        mid_step(0, 7)
        rests.advance(4)
        mid_step(1, 7)
        mid_file = pltpu.make_async_copy(total_mid, out_mid, file_sems.at[0])
        mid_file.start()
        rests.advance(5)
        rest_file = pltpu.make_async_copy(total_rest.at[pl.ds(0, hops * LANES)], out_rest, file_sems.at[1])
        rest_file.start()
        features_copy(final).wait()
        mid_file.wait()
        rest_file.wait()

    return kernel


def make_finish(dims):
    (groups, dps, batches, nodes, hops, feats, width, classes) = dims
    pieces = width // LANES
    spare = -(-classes // 16) * 16 // hops

    def kernel(
        features_in, mid_in, rest_in, small_in,
        features, mid, hops_grad, gain, shift, slope, cat, gain_mid, shift_mid, slope_mid, out_grad, bias, loss,
        low, wide, held, rest, spread, sems,
    ):
        rest_copy = pltpu.make_async_copy(rest_in, rest, sems.at[4, 0])
        spread_rows = feats * pieces * hops
        spread_copy = pltpu.make_async_copy(spread.at[pl.ds(0, spread_rows)], hops_grad, sems.at[4, 1])
        in_copy = [pltpu.make_async_copy(features_in.at[m], held.at[m], sems.at[0, m]) for m in range(batches)]
        out_copy = [pltpu.make_async_copy(held.at[m], features.at[m], sems.at[3, m]) for m in range(batches)]
        low_copy = [pltpu.make_async_copy(mid_in.at[pl.ds(k * width, width)], low.at[k], sems.at[1, k]) for k in range(hops)]
        wide_copy = [pltpu.make_async_copy(wide.at[k], mid.at[pl.ds(k * width, width)], sems.at[2, k]) for k in range(hops)]
        for copy in [rest_copy] + [c for pair in zip(in_copy, low_copy) for c in pair]:
            copy.start()
        rest_copy.wait()
        for k in range(hops):
            values = rest[k * LANES : (k + 1) * LANES].astype(F32)
            for j in range(pieces):
                spread[pl.ds(j * hops + k, feats, stride=pieces * hops)] = values[:feats, j * LANES : (j + 1) * LANES]
            slope[k : k + 1] = values[feats : feats + 1]
            cat[:, k * width : (k + 1) * width] = values[feats + 1 : feats + 2]
            count = min(spare, classes - k * spare)
            out_grad[k * spare : k * spare + count] = values[SPARE : SPARE + count]
        spread_copy.start()
        gain[...] = small_in[:hops]
        shift[...] = small_in[hops : 2 * hops]
        gain_mid[...] = small_in[2 * hops : 2 * hops + 1]
        shift_mid[...] = small_in[2 * hops + 1 : 2 * hops + 2]
        slope_mid[...] = small_in[2 * hops + 2 : 2 * hops + 3]
        bias[...] = small_in[2 * hops + 3 : 2 * hops + 4, :classes]
        loss[...] = small_in[2 * hops + 3 : 2 * hops + 4, LANES : LANES + 1]
        for i in range(max(batches, hops)):
            if i < batches:
                in_copy[i].wait()
                out_copy[i].start()
            if i < hops:
                low_copy[i].wait()
                wide[i] = low[i].astype(F32)
                wide_copy[i].start()
        for copy in wide_copy + out_copy + [spread_copy]:
            copy.wait()

    return kernel


def by_piece(values):
    *lead, feats, hops, width = values.shape
    values = jnp.swapaxes(values.reshape(*lead, feats, hops, width // LANES, LANES), -3, -2)
    return values.reshape(*lead, feats * hops * width // LANES, LANES)


def by_hop(rows, hops, pieces):
    *lead, count, _ = rows.shape
    values = rows.reshape(*lead, count // (hops * pieces), pieces, hops, LANES)
    return jnp.swapaxes(values, -3, -2).reshape(*lead, count // (hops * pieces), hops, pieces * LANES)


def shards(
    features,
    buckets,
    hop_mask,
    labels,
    w_hops,
    gain_hops,
    shift_hops,
    slope_hops,
    slope_cat,
    w_mid,
    gain_mid,
    shift_mid,
    slope_mid,
    w_out,
    bias_out,
):
    batches, nodes, hops, feats = features.shape
    width, classes = w_out.shape
    groups, dps = lax.axis_size("bucket"), lax.axis_size("dp")
    dims = (groups, dps, batches, nodes, hops, feats, width, classes)
    pieces = width // LANES
    joined_width = hops * width
    tables = hops * groups
    padded = -(-classes // 16) * 16

    wide, low, high = groups // 2, dps // 4, 4
    sizes = {"wide": wide, "low": low, "high": high, "plane": wide * low}
    rows_rest = max(hops * LANES, 2 * wide * low * 16)
    early, mid_parts = plan(groups, dps, hops, width)
    mid_shapes = GradSum.stage_shapes(joined_width // mid_parts, width, MID_ORDERS, sizes)
    gram_count = batches if early else 0
    own_rows = 16 * batches if early else 16
    rest_shapes = GradSum.stage_shapes(rows_rest, width, REST_ORDERS, sizes)
    _, nears, fars = Place.group_sizes(groups, dps)
    table_rows = 2 * tables * pieces
    share = table_rows // nears
    sem = pltpu.SemaphoreType.DMA

    def small_scratch(rows, copies=batches):
        return [
            pltpu.VMEM((copies, nears, rows, LANES), F32),
            pltpu.VMEM((copies, fars, rows, LANES), F32),
            pltpu.VMEM((copies, rows, LANES), F32),
        ]

    vmem = pl.BlockSpec(memory_space=pltpu.VMEM)
    hbm = pl.BlockSpec(memory_space=pl.ANY)

    def real(*shape):
        return jax.ShapeDtypeStruct(shape, F32)

    outs = pl.pallas_call(
        make_kernel(dims),
        name="train_step",
        out_shape=(
            real(batches, feats * pieces * hops, LANES),
            jax.ShapeDtypeStruct((joined_width, width), BF16),
            jax.ShapeDtypeStruct((hops * LANES, width), BF16),
            real(2 * hops + 4, width),
        ),
        in_specs=[hbm] + [vmem] * 3 + [hbm] + [vmem] * 4 + [hbm] + [vmem] * 5,
        out_specs=(hbm, hbm, hbm, vmem),
        scratch_shapes=[
            pltpu.VMEM((HOT * pieces * hops, LANES), F32),
            pltpu.VMEM((batches, hops, nodes, width), F32),
            pltpu.VMEM((batches, nodes, joined_width), BF16),
            pltpu.VMEM((batches, hops, LANES, nodes), BF16),
            pltpu.VMEM((batches, nodes, LANES), BF16),
            pltpu.VMEM((hops, LANES, width), BF16),
            pltpu.VMEM((batches, nodes, width), F32),
            pltpu.VMEM((batches, nodes, width), F32),
            pltpu.VMEM((batches, nodes, width), BF16),
            pltpu.VMEM((hops, LANES, width), F32),
            pltpu.VMEM((padded, width), F32),
            pltpu.VMEM((hops, LANES, width), BF16),
            pltpu.VMEM((joined_width, width), BF16),
            pltpu.VMEM((padded, width), BF16),
            pltpu.VMEM((padded, LANES), F32),
            pltpu.VMEM((tables, width), F32),
            pltpu.VMEM((tables, width), F32),
        ]
        + [pltpu.VMEM((batches, tables, width), F32) for _ in range(2)]
        + [pltpu.VMEM((tables, width), F32) for _ in range(2)]
        + [pltpu.VMEM((2 * hops, width), F32)]
        + [pltpu.VMEM((batches, table_rows, LANES), F32)]
        + [pltpu.VMEM((batches, nears, share, LANES), F32), pltpu.VMEM((batches, fars, share, LANES), F32)]
        + [pltpu.VMEM((batches, table_rows, LANES), F32)]
        + small_scratch(8)
        + small_scratch(16)
        + small_scratch(tables, 1)
        + [
            pltpu.VMEM((joined_width, width), BF16),
            pltpu.VMEM((joined_width, width), BF16),
            pltpu.VMEM((rows_rest, width), BF16),
            pltpu.VMEM((rows_rest, width), BF16),
            [[pltpu.VMEM(s, BF16) for s in mid_shapes] for _ in range(mid_parts)],
            [pltpu.VMEM(s, BF16) for s in rest_shapes],
            pltpu.VMEM((own_rows, width), BF16),
            pltpu.VMEM((batches, groups, width), F32),
            pltpu.VMEM((batches, groups, width), F32),
            [[pltpu.VMEM(s, BF16) for s in rest_shapes] for _ in range(gram_count)],
            [sem((batches,)) for _ in range(6)],
            [sem((batches,)) for _ in range(4)],
            [sem((batches,)) for _ in range(4)],
            [sem((1,)) for _ in range(4)],
            [sem((batches,)) for _ in range(6)],
            [[sem((len(mid_shapes),)) for _ in range(4)] for _ in range(mid_parts)],
            [sem((len(rest_shapes),)) for _ in range(4)],
            [[sem((len(rest_shapes),)) for _ in range(4)] for _ in range(gram_count)],
            sem((max(batches, hops),)),
            sem((batches,)),
            sem((3,)),
        ],
        compiler_params=pltpu.CompilerParams(
            collective_id=0, has_side_effects=True, vmem_limit_bytes=int(63.9 * 2**20)
        ),
    )(
        by_piece(jnp.transpose(features, (0, 3, 2, 1))),
        jnp.transpose(buckets, (0, 2, 1)),
        jnp.transpose(hop_mask, (2, 0, 1)),
        labels,
        by_piece(jnp.transpose(w_hops, (1, 0, 2))),
        gain_hops,
        shift_hops,
        slope_hops,
        slope_cat[None],
        w_mid,
        gain_mid[None],
        shift_mid[None],
        slope_mid[None],
        w_out.T,
        bias_out[None],
    )
    outs = pl.pallas_call(
        make_finish(dims),
        name="finish",
        out_shape=(
            real(batches, feats * pieces * hops, LANES),
            real(joined_width, width),
            real(feats * pieces * hops, LANES),
            real(hops, width),
            real(hops, width),
            real(hops, width),
            real(1, joined_width),
            real(1, width),
            real(1, width),
            real(1, width),
            real(classes, width),
            real(1, classes),
            real(1, 1),
        ),
        in_specs=[hbm, hbm, hbm, vmem],
        out_specs=(hbm, hbm, hbm) + (vmem,) * 10,
        scratch_shapes=[
            pltpu.VMEM((hops, width, width), BF16),
            pltpu.VMEM((hops, width, width), F32),
            pltpu.VMEM((batches, feats * pieces * hops, LANES), F32),
            pltpu.VMEM((hops * LANES, width), BF16),
            pltpu.VMEM((HOT * pieces * hops, LANES), F32),
            sem((5, max(batches, hops))),
        ],
        compiler_params=pltpu.CompilerParams(vmem_limit_bytes=int(63.9 * 2**20)),
    )(*outs)
    (features_grad, mid_grad, hops_grad, gain, shift, slope, cat, gain_m, shift_m, slope_m, out_grad, bias, loss) = outs
    return (
        loss[0, 0],
        jnp.transpose(by_hop(features_grad, hops, nodes // LANES), (0, 3, 2, 1)),
        jnp.transpose(by_hop(hops_grad, hops, pieces), (1, 0, 2)),
        gain,
        shift,
        slope,
        cat[0],
        mid_grad,
        gain_m[0],
        shift_m[0],
        slope_m[0],
        out_grad.T,
        bias[0],
    )


def solution(mesh):
    nodes_split = ("bucket", "dp")
    placed = (
        P(None, nodes_split, None, None),
        P(None, nodes_split, None),
        P(None, nodes_split, None),
        P(None, nodes_split),
    ) + (P(),) * 11
    return jax.shard_map(
        shards,
        mesh=mesh,
        in_specs=placed,
        out_specs=(P(), P(None, nodes_split, None, None)) + (P(),) * 11,
        check_vma=False,
    )
```

```python
import functools

import jax
import jax.numpy as jnp
from jax import lax
from jax.experimental import pallas as pl
from jax.experimental.pallas import tpu as pltpu
from jax.sharding import PartitionSpec as P

F32 = jnp.float32
BF16 = jnp.bfloat16
EPSILON = 1e-05
MESH = pl.DeviceIdType.MESH
LANES = 128
HOT = 112
SPARE = 104
MID_ORDERS = (("wide", "low", "high"), ("low", "wide", "high"))
REST_ORDERS = (("plane", "high"),)
NN, NT, TN = ((1,), (0,)), ((1,), (1,)), ((0,), (0,))


def dot(left, right, dims=NN):
    return lax.dot_general(left, right, (dims, ((), ())), preferred_element_type=F32)


def split_high(values):
    high = values.astype(BF16)
    return high, (values - high.astype(F32)).astype(BF16)


class Place:
    def __init__(self, groups, dps):
        self.groups, self.dps = groups, dps
        self.high = 4
        self.low = dps // self.high
        self.wide = groups // 2
        self.b = lax.axis_index("bucket")
        self.d = lax.axis_index("dp")
        self.core = lax.rem(self.b, 2)
        self.x = lax.div(self.b, 2)
        self.lo = lax.rem(self.d, self.low)
        self.hi = lax.div(self.d, self.low)
        self.fold, self.nears, self.fars = self.group_sizes(groups, dps)
        self.near = self.b * self.fold + lax.rem(self.d, self.fold)
        self.far = lax.div(self.d, self.fold)

    @staticmethod
    def group_sizes(groups, dps):
        low = dps // 4
        fold = low if groups * low <= 8 else 1
        return fold, groups * fold, dps // fold

    def at(self, b=None, d=None):
        return {"bucket": self.b if b is None else b, "dp": self.d if d is None else d}

    def near_peer(self, o):
        i = lax.rem(self.near + o, self.nears)
        b, lo = lax.div(i, self.fold), lax.rem(i, self.fold)
        return i, self.at(b=b, d=lax.div(self.d, self.fold) * self.fold + lo)

    def far_peer(self, o):
        i = lax.rem(self.far + o, self.fars)
        return i, self.at(d=i * self.fold + lax.rem(self.d, self.fold))

    def axis(self, name):
        if name == "core":
            return self.core, 2, lambda o: (1 - self.core, self.at(b=2 * self.x + 1 - self.core))
        if name == "wide":
            def peer(o):
                i = lax.rem(self.x + o, self.wide)
                return i, self.at(b=2 * i + self.core)
            return self.x, self.wide, peer
        if name == "low":
            def peer(o):
                i = lax.rem(self.lo + o, self.low)
                return i, self.at(d=self.hi * self.low + i)
            return self.lo, self.low, peer

        if name == "plane":
            own = self.x * self.low + self.lo

            def peer(o):
                i = lax.rem(own + o, self.wide * self.low)
                b = 2 * lax.div(i, self.low) + self.core
                return i, self.at(b=b, d=self.hi * self.low + lax.rem(i, self.low))
            return own, self.wide * self.low, peer

        def peer(o):
            i = lax.rem(self.hi + o, self.high)
            return i, self.at(d=i * self.low + self.lo)
        return self.hi, self.high, peer


def remote(src, dst, sems, index, device):
    send, recv = sems
    return pltpu.make_async_remote_copy(
        src_ref=src,
        dst_ref=dst,
        send_sem=send.at[index],
        recv_sem=recv.at[index],
        device_id=device,
        device_id_type=MESH,
    )


def wait_all(copied, sems, index, device):
    remote(copied, copied, sems, index, device).wait()


class SmallSum:
    def __init__(self, place, near, far, total, near_sems, far_sems):
        self.place, self.near, self.far, self.total = place, near, far, total
        self.near_sems, self.far_sems = near_sems, far_sems

    def own(self, m):
        return self.near.at[m, self.place.near]

    def near_copies(self, m):
        mine = self.near.at[m, self.place.near]
        return [
            remote(mine, mine, self.near_sems, m, self.place.near_peer(o)[1])
            for o in range(1, self.place.nears)
        ]

    def far_copies(self, m):
        mine = self.far.at[m, self.place.far]
        return [
            remote(mine, mine, self.far_sems, m, self.place.far_peer(o)[1])
            for o in range(1, self.place.fars)
        ]

    def start(self, m):
        for copy in self.near_copies(m):
            copy.start()

    def forward(self, m):
        place = self.place
        wait_all(self.near.at[m, pl.ds(0, place.nears - 1)], self.near_sems, m, place.near_peer(1)[1])
        self.far[m, self.place.far] = sum(self.near[m, i] for i in range(self.place.nears))
        for copy in self.far_copies(m):
            copy.start()

    def finish(self, m):
        place = self.place
        wait_all(self.far.at[m, pl.ds(0, place.fars - 1)], self.far_sems, m, place.far_peer(1)[1])
        self.total[m] = sum(self.far[m, i] for i in range(self.place.fars))


class TableSum:
    def __init__(self, place, table, near, far, total, near_sems, far_sems, back_sems):
        self.place, self.table, self.near, self.far, self.total = place, table, near, far, total
        self.near_sems, self.far_sems, self.back_sems = near_sems, far_sems, back_sems
        self.rows = table.shape[1] // place.nears

    def share(self, i):
        return pl.ds(pl.multiple_of(i * self.rows, 8), self.rows)

    def near_copies(self, m):
        mine = self.near.at[m, self.place.near]
        copies = []
        for o in range(1, self.place.nears):
            i, device = self.place.near_peer(o)
            copies.append(remote(self.table.at[m, self.share(i)], mine, self.near_sems, m, device))
        return copies

    def far_copies(self, m):
        mine = self.far.at[m, self.place.far]
        return [
            remote(mine, mine, self.far_sems, m, self.place.far_peer(o)[1])
            for o in range(1, self.place.fars)
        ]

    def back_copies(self, m):
        mine = self.total.at[m, self.share(self.place.near)]
        return [
            remote(mine, mine, self.back_sems, m, self.place.near_peer(o)[1])
            for o in range(1, self.place.nears)
        ]

    def start(self, m):
        for copy in self.near_copies(m):
            copy.start()
        self.near[m, self.place.near] = self.table[m, self.share(self.place.near)]

    def forward(self, m):
        place = self.place
        wait_all(self.near.at[m, pl.ds(0, place.nears - 1)], self.near_sems, m, place.near_peer(1)[1])
        self.far[m, self.place.far] = sum(self.near[m, i] for i in range(self.place.nears))
        for copy in self.far_copies(m):
            copy.start()

    def back(self, m):
        place = self.place
        wait_all(self.far.at[m, pl.ds(0, place.fars - 1)], self.far_sems, m, place.far_peer(1)[1])
        self.total[m, self.share(self.place.near)] = sum(self.far[m, i] for i in range(self.place.fars))
        for copy in self.back_copies(m):
            copy.start()

    def finish(self, m):
        place = self.place
        rows = self.total.at[m, pl.ds(0, (place.nears - 1) * self.rows)]
        wait_all(rows, self.back_sems, m, place.near_peer(1)[1])


class GradSum:
    def __init__(self, place, part, total, stages, sems, orders):
        self.part, self.total, self.stages, self.sems = part, total, stages, sems
        half = part.shape[0] // 2
        core = place.axis("core")
        self.steps = [[(core, 0, half, 0)]] + [[] for _ in orders[0]]
        slot = 1
        for h, order in enumerate(orders):
            size = half // len(orders)
            start = core[0] * half + h * size
            for i, name in enumerate(order):
                axis = place.axis(name)
                self.shared = i == len(order) - 1 and size % (16 * axis[1]) != 0
                if not self.shared:
                    size = size // axis[1]
                self.steps[i + 1].append((axis, start, size, slot))
                start = start + axis[0] * size
                slot += 1

    @staticmethod
    def stage_shapes(rows, columns, orders, sizes):
        shapes = [(1, rows // 2, columns)]
        for order in orders:
            size = rows // 2 // len(orders)
            for i, name in enumerate(order):
                n = sizes[name]
                if i == len(order) - 1 and size % (16 * n):
                    shapes.append((n, size, columns))
                else:
                    size //= n
                    shapes.append((n - 1, size, columns))
            assert size % 16 == 0
        return shapes

    def rows(self, base, size, index):
        return pl.ds(pl.multiple_of(base + index * size, 16), size)

    def whole(self, step):
        return self.shared and step == len(self.steps) - 1

    def down(self, step):
        copies = []
        for (own, n, peer), base, size, slot in self.steps[step]:
            for o in range(1, n):
                i, device = peer(o)
                if self.whole(step):
                    src, dst = self.part.at[self.rows(base, size, 0)], self.stages[slot].at[own]
                else:
                    src, dst = self.part.at[self.rows(base, size, i)], self.stages[slot].at[o - 1]
                copies.append(remote(src, dst, self.sems[:2], slot, device))
        return copies

    def up(self, step):
        copies = []
        for (own, n, peer), base, size, slot in [] if self.whole(step) else self.steps[step]:
            mine = self.total.at[self.rows(base, size, own)]
            for o in range(1, n):
                copies.append(remote(mine, mine, self.sems[2:], slot, peer(o)[1]))
        return copies

    def start_down(self, step):
        for copy in self.down(step):
            copy.start()

    def end_down(self, step, less=None):
        last = step == len(self.steps) - 1
        for (own, n, peer), base, size, slot in self.steps[step]:
            wait_all(self.stages[slot].at[pl.ds(0, n - 1)], self.sems[:2], slot, peer(1)[1])
            piece = min(size, 64)
            if self.whole(step):
                rows = self.rows(base, size, 0)
                self.stages[slot][own] = self.part[rows]
                self.total[rows] = sum(self.stages[slot][i].astype(F32) for i in range(n)).astype(BF16)
                continue

            def add(i, carry):
                rows = pl.ds(pl.multiple_of(base + own * size + i * piece, 16), piece)
                there = pl.ds(pl.multiple_of(i * piece, 16), piece)
                total = self.part[rows].astype(F32)
                for o in range(1, n):
                    total = total + self.stages[slot][o - 1, there].astype(F32)
                if less is not None:
                    total = total - less
                (self.total if last else self.part)[rows] = total.astype(BF16)
                return carry

            lax.fori_loop(0, size // piece, add, 0)

    def start_up(self, step):
        for copy in self.up(step):
            copy.start()

    def end_up(self, step):
        for (own, n, peer), base, size, slot in [] if self.whole(step) else self.steps[step]:
            rows = self.total.at[pl.ds(pl.multiple_of(base, 16), (n - 1) * size)]
            wait_all(rows, self.sems[2:], slot, peer(1)[1])

    def advance(self, stage, less=None):
        last = len(self.steps) - 1
        if stage <= last:
            self.end_down(stage, less if stage == last else None)
            if stage < last:
                self.start_down(stage + 1)
            else:
                self.start_up(last)
        else:
            step = 2 * last + 1 - stage
            self.end_up(step)
            if step:
                self.start_up(step - 1)


def plan(groups, dps, hops, width):
    wide, low, high = groups // 2, dps // 4, 4
    early = groups * LANES == width and 2 * wide * low * high * 16 == hops * LANES
    parts = 2 if hops % 2 == 0 and hops * width % (2 * 4 * wide * low * high * 16) == 0 else 1
    return early, parts


def make_kernel(dims):
    (groups, dps, batches, nodes, hops, feats, width, classes) = dims
    pieces = width // LANES
    tables = hops * groups
    nodes_batch = nodes * groups * dps
    total_nodes = batches * nodes_batch
    chunk = 64
    final = batches - 1
    early, mid_parts = plan(groups, dps, hops, width)
    bands = LANES // 16
    lane = [slice(j * LANES, (j + 1) * LANES) for j in range(pieces)]
    columns = [slice(k * width, (k + 1) * width) for k in range(hops)]

    def kernel(
        x_in, bucket_ref, mask_ref, labels_ref, w_in, gain_ref, shift_ref, slope_ref, slope_cat_ref, w_mid_in,
        gain_mid_ref, shift_mid_ref, slope_mid_ref, w_out_in, bias_in,
        out_features, out_mid, out_rest, out_small,
        spread, u_ref, join_ref, xt_ref, cat_ref, w_shift_ref, mid_ref, dshaped_ref, dmid_ref, grad_hops_ref, grad_out_ref,
        w_ref, w_mid_ref, w_out_ref, bias_ref, gain_rep, shift_rep, tab_a, tab_b, tab_e, tab_f, slopes_ref,
        table, table_near, table_far, t_total, s_near, s_far, s_total, e_near, e_far, e_total, c_near, c_far, c_total,
        part_mid, total_mid, part_rest, total_rest, stages_mid, stages_rest, gram_own, scale_own, level_own, stages_gram,
        t_sems, s_sems, e_sems, c_sems, d_sems, mid_sems, rest_sems, gram_sems, in_sems, out_sems, file_sems,
    ):
        spread_rows = feats * pieces * hops
        place = Place(groups, dps)
        barrier = pltpu.get_barrier_semaphore()
        for o in range(1, place.nears):
            pl.semaphore_signal(barrier, inc=1, device_id=place.near_peer(o)[1], device_id_type=MESH)
        for o in range(1, place.fars):
            pl.semaphore_signal(barrier, inc=1, device_id=place.far_peer(o)[1], device_id_type=MESH)

        def landing(ref, m):
            return ref.at[pl.ds(0, spread_rows), pl.ds(pl.multiple_of(m * LANES, LANES), LANES)]

        def x_copy(m):
            return pltpu.make_async_copy(x_in.at[m], landing(part_mid, m), in_sems.at[m])

        w_copy = pltpu.make_async_copy(w_in, landing(total_mid, 0), file_sems.at[1])
        w_mid_copy = pltpu.make_async_copy(w_mid_in, w_mid_ref, file_sems.at[2])
        w_copy.start()
        for m in range(batches):
            x_copy(m).start()
        w_mid_copy.start()

        stats = TableSum(place, table, table_near, table_far, t_total, t_sems[0:2], t_sems[2:4], t_sems[4:6])
        heads = SmallSum(place, s_near, s_far, s_total, s_sems[0:2], s_sems[2:4])
        backs = SmallSum(place, e_near, e_far, e_total, e_sems[0:2], e_sems[2:4])
        dots = TableSum(place, table, table_near, table_far, t_total, d_sems[0:2], d_sems[2:4], d_sems[4:6])
        amounts = SmallSum(place, c_near, c_far, c_total, c_sems[0:2], c_sems[2:4])
        mid_rows = [pl.ds(i * hops * width // mid_parts, hops * width // mid_parts) for i in range(mid_parts)]
        mids = [
            GradSum(place, part_mid.at[rows], total_mid.at[rows], stages_mid[i], mid_sems[i], MID_ORDERS)
            for i, rows in enumerate(mid_rows)
        ]
        if early:
            gram_rows = [pl.ds(m * hops * LANES, hops * LANES) for m in range(batches)]
            grams = [
                GradSum(place, part_mid.at[rows], part_mid.at[rows], stages_gram[m], gram_sems[m], REST_ORDERS)
                for m, rows in enumerate(gram_rows)
            ]
            owned = (place.core * place.wide * place.low + place.axis("plane")[0]) * place.high + place.hi
            owned_hop = lax.div(owned, bands)

        def mid_step(i, stage):
            if i < mid_parts:
                mids[i].advance(stage)
        rests = GradSum(place, part_rest, total_rest, stages_rest, rest_sems, REST_ORDERS)

        def loop(first, last, body):
            def step(m, carry):
                body(m)
                return carry

            lax.fori_loop(first, last, step, 0)

        def at(m, when, body):
            pl.when(m == when)(body)

        spread[spread_rows:] = jnp.zeros((spread.shape[0] - spread_rows, LANES), F32)

        def hop_rows(k):
            parts = [spread[pl.ds(j * hops + k, HOT, stride=pieces * hops)] for j in range(pieces)]
            return jnp.concatenate(parts, axis=1)

        w_copy.wait()
        spread[:spread_rows] = landing(total_mid, 0)[...].astype(F32)
        for k in range(hops):
            w_ref[k] = jnp.concatenate([hop_rows(k), jnp.zeros((LANES - HOT, width), F32)], axis=0).astype(BF16)
            w_shift_ref[k] = w_ref[k]
            for g in range(groups):
                gain_rep[k * groups + g : k * groups + g + 1] = gain_ref[k : k + 1]
                shift_rep[k * groups + g : k * groups + g + 1] = shift_ref[k : k + 1]
        grad_out_ref[...] = jnp.zeros_like(grad_out_ref)
        grad_out_ref[:classes] = w_out_in[...].astype(F32)
        w_out_ref[...] = grad_out_ref[...].astype(BF16)
        bias_ref[...] = jnp.full(bias_ref.shape, -1e30, F32)
        bias_ref[0:1, :classes] = bias_in[...]
        bias_row = jnp.broadcast_to(bias_ref[0:1], (LANES, LANES))
        bias_ref[...] = jnp.transpose(bias_row)[: bias_ref.shape[0]]
        grad_hops_ref[...] = jnp.zeros_like(grad_hops_ref)
        grad_out_ref[...] = jnp.zeros_like(grad_out_ref)
        slopes_ref[...] = jnp.zeros_like(slopes_ref)

        def hot_rows(m):
            ids = lax.rem(lax.broadcasted_iota(jnp.int32, (LANES - HOT, nodes), 0), 8)
            return (ids == bucket_ref[m]).astype(F32)

        def active_row(m, k):
            if k == 0:
                return jnp.ones((1, nodes), F32)
            return mask_ref[k - 1, pl.ds(m, 1)].astype(F32)

        which = lax.broadcasted_iota(jnp.int32, (groups, LANES), 1)
        amount = [jnp.zeros((groups, LANES), F32) for _ in range(hops)]
        for m in range(batches):
            hot = hot_rows(m)
            for k in range(hops):
                here = jnp.sum(hot * active_row(m, k), axis=1, keepdims=True)
                amount[k] = jnp.where(which == m, here[:groups], amount[k])
        for k in range(hops):
            c_near[0, place.near, k * groups : (k + 1) * groups] = amount[k]

        def by_node(row):
            return jnp.transpose(jnp.broadcast_to(row, (LANES, nodes)))

        def moments(m):
            x_copy(m).wait()
            spread[:spread_rows] = landing(part_mid, m)[...].astype(F32)
            hot_all = hot_rows(m)
            cat_ref[m] = by_node(bucket_ref[m].astype(F32)).astype(BF16)
            for k in range(hops):
                block = jnp.concatenate([hop_rows(k), hot_all], axis=0) * active_row(m, k)
                xt = block.astype(BF16)
                hot = xt[HOT:]
                xt_ref[m, k] = xt
                pre = dot(xt, w_ref[k], TN)
                square = (pre * pre).astype(BF16)
                second = dot(hot, square)
                sums = jnp.concatenate(split_high(dot(hot, xt, NT)), axis=1)
                first = dot(sums, jnp.concatenate([w_ref[k], w_ref[k]], axis=0))
                for j in range(pieces):
                    base = 2 * tables * j + k * groups
                    table[m, base : base + groups] = first[:groups, lane[j]]
                    table[m, base + tables : base + tables + groups] = second[:groups, lane[j]]

        def moments_step(m):
            moments(m)

            @pl.when(m == 0)
            def _():
                pl.semaphore_wait(barrier, place.nears + place.fars - 2)
                amounts.start(0)

            stats.start(m)
            at(m, 2, lambda: amounts.forward(0))
            pl.when(m >= 2)(lambda: stats.forward(m - 2))

        loop(0, batches, moments_step)

        def gram(m):
            for k in range(hops):
                xt = xt_ref[m, k]
                masked = [xt[:HOT] * xt[HOT + g : HOT + g + 1] for g in range(groups)]
                here = dot(jnp.concatenate(masked, axis=0), xt, NT)
                by_bucket = [here[g * HOT : (g + 1) * HOT] for g in range(groups)]
                block = jnp.concatenate(by_bucket, axis=1)
                block = jnp.concatenate([block, jnp.zeros((LANES - HOT, width), F32)], axis=0)
                start = pl.multiple_of((m * hops + k) * LANES, LANES)
                part_mid[pl.ds(start, LANES)] = block.astype(BF16)

        def end_gram(m):
            grams[m].end_down(2)
            rows = pl.multiple_of(m * hops * LANES + owned * 16, 16)
            gram_own[m * 16 : (m + 1) * 16] = part_mid[pl.ds(rows, 16)]

        def gram_step(m):
            if early:
                gram(m)
                for i in range(batches):
                    at(m, i, lambda i=i: grams[i].start_down(0))

            @pl.when(m == 0)
            def _():
                stats.forward(final - 1)
                stats.back(0)

            @pl.when(m == 1)
            def _():
                stats.forward(final)
                stats.back(1)

        loop(0, batches, gram_step)
        if early:
            grams[0].advance(0)
        amounts.finish(0)
        w_mid_copy.wait()
        stats.back(final - 1)
        stats.finish(0)

        def counts_of(m):
            here = lax.broadcasted_iota(jnp.int32, (tables, LANES), 1) == m
            counts = jnp.sum(jnp.where(here, c_total[0], 0.0), axis=1, keepdims=True)
            return jnp.broadcast_to(counts, (tables, LANES))

        def bucket_tables(m):
            counts = counts_of(m)
            for j in range(pieces):
                base = 2 * tables * j
                mean = t_total[m, base : base + tables] / counts
                second = t_total[m, base + tables : base + 2 * tables] / counts
                inv = lax.rsqrt(second - mean * mean + EPSILON)
                a = 0.5 * gain_rep[:, lane[j]] * inv
                tab_a[m, :, lane[j]] = a
                tab_b[m, :, lane[j]] = 0.5 * shift_rep[:, lane[j]] - a * mean
                high, low = split_high(0.5 * shift_rep[:, lane[j]] / a - mean)
                for k in range(hops):
                    rows = slice(k * groups, (k + 1) * groups)
                    parts = []
                    for part in (high, low):
                        parts.append(part[rows].astype(F32))
                        if groups < 8:
                            parts.append(jnp.zeros((8 - groups, LANES), F32))
                    w_shift_ref[k, HOT:, lane[j]] = jnp.concatenate(parts, axis=0).astype(BF16)

        def choose(masks, values, k, j):
            result = values[k * groups + groups - 1 : k * groups + groups, lane[j]]
            for g in range(groups - 2, -1, -1):
                result = jnp.where(masks[g], values[k * groups + g : k * groups + g + 1, lane[j]], result)
            return result

        def masks_of(m, rows):
            cat = cat_ref[m, rows].astype(F32)
            return [cat == float(g) for g in range(groups - 1)]

        projected = [dshaped_ref.at[final], dshaped_ref.at[final - 1]]

        halves = [slice(0, nodes // 2), slice(nodes // 2, nodes)]
        chunks = [slice(i * chunk, (i + 1) * chunk) for i in range(nodes // chunk)]

        def put_beside(beside, i):
            for n, body in enumerate(beside):
                if i == n * len(chunks) // len(beside):
                    body()

        def forward(m):
            bucket_tables(m)

            def projection(k, rows):
                projected[k % 2][rows] = dot(xt_ref[m, k, :, rows], w_shift_ref[k], TN)

            def product(k, rows):
                middle = dot(join_ref[m, rows, columns[k]], w_mid_ref[columns[k]])
                mid_ref[m, rows] = middle if k == 0 else mid_ref[m, rows] + middle

            for rows in halves:
                projection(0, rows)
            for k in range(hops):
                beside = [functools.partial(projection, k + 1, rows) for rows in halves] if k + 1 < hops else []
                beside += [functools.partial(product, k - 1, rows) for rows in halves] if k else []
                for i, rows in enumerate(chunks):
                    put_beside(beside, i)
                    masks = masks_of(m, rows)
                    for j in range(pieces):
                        bend = 0.5 - 0.5 * slope_ref[k : k + 1, lane[j]]
                        bend_cat = 0.5 - 0.5 * slope_cat_ref[:, k * width + j * LANES : k * width + (j + 1) * LANES]
                        scale = choose(masks, tab_a.at[m], k, j)
                        u = projected[k % 2][rows, lane[j]] * scale
                        u_ref[m, k, rows, lane[j]] = u
                        half = u - (bend * u) * (1.0 - jnp.tanh(u))
                        half = half - (bend_cat * half) * (1.0 - jnp.tanh(half))
                        join_ref[m, rows, k * width + j * LANES : k * width + (j + 1) * LANES] = half.astype(BF16)
            for rows in halves:
                product(hops - 1, rows)
            middle = mid_ref[m]
            first = jnp.sum(middle, axis=0, keepdims=True)
            second = jnp.sum(middle * middle, axis=0, keepdims=True)
            own = heads.own(m)
            for j in range(pieces):
                own[j : j + 1] = first[:, lane[j]]
                own[pieces + j : pieces + j + 1] = second[:, lane[j]]

        def row_of(ref, m, first):
            return jnp.concatenate([ref[m, first + j : first + j + 1] for j in range(pieces)], axis=1)

        def head_scale(m):
            mean = row_of(s_total, m, 0) * (1.0 / nodes_batch)
            second = row_of(s_total, m, pieces) * (1.0 / nodes_batch)
            inv = lax.rsqrt(4.0 * (second - mean * mean) + EPSILON)
            return mean, inv

        def head(m):
            heads.finish(m)
            mean, inv = head_scale(m)
            scale = gain_mid_ref[...] * inv
            offset = 0.5 * shift_mid_ref[...] - scale * mean
            slope = slope_mid_ref[...]
            u = mid_ref[m] * scale + offset
            mid_ref[m] = u
            tanh = jnp.tanh(u)
            gap = u * (1.0 - tanh)
            outer = (2.0 * u - (1.0 - slope) * gap).astype(BF16)
            logits = dot(w_out_ref[...], outer, NT) + bias_ref[:, 0:1]
            top = jnp.max(logits, axis=0, keepdims=True)
            powers = jnp.exp(logits - top)
            total = jnp.sum(powers, axis=0, keepdims=True)
            wanted = (lax.broadcasted_iota(jnp.int32, logits.shape, 0) == labels_ref[pl.ds(m, 1)]).astype(F32)
            loss = jnp.log(total) + top - jnp.sum(logits * wanted, axis=0, keepdims=True)
            dlogits = (powers / total - wanted) * (1.0 / total_nodes)
            low = dlogits.astype(BF16)
            grad_out_ref[...] += dot(low, outer)
            douter = dot(low, w_out_ref[...], TN)
            grad_slope = jnp.sum(douter * gap, axis=0, keepdims=True)
            dshaped = douter * (slope + (0.5 - 0.5 * slope) * (1.0 + tanh) * (1.0 + gap))
            dshaped_ref[m] = dshaped
            head_sum = jnp.sum(dshaped, axis=0, keepdims=True)
            head_dot = jnp.sum(dshaped * u, axis=0, keepdims=True)
            own = backs.own(m)
            for j in range(pieces):
                own[j : j + 1] = head_sum[:, lane[j]]
                own[pieces + j : pieces + j + 1] = head_dot[:, lane[j]]
                own[2 * pieces + j : 2 * pieces + j + 1] = grad_slope[:, lane[j]]
            folded = sum(dlogits[:, i * LANES : (i + 1) * LANES] for i in range(nodes // LANES))
            square = jnp.concatenate([folded, jnp.zeros((LANES - folded.shape[0], LANES), F32)], axis=0)
            own[3 * pieces : 3 * pieces + 1] = jnp.sum(jnp.transpose(square), axis=0, keepdims=True)
            own[3 * pieces + 1 : 3 * pieces + 2] = sum(
                loss[:, i * LANES : (i + 1) * LANES] for i in range(nodes // LANES)
            )
            own[3 * pieces + 2 :] = jnp.zeros((own.shape[0] - 3 * pieces - 2, LANES), F32)
            backs.start(m)

        def head_grads(m):
            inv = head_scale(m)[1]
            head_sum = row_of(e_total, m, 0)
            head_dot = (2.0 * row_of(e_total, m, pieces) - shift_mid_ref[...] * head_sum) / gain_mid_ref[...]
            return inv, head_sum, head_dot

        def back_head(m):
            backs.finish(m)
            inv, head_sum, head_dot = head_grads(m)
            scale = gain_mid_ref[...] * inv
            tilt = 2.0 * inv * head_dot * (1.0 / nodes_batch)
            level = scale * head_sum * (1.0 / nodes_batch) - 0.5 * shift_mid_ref[...] * tilt
            dmid_ref[m] = (scale * dshaped_ref[m] - level - mid_ref[m] * tilt).astype(BF16)

        gradients = [mid_ref.at[0], dshaped_ref.at[0]]

        def products(k):
            return (part_rest, total_rest)[k % 2].at[pl.ds(0, nodes)]

        def backward(m, which_hops, target, tick):
            def into(k, rows):
                gradients[k % 2][rows] = dot(dmid_ref[m, rows], w_mid_ref[columns[k]], NT)

            def bucket_sums(k):
                first_sums(k)
                second_sums(k)

            def first_sums(k):
                hot = xt_ref[m, k, HOT:LANES]
                if early:
                    both = dot(xt_ref[m, k], target(k)[...])
                    grad_hops_ref[k, :HOT] += 2.0 * both[:HOT]
                    first = both[HOT:]
                else:
                    first = dot(hot, target(k)[...])
                for j in range(pieces):
                    base = 2 * tables * j + k * groups
                    table[m, base : base + groups] = first[:groups, lane[j]]

            def second_sums(k):
                second = dot(xt_ref[m, k, HOT:LANES], products(k)[...])
                for j in range(pieces):
                    base = 2 * tables * j + k * groups
                    table[m, base + tables : base + tables + groups] = second[:groups, lane[j]]

            for rows in halves:
                into(which_hops[0], rows)
            for k in which_hops:
                beside = [functools.partial(into, k + 1, rows) for rows in halves] if k + 1 in which_hops else []
                beside += [functools.partial(f, k - 1) for f in (first_sums, second_sums)] if k - 1 in which_hops else []
                slope_sums = [jnp.zeros((8, LANES), F32) for _ in range(2 * pieces)]
                result = target(k)
                for i, rows in enumerate(chunks):
                    put_beside(beside, i)
                    masks = masks_of(m, rows)
                    for j in range(pieces):
                        slope = slope_ref[k : k + 1, lane[j]]
                        slope_cat = slope_cat_ref[:, k * width + j * LANES : k * width + (j + 1) * LANES]
                        bend, bend_cat = 0.5 - 0.5 * slope, 0.5 - 0.5 * slope_cat
                        u = u_ref[m, k, rows, lane[j]]
                        tanh = jnp.tanh(u)
                        gap = (bend * u) * (1.0 - tanh)
                        half = u - gap
                        tanh_cat = jnp.tanh(half)
                        gap_cat = (bend_cat * half) * (1.0 - tanh_cat)
                        grad = gradients[k % 2][rows, lane[j]]
                        slope_sums[pieces + j] += jnp.sum((grad * gap_cat).reshape(-1, 8, LANES), axis=0)
                        grad = grad * (slope_cat + (1.0 + tanh_cat) * (bend_cat + gap_cat))
                        slope_sums[j] += jnp.sum((grad * gap).reshape(-1, 8, LANES), axis=0)
                        grad = grad * (slope + (1.0 + tanh) * (bend + gap))
                        grad = grad * choose(masks, tab_a.at[m], k, j)
                        result[rows, lane[j]] = grad.astype(BF16)
                        products(k)[rows, lane[j]] = (grad * u).astype(BF16)
                for j in range(pieces):
                    slope = slope_ref[k : k + 1, lane[j]]
                    slope_cat = slope_cat_ref[:, k * width + j * LANES : k * width + (j + 1) * LANES]
                    for s, values in enumerate((slope, slope_cat)):
                        grad_hops_ref[k, feats + s : feats + s + 1, lane[j]] += jnp.sum(
                            slope_sums[s * pieces + j], axis=0, keepdims=True
                        ) / (0.5 - 0.5 * values)
                if k == which_hops[-1]:
                    bucket_sums(k)
                tick(k)

        def first_target(k):
            return total_mid.at[pl.ds(k * nodes, nodes)]

        def first_copy(k):
            return pltpu.make_async_copy(first_target(k), join_ref.at[0, :, pl.ds(k * width, width)], in_sems.at[k])

        def no_tick(k):
            pass

        def forward_step(m):
            pl.when(m >= 1)(lambda: stats.finish(m))
            forward(m)
            heads.start(m)
            pl.when(m >= 1)(lambda: heads.forward(m - 1))
            at(m, 0, lambda: stats.back(final))
            if early:
                at(m, 3, lambda: end_gram(0))
                for i in range(2, final + 1):
                    at(m, i, lambda i=i: grams[i - 2].advance(1))
                for i in range(1, final + 1):
                    at(m, i - 1, lambda i=i: grams[i].advance(0))
            at(m, 2, lambda: head(0))

        loop(0, batches, forward_step)
        backs.forward(0)

        def head_step(m):
            head(m)

            @pl.when(m == 1)
            def _():
                heads.forward(final)
                if early:
                    grams[2].advance(1)
                    end_gram(1)

            @pl.when(m == 2)
            def _():
                backs.forward(1)
                back_head(0)
                backward(0, [0, 1], first_target, no_tick)
                if early:
                    grams[final].advance(1)
                    end_gram(2)

        loop(1, batches, head_step)
        backs.forward(2)
        if early:
            end_gram(final)

        def late_tick(k):
            if k == hops - 1:
                backs.forward(final)

        backward(0, list(range(2, hops)), first_target, late_tick)
        dots.start(0)
        for m in range(1, final):
            back_head(m)

        held = [mid_ref.at[m] for m in range(final)] + [dshaped_ref.at[0]]
        for k in range(hops):
            held[k][...] = sum(dot(join_ref[m, :, columns[k]], dmid_ref[m], TN) for m in range(final))
        back_head(final)
        for k in range(hops):
            total = held[k][...] + dot(join_ref[final, :, columns[k]], dmid_ref[final], TN)
            part_mid[columns[k]] = (2.0 * total).astype(BF16)
            if (k + 1) * mid_parts % hops == 0:
                mids[(k + 1) * mid_parts // hops - 1].start_down(0)
        for k in range(hops):
            first_copy(k).start()
        dots.forward(0)

        def wait_first():
            for k in range(hops):
                first_copy(k).wait()

        ticks = {
            (1, 0): [wait_first],
            (1, 1): [lambda: mid_step(0, 0)],
            (1, 2): [lambda: mid_step(1, 0), lambda: dots.back(0)],
            (2, 0): [lambda: mid_step(0, 1)],
            (2, 2): [lambda: mid_step(1, 1), lambda: dots.forward(1)],
            (2, 3): [lambda: mid_step(0, 2)],
            (3, 0): [lambda: mid_step(1, 2)],
            (3, 1): [lambda: dots.back(1)],
            (3, 2): [lambda: dots.forward(2)],
            (3, 3): [lambda: mid_step(0, 3)],
        }

        def backward_step(m):
            def tick(k):
                for when, bodies in ticks.items():
                    if when[1] == k:
                        for body in bodies:
                            at(m, when[0], body)

            backward(m, list(range(hops)), lambda k: join_ref.at[m, :, columns[k]], tick)
            dots.start(m)

        loop(1, batches, backward_step)

        def last_tables(m):
            counts = counts_of(m)
            for j in range(pieces):
                base = 2 * tables * j
                a = tab_a[m, :, lane[j]]
                inv = 2.0 * a / gain_rep[:, lane[j]]
                shift = shift_rep[:, lane[j]]
                scaled = t_total[m, base : base + tables]
                bucket_sum = scaled / a
                bucket_dot = (2.0 * t_total[m, base + tables : base + 2 * tables] / a - shift * bucket_sum) / gain_rep[
                    :, lane[j]
                ]
                tilt = inv * bucket_dot / counts
                tab_f[:, lane[j]] = tilt
                tab_e[:, lane[j]] = scaled / counts - 0.5 * shift * tilt
                for k in range(hops):
                    here = slice(k * groups, (k + 1) * groups)
                    slopes_ref[k : k + 1, lane[j]] += jnp.sum(bucket_dot[here], axis=0, keepdims=True)
                    slopes_ref[hops + k : hops + k + 1, lane[j]] += jnp.sum(bucket_sum[here], axis=0, keepdims=True)

        def own_tables(m):
            for k in range(hops):
                rows = slice(k * groups, (k + 1) * groups)

                @pl.when(owned_hop == k)
                def _(rows=rows):
                    tilt = tab_f[rows]
                    scale_own[m] = tilt * tab_a[m, rows]
                    level_own[m] = tab_e[rows] + tilt * tab_b[m, rows]

        def last(m):
            dots.finish(m)
            last_tables(m)
            if early:
                own_tables(m)
                at(m, final, lambda: rests.advance(2, correction()))

            def weights(k):
                grad_hops_ref[k, :HOT] += dot(xt_ref[m, k, :HOT], join_ref[m, :, columns[k]]) * 2.0

            for k in range(hops):
                if k and not early:
                    weights(k - 1)
                for rows in chunks:
                    masks = masks_of(m, rows)
                    for j in range(pieces):
                        here = slice(k * width + j * LANES, k * width + (j + 1) * LANES)
                        grad = join_ref[m, rows, here].astype(F32) - choose(masks, tab_e, k, j)
                        grad = grad - choose(masks, tab_f, k, j) * u_ref[m, k, rows, lane[j]]
                        join_ref[m, rows, here] = grad.astype(BF16)
            if not early:
                weights(hops - 1)

        def correction():
            total = jnp.zeros((16, width), F32)
            weights = w_ref[owned_hop].astype(F32)
            row = lax.broadcasted_iota(jnp.int32, (LANES, width), 0)
            for m in range(batches):
                scaled = [
                    jnp.where(row == HOT + g, level_own[m, g : g + 1], weights * scale_own[m, g : g + 1]).astype(BF16)
                    for g in range(groups)
                ]
                total = total + dot(gram_own[m * 16 : (m + 1) * 16], jnp.concatenate(scaled, axis=0))
            return 2.0 * total

        def features_copy(m):
            return pltpu.make_async_copy(spread.at[pl.ds(0, spread_rows)], out_features.at[m], out_sems.at[m])

        def features(m):
            pl.when(m >= 1)(lambda: features_copy(m - 1).wait())
            for k in range(hops):
                scale = active_row(m, k) * float(2 * total_nodes)
                values = dot(w_ref[k], join_ref[m, :, columns[k]], NT) * scale
                for j in range(pieces):
                    spread[pl.ds(j * hops + k, feats, stride=pieces * hops)] = values[:feats, lane[j]]
            features_copy(m).start()

        def start_rests():
            rows = grad_out_ref.shape[0] // hops
            for k in range(hops):
                grad_hops_ref[k, SPARE : SPARE + rows] = grad_out_ref[k * rows : (k + 1) * rows]
                part_rest[k * LANES : (k + 1) * LANES] = grad_hops_ref[k].astype(BF16)
            if part_rest.shape[0] > hops * LANES:
                part_rest[hops * LANES :] = jnp.zeros((part_rest.shape[0] - hops * LANES, width), BF16)
            rests.start_down(0)

        def last_step(m):
            last(m)

            @pl.when(m == 0)
            def _():
                if early:
                    rests.advance(0)
                dots.back(2)
                mid_step(1, 3)

            at(m, 1, lambda: mid_step(0, 4))
            at(m, 2, lambda: mid_step(0, 5))

            @pl.when(m == 3)
            def _():
                if not early:
                    start_rests()

            features(m)
            at(m, 0, lambda: dots.forward(final))

            @pl.when(m == 1)
            def _():
                dots.back(final)
                if early:
                    rests.advance(1)
                mid_step(1, 4)

            at(m, 2, lambda: mid_step(1, 5))
            at(m, 3, lambda: mid_step(0, 6))

        if early:
            start_rests()
        loop(0, batches, last_step)
        if not early:
            for stage in range(3):
                rests.advance(stage)

        grad_gain = jnp.zeros((1, width), F32)
        grad_shift = jnp.zeros((1, width), F32)
        grad_slope = jnp.zeros((1, width), F32)
        bias_loss = jnp.zeros((2, LANES), F32)
        for m in range(batches):
            _, head_sum, head_dot = head_grads(m)
            grad_gain = grad_gain + head_dot
            grad_shift = grad_shift + head_sum
            grad_slope = grad_slope + row_of(e_total, m, 2 * pieces)
            bias_loss = bias_loss + e_total[m, 3 * pieces : 3 * pieces + 2]
        out_small[: 2 * hops] = slopes_ref[...]
        loss = jnp.sum(bias_loss[1:2], axis=1, keepdims=True) * (1.0 / total_nodes)
        last_row = [bias_loss[0:1], jnp.broadcast_to(loss, (1, LANES)), jnp.zeros((1, width - 2 * LANES), F32)]
        for i, row in enumerate((grad_gain, grad_shift, grad_slope, jnp.concatenate(last_row, axis=1))):
            out_small[2 * hops + i : 2 * hops + i + 1] = row

        rests.advance(3)
        mid_step(1, 6)
        mid_step(0, 7)
        rests.advance(4)
        mid_step(1, 7)
        mid_file = pltpu.make_async_copy(total_mid, out_mid, file_sems.at[0])
        mid_file.start()
        rests.advance(5)
        rest_file = pltpu.make_async_copy(total_rest.at[pl.ds(0, hops * LANES)], out_rest, file_sems.at[1])
        rest_file.start()
        features_copy(final).wait()
        mid_file.wait()
        rest_file.wait()

    return kernel


def make_finish(dims):
    (groups, dps, batches, nodes, hops, feats, width, classes) = dims
    pieces = width // LANES
    spare = -(-classes // 16) * 16 // hops

    def kernel(
        features_in, mid_in, rest_in, small_in,
        features, mid, hops_grad, gain, shift, slope, cat, gain_mid, shift_mid, slope_mid, out_grad, bias, loss,
        low, wide, held, rest, spread, sems,
    ):
        rest_copy = pltpu.make_async_copy(rest_in, rest, sems.at[4, 0])
        spread_rows = feats * pieces * hops
        spread_copy = pltpu.make_async_copy(spread.at[pl.ds(0, spread_rows)], hops_grad, sems.at[4, 1])
        in_copy = [pltpu.make_async_copy(features_in.at[m], held.at[m], sems.at[0, m]) for m in range(batches)]
        out_copy = [pltpu.make_async_copy(held.at[m], features.at[m], sems.at[3, m]) for m in range(batches)]
        low_copy = [pltpu.make_async_copy(mid_in.at[pl.ds(k * width, width)], low.at[k], sems.at[1, k]) for k in range(hops)]
        wide_copy = [pltpu.make_async_copy(wide.at[k], mid.at[pl.ds(k * width, width)], sems.at[2, k]) for k in range(hops)]
        for copy in [rest_copy] + [c for pair in zip(in_copy, low_copy) for c in pair]:
            copy.start()
        rest_copy.wait()
        for k in range(hops):
            values = rest[k * LANES : (k + 1) * LANES].astype(F32)
            for j in range(pieces):
                spread[pl.ds(j * hops + k, feats, stride=pieces * hops)] = values[:feats, j * LANES : (j + 1) * LANES]
            slope[k : k + 1] = values[feats : feats + 1]
            cat[:, k * width : (k + 1) * width] = values[feats + 1 : feats + 2]
            count = min(spare, classes - k * spare)
            out_grad[k * spare : k * spare + count] = values[SPARE : SPARE + count]
        spread_copy.start()
        gain[...] = small_in[:hops]
        shift[...] = small_in[hops : 2 * hops]
        gain_mid[...] = small_in[2 * hops : 2 * hops + 1]
        shift_mid[...] = small_in[2 * hops + 1 : 2 * hops + 2]
        slope_mid[...] = small_in[2 * hops + 2 : 2 * hops + 3]
        bias[...] = small_in[2 * hops + 3 : 2 * hops + 4, :classes]
        loss[...] = small_in[2 * hops + 3 : 2 * hops + 4, LANES : LANES + 1]
        for i in range(max(batches, hops)):
            if i < batches:
                in_copy[i].wait()
                out_copy[i].start()
            if i < hops:
                low_copy[i].wait()
                wide[i] = low[i].astype(F32)
                wide_copy[i].start()
        for copy in wide_copy + out_copy + [spread_copy]:
            copy.wait()

    return kernel


def by_piece(values):
    *lead, feats, hops, width = values.shape
    values = jnp.swapaxes(values.reshape(*lead, feats, hops, width // LANES, LANES), -3, -2)
    return values.reshape(*lead, feats * hops * width // LANES, LANES)


def by_hop(rows, hops, pieces):
    *lead, count, _ = rows.shape
    values = rows.reshape(*lead, count // (hops * pieces), pieces, hops, LANES)
    return jnp.swapaxes(values, -3, -2).reshape(*lead, count // (hops * pieces), hops, pieces * LANES)


def shards(
    features,
    buckets,
    hop_mask,
    labels,
    w_hops,
    gain_hops,
    shift_hops,
    slope_hops,
    slope_cat,
    w_mid,
    gain_mid,
    shift_mid,
    slope_mid,
    w_out,
    bias_out,
):
    batches, nodes, hops, feats = features.shape
    width, classes = w_out.shape
    groups, dps = lax.axis_size("bucket"), lax.axis_size("dp")
    dims = (groups, dps, batches, nodes, hops, feats, width, classes)
    pieces = width // LANES
    joined_width = hops * width
    tables = hops * groups
    padded = -(-classes // 16) * 16

    wide, low, high = groups // 2, dps // 4, 4
    sizes = {"wide": wide, "low": low, "high": high, "plane": wide * low}
    rows_rest = max(hops * LANES, 2 * wide * low * 16)
    early, mid_parts = plan(groups, dps, hops, width)
    mid_shapes = GradSum.stage_shapes(joined_width // mid_parts, width, MID_ORDERS, sizes)
    gram_count = batches if early else 0
    own_rows = 16 * batches if early else 16
    rest_shapes = GradSum.stage_shapes(rows_rest, width, REST_ORDERS, sizes)
    _, nears, fars = Place.group_sizes(groups, dps)
    table_rows = 2 * tables * pieces
    share = table_rows // nears
    sem = pltpu.SemaphoreType.DMA

    def small_scratch(rows, copies=batches):
        return [
            pltpu.VMEM((copies, nears, rows, LANES), F32),
            pltpu.VMEM((copies, fars, rows, LANES), F32),
            pltpu.VMEM((copies, rows, LANES), F32),
        ]

    vmem = pl.BlockSpec(memory_space=pltpu.VMEM)
    hbm = pl.BlockSpec(memory_space=pl.ANY)

    def real(*shape):
        return jax.ShapeDtypeStruct(shape, F32)

    outs = pl.pallas_call(
        make_kernel(dims),
        name="train_step",
        out_shape=(
            real(batches, feats * pieces * hops, LANES),
            jax.ShapeDtypeStruct((joined_width, width), BF16),
            jax.ShapeDtypeStruct((hops * LANES, width), BF16),
            real(2 * hops + 4, width),
        ),
        in_specs=[hbm] + [vmem] * 3 + [hbm] + [vmem] * 4 + [hbm] + [vmem] * 5,
        out_specs=(hbm, hbm, hbm, vmem),
        scratch_shapes=[
            pltpu.VMEM((HOT * pieces * hops, LANES), F32),
            pltpu.VMEM((batches, hops, nodes, width), F32),
            pltpu.VMEM((batches, nodes, joined_width), BF16),
            pltpu.VMEM((batches, hops, LANES, nodes), BF16),
            pltpu.VMEM((batches, nodes, LANES), BF16),
            pltpu.VMEM((hops, LANES, width), BF16),
            pltpu.VMEM((batches, nodes, width), F32),
            pltpu.VMEM((batches, nodes, width), F32),
            pltpu.VMEM((batches, nodes, width), BF16),
            pltpu.VMEM((hops, LANES, width), F32),
            pltpu.VMEM((padded, width), F32),
            pltpu.VMEM((hops, LANES, width), BF16),
            pltpu.VMEM((joined_width, width), BF16),
            pltpu.VMEM((padded, width), BF16),
            pltpu.VMEM((padded, LANES), F32),
            pltpu.VMEM((tables, width), F32),
            pltpu.VMEM((tables, width), F32),
        ]
        + [pltpu.VMEM((batches, tables, width), F32) for _ in range(2)]
        + [pltpu.VMEM((tables, width), F32) for _ in range(2)]
        + [pltpu.VMEM((2 * hops, width), F32)]
        + [pltpu.VMEM((batches, table_rows, LANES), F32)]
        + [pltpu.VMEM((batches, nears, share, LANES), F32), pltpu.VMEM((batches, fars, share, LANES), F32)]
        + [pltpu.VMEM((batches, table_rows, LANES), F32)]
        + small_scratch(8)
        + small_scratch(16)
        + small_scratch(tables, 1)
        + [
            pltpu.VMEM((joined_width, width), BF16),
            pltpu.VMEM((joined_width, width), BF16),
            pltpu.VMEM((rows_rest, width), BF16),
            pltpu.VMEM((rows_rest, width), BF16),
            [[pltpu.VMEM(s, BF16) for s in mid_shapes] for _ in range(mid_parts)],
            [pltpu.VMEM(s, BF16) for s in rest_shapes],
            pltpu.VMEM((own_rows, width), BF16),
            pltpu.VMEM((batches, groups, width), F32),
            pltpu.VMEM((batches, groups, width), F32),
            [[pltpu.VMEM(s, BF16) for s in rest_shapes] for _ in range(gram_count)],
            [sem((batches,)) for _ in range(6)],
            [sem((batches,)) for _ in range(4)],
            [sem((batches,)) for _ in range(4)],
            [sem((1,)) for _ in range(4)],
            [sem((batches,)) for _ in range(6)],
            [[sem((len(mid_shapes),)) for _ in range(4)] for _ in range(mid_parts)],
            [sem((len(rest_shapes),)) for _ in range(4)],
            [[sem((len(rest_shapes),)) for _ in range(4)] for _ in range(gram_count)],
            sem((max(batches, hops),)),
            sem((batches,)),
            sem((3,)),
        ],
        compiler_params=pltpu.CompilerParams(
            collective_id=0, has_side_effects=True, vmem_limit_bytes=int(63.9 * 2**20)
        ),
    )(
        by_piece(jnp.transpose(features, (0, 3, 2, 1))),
        jnp.transpose(buckets, (0, 2, 1)),
        jnp.transpose(hop_mask, (2, 0, 1)),
        labels,
        by_piece(jnp.transpose(w_hops, (1, 0, 2))),
        gain_hops,
        shift_hops,
        slope_hops,
        slope_cat[None],
        w_mid,
        gain_mid[None],
        shift_mid[None],
        slope_mid[None],
        w_out.T,
        bias_out[None],
    )
    outs = pl.pallas_call(
        make_finish(dims),
        name="finish",
        out_shape=(
            real(batches, feats * pieces * hops, LANES),
            real(joined_width, width),
            real(feats * pieces * hops, LANES),
            real(hops, width),
            real(hops, width),
            real(hops, width),
            real(1, joined_width),
            real(1, width),
            real(1, width),
            real(1, width),
            real(classes, width),
            real(1, classes),
            real(1, 1),
        ),
        in_specs=[hbm, hbm, hbm, vmem],
        out_specs=(hbm, hbm, hbm) + (vmem,) * 10,
        scratch_shapes=[
            pltpu.VMEM((hops, width, width), BF16),
            pltpu.VMEM((hops, width, width), F32),
            pltpu.VMEM((batches, feats * pieces * hops, LANES), F32),
            pltpu.VMEM((hops * LANES, width), BF16),
            pltpu.VMEM((HOT * pieces * hops, LANES), F32),
            sem((5, max(batches, hops))),
        ],
        compiler_params=pltpu.CompilerParams(vmem_limit_bytes=int(63.9 * 2**20)),
    )(*outs)
    (features_grad, mid_grad, hops_grad, gain, shift, slope, cat, gain_m, shift_m, slope_m, out_grad, bias, loss) = outs
    return (
        loss[0, 0],
        jnp.transpose(by_hop(features_grad, hops, nodes // LANES), (0, 3, 2, 1)),
        jnp.transpose(by_hop(hops_grad, hops, pieces), (1, 0, 2)),
        gain,
        shift,
        slope,
        cat[0],
        mid_grad,
        gain_m[0],
        shift_m[0],
        slope_m[0],
        out_grad.T,
        bias[0],
    )


def solution(mesh):
    nodes_split = ("bucket", "dp")
    placed = (
        P(None, nodes_split, None, None),
        P(None, nodes_split, None),
        P(None, nodes_split, None),
        P(None, nodes_split),
    ) + (P(),) * 11
    return jax.shard_map(
        shards,
        mesh=mesh,
        in_specs=placed,
        out_specs=(P(), P(None, nodes_split, None, None)) + (P(),) * 11,
        check_vma=False,
    )
```
